256 devices in a mesh: seq: 32 (over x, z), chan: 8 (over y, core).
Axes of the slice: x: 4, y: 4, z: 8, core: 2. Of those that a mesh axis runs over, the one named last changes fastest.
Arguments:
- input_triple_streams: bfloat16 [10240, 3, 8192], P('seq', None, 'chan'), may hold values from -6 to 6
- former_piece_sizes: int32 [32], replicated, may hold values from 1 to 320, 8192 in all
- updated_piece_sizes: int32 [28], replicated, may hold values from 1 to 320, 8192 in all
- remaining_indices: int32 [28], replicated, may hold values from 0 to 31, as said below
- short_causal_filters: float32 [3, 3, 8192], P(None, None, 'chan'), may hold values from -3 to 3
- pole_coefficients: float32 [16, 8192], P(None, 'chan'), may hold values from -0.4375 to 0.4375
- pole_damping: float32 [16, 8192], P(None, 'chan'), may hold values from 6.1035156e-05 to 0.03125
- direct_coefficient: float32 [8192], P('chan'), may hold values from 0.5 to 1.5
- final_projector: bfloat16 [8192, 8192], P('seq', 'chan'), may hold values from -0.0625 to 0.0625
Outputs:
- mixed_rows: bfloat16 [10240, 8192], P('seq', 'chan')
The draws below stay inside these ranges and needn't reach their ends.
Inputs may be any that keep to these rules, and one draw needn't show every extreme that they name: `former_piece_sizes`: the counts sum to 8192; an index's rows fill its first slots in sequence order. `updated_piece_sizes`: the counts sum to 8192. `remaining_indices`: distinct indices of seq.
All inputs are finite; a program needn't handle non-finite values.
Results may differ from the reference program's by a relative error of at most 0.0064.
Values may be sent and summed in bfloat16 or wider, within the bound.
A program may use at most 128 MiB of HBM per device.

```python
import math
import jax
import jax.numpy as jnp
import numpy as np
from jax import lax

D = 8192
MODES = 16
CAP = 320
SEQ_LEN = 8192
SLOTS = 10240
N_SURV = 28
N_SEQ = 32


def draw_remaining_indices(key, part):
    key = jax.random.fold_in(key, 11)
    return jax.random.permutation(key, N_SEQ)[:N_SURV].astype(jnp.int32)


def shard_levels(own_key, dims, split, smallest, high):
    def one(position, parts):
        steps = jax.random.uniform(jax.random.fold_in(jax.random.fold_in(own_key, 6), position), (parts,), jnp.float32, smallest / len(split), high / len(split))
        return jnp.repeat(jnp.exp(steps), dims[position] // parts).reshape((-1,) + (1,) * (len(dims) - position - 1))

    loudness = one(*split[0])
    for cut in split[1:]:
        loudness = loudness * one(*cut)
    return loudness


def split_up(number_of, total, limit, lean):
    loads = [(1 << 20) // math.isqrt(rank ** lean) + 1 for rank in range(2, number_of + 1)]
    surplus, counts = total - limit - (number_of - 1), [1] * (number_of - 1)
    while surplus > 0:
        movable = [i for i in range(number_of - 1) if counts[i] < limit]
        mass, remaining = sum([loads[i] for i in movable]), surplus
        for i in movable:
            addition = min(limit - counts[i], max(1, remaining * loads[i] // mass), surplus)
            counts[i] = counts[i] + addition
            surplus = surplus - addition
    return np.array([limit] + counts)


def uneven(key, number_of, total, bound, slope):
    if number_of == 2:
        one = jax.random.randint(key, (), max(1, total - bound), min(bound, total - 1) + 1)
        return jnp.stack([one, total - one])
    tallies = jnp.asarray(split_up(number_of, total, bound, slope), jnp.int32)
    twos = (number_of - 1) // 2
    giver, taker = tallies[1:1 + 2 * twos:2], tallies[2:2 + 2 * twos:2]
    margin = jnp.minimum(giver - 1, bound - taker)
    shifted = jax.random.randint(jax.random.fold_in(key, 1), (twos,), 0, 1 << 20) % (margin + 1)
    tallies = tallies.at[1:1 + 2 * twos:2].set(giver - shifted).at[2:2 + 2 * twos:2].set(taker + shifted)
    return tallies[jax.random.permutation(jax.random.fold_in(key, 2), number_of)]


def scatter_about(key, dims, scale, reach, cuts=(), held_as=jnp.bfloat16):
    drawn = jax.random.normal(key, dims, jnp.float32) * scale
    if len(cuts) > 0:
        drawn = shard_levels(key, dims, cuts, -0.22, 0.18) * drawn
    return jnp.clip(drawn, min=-reach, max=reach).astype(held_as)


def setup_inputs(seed: int = 0) -> dict:
    keys = jax.random.split(jax.random.key(seed), 10)
    return {
        "input_triple_streams": scatter_about(keys[0], (SLOTS, 3, D), 1.0, 6.0, ((0, 32), (2, 8))),
        "former_piece_sizes": uneven(keys[1], N_SEQ, SEQ_LEN, CAP, 2).astype(jnp.int32),
        "updated_piece_sizes": uneven(keys[2], N_SURV, SEQ_LEN, CAP, 2).astype(jnp.int32),
        "remaining_indices": draw_remaining_indices(jax.random.fold_in(keys[9], 71), 0),
        "short_causal_filters": scatter_about(keys[4], (3, 3, D), 0.7, 3.0, ((2, 8),), jnp.float32),
        "pole_coefficients": scatter_about(keys[5], (MODES, D), 0.03, 0.4375, ((1, 8),), jnp.float32),
        "pole_damping": jnp.clip(jnp.exp(math.log(0.03125) - 6.2383246 * jax.random.uniform(keys[6], (MODES, D), jnp.float32) ** shard_levels(keys[6], (MODES, D), ((1, 8),), -0.2, 0.2)), 6.103515625e-05, 0.03125),
        "direct_coefficient": jnp.clip(0.5 + 1.0 * jax.random.uniform(keys[7], (D,), jnp.float32) ** shard_levels(keys[7], (D,), ((0, 8),), -0.2, 0.2), 0.5, 1.5),
        "final_projector": scatter_about(keys[8], (D, D), D ** -0.5, 0.0625, ((0, 32), (1, 8))),
    }


def featurize(signal, taps):
    lag_one = jnp.pad(signal, ((1, 0), (0, 0), (0, 0)))[:-1]
    lag_two = jnp.pad(signal, ((2, 0), (0, 0), (0, 0)))[:-2]
    return taps[:, 0] * signal + taps[:, 1] * lag_one + taps[:, 2] * lag_two


def reference(input_triple_streams, former_piece_sizes, updated_piece_sizes, remaining_indices, short_causal_filters, pole_coefficients, pole_damping, direct_coefficient, final_projector):
    positions = jnp.arange(SEQ_LEN, dtype=jnp.int32)
    old_end = jnp.cumsum(former_piece_sizes).astype(jnp.int32)
    passed = (old_end[None, :] <= positions[:, None]).astype(jnp.int32)
    slot_index = (positions + jnp.sum(passed * (CAP - former_piece_sizes)[None, :], axis=1)).astype(jnp.int32)
    seq_rows = jnp.take(input_triple_streams, slot_index, axis=0)
    chan_block = min(256, D)
    block_count = D // chan_block
    time_steps = jnp.arange(SEQ_LEN, dtype=jnp.float32)
    fft_length = 2 * SEQ_LEN

    def one_block(block_index):
        first = block_index * chan_block
        signal = lax.dynamic_slice_in_dim(seq_rows, first, chan_block, 2).astype(jnp.float32)
        taps = lax.dynamic_slice_in_dim(short_causal_filters, first, chan_block, 2)
        featured = featurize(signal, taps)
        queries = lax.optimization_barrier(featured[:, 0].astype(jnp.bfloat16)).astype(jnp.float32)
        gated_prod = lax.optimization_barrier((featured[:, 1] * featured[:, 2]).astype(jnp.bfloat16)).astype(jnp.float32)
        residue_block = lax.dynamic_slice_in_dim(pole_coefficients, first, chan_block, 1)
        decay_block = lax.dynamic_slice_in_dim(pole_damping, first, chan_block, 1)
        skip_block = lax.dynamic_slice_in_dim(direct_coefficient, first, chan_block, 0)
        powers = jnp.exp(-decay_block[:, None, :] * time_steps[None, :, None])
        long_filter = jnp.einsum('mc,mtc->tc', residue_block, powers, precision=lax.Precision.HIGHEST)
        spectrum = jnp.fft.rfft(gated_prod, n=fft_length, axis=0) * jnp.fft.rfft(long_filter, n=fft_length, axis=0)
        conv_total = jnp.fft.irfft(spectrum, n=fft_length, axis=0)[:SEQ_LEN]
        conv_total = conv_total + skip_block[None, :] * gated_prod
        return (queries * conv_total).astype(jnp.bfloat16)

    blocks = lax.map(one_block, jnp.arange(block_count, dtype=jnp.int32))
    hidden = jnp.transpose(blocks, (1, 0, 2)).reshape(SEQ_LEN, D)
    projected = jnp.dot(hidden, final_projector, preferred_element_type=jnp.float32).astype(jnp.bfloat16)
    new_end = jnp.cumsum(updated_piece_sizes).astype(jnp.int32)
    new_start = new_end - updated_piece_sizes
    device_names = jnp.arange(N_SEQ, dtype=jnp.int32)
    partner_table = (remaining_indices[None, :] == device_names[:, None]).astype(jnp.int32)
    start_dev = jnp.sum(partner_table * new_start[None, :], axis=1)
    count_dev = jnp.sum(partner_table * updated_piece_sizes[None, :], axis=1)
    offsets = jnp.arange(CAP, dtype=jnp.int32)
    source_row = (start_dev[:, None] + offsets[None, :]).reshape(-1)
    valid_slot = (offsets[None, :] < count_dev[:, None]).reshape(-1)
    source_row = jnp.minimum(source_row, SEQ_LEN - 1).astype(jnp.int32)
    picked = jnp.take(projected, source_row, axis=0)
    return jnp.where(valid_slot[:, None], picked, jnp.zeros_like(picked))
```

```python
import jax
import jax.numpy as jnp
from jax import lax
from jax.sharding import PartitionSpec as P

GROUP = 128


def long_mix(queries, gated_prod, pole_coefficients, pole_damping, direct_coefficient):
    chan_count, length = gated_prod.shape
    group_count = length // GROUP
    gated_full = gated_prod.astype(jnp.float32)
    signal = gated_full.reshape(chan_count, group_count, GROUP)
    offsets = jnp.arange(GROUP, dtype=jnp.float32)
    decay_rates = pole_damping[:, :, None]
    lag_value = offsets[:, None] - offsets[None, :]
    lag_clip = jnp.maximum(lag_value, 0.0)
    lag_powers = jnp.exp(-pole_damping[:, :, None, None] * lag_clip[None, None, :, :])
    toeplitz_full = jnp.einsum(
        "mc,mcij->cij", pole_coefficients, lag_powers, precision=lax.Precision.HIGHEST
    )
    toeplitz = jnp.where(lag_value[None] >= 0.0, toeplitz_full, 0.0)
    within_sum = jnp.einsum("cij,cnj->cni", toeplitz, signal, precision=lax.Precision.HIGHEST)
    tail_weights = jnp.exp(-decay_rates * (GROUP - 1.0 - offsets)[None, None, :])
    summary = jnp.einsum("mcj,cnj->mcn", tail_weights, signal, precision=lax.Precision.HIGHEST)
    step_decay = jnp.broadcast_to(jnp.exp(-pole_damping * GROUP)[:, :, None], summary.shape)

    def combine(earlier, later):
        return (earlier[0] * later[0], earlier[1] * later[0] + later[1])

    carried = lax.associative_scan(combine, (step_decay, summary), axis=2)[1]
    before = jnp.concatenate([jnp.zeros_like(carried[:, :, :1]), carried[:, :, :-1]], axis=2)
    head_weights = pole_coefficients[:, :, None] * jnp.exp(
        -decay_rates * (offsets + 1.0)[None, None, :]
    )
    remote = jnp.einsum("mci,mcn->cni", head_weights, before, precision=lax.Precision.HIGHEST)
    conv_total = (within_sum + remote).reshape(chan_count, length) + direct_coefficient[
        :, None
    ] * gated_full
    return (queries.astype(jnp.float32) * conv_total).astype(jnp.bfloat16)


def running_ends(sizes):
    index = jnp.arange(sizes.shape[0], dtype=jnp.int32)
    return jnp.sum(jnp.where(index[None, :] <= index[:, None], sizes[None, :], 0), axis=1)


def compact_rows(moved_rows, former_piece_sizes, capacity, seq_len, seq_count):
    old_end = running_ends(former_piece_sizes)
    old_start = old_end - former_piece_sizes
    lead_shape = moved_rows.shape[:2]
    buffer = jnp.zeros(lead_shape + (seq_len + capacity,), moved_rows.dtype)

    def place(source, current):
        piece = lax.dynamic_slice_in_dim(moved_rows, source * capacity, capacity, 2)
        return lax.dynamic_update_slice_in_dim(current, piece, old_start[source], 2)

    filled = lax.fori_loop(0, seq_count, place, buffer)
    return filled[:, :, :seq_len]


def shards(
    input_triple_streams,
    former_piece_sizes,
    updated_piece_sizes,
    remaining_indices,
    short_causal_filters,
    pole_coefficients,
    pole_damping,
    direct_coefficient,
    final_projector,
):
    seq_count = lax.axis_size("seq")
    own_index = lax.axis_index("seq")
    capacity = input_triple_streams.shape[0]
    chan_width = input_triple_streams.shape[2]
    narrow = chan_width // seq_count
    seq_len = capacity * 4 // 5 * seq_count
    first_chan = own_index * narrow
    moved_rows = lax.all_to_all(
        jnp.transpose(input_triple_streams, (1, 2, 0)),
        "seq",
        split_axis=1,
        concat_axis=2,
        tiled=True,
    )
    compact = compact_rows(moved_rows, former_piece_sizes, capacity, seq_len, seq_count)
    signal = compact.astype(jnp.float32)
    lag_one = jnp.pad(signal, ((0, 0), (0, 0), (1, 0)))[:, :, :-1]
    lag_two = jnp.pad(signal, ((0, 0), (0, 0), (2, 0)))[:, :, :-2]
    taps = lax.dynamic_slice_in_dim(short_causal_filters, first_chan, narrow, 2)
    featured = (
        taps[:, 0, :, None] * signal + taps[:, 1, :, None] * lag_one + taps[:, 2, :, None] * lag_two
    )
    queries = lax.optimization_barrier(featured[0].astype(jnp.bfloat16))
    gated_prod = lax.optimization_barrier((featured[1] * featured[2]).astype(jnp.bfloat16))
    residue_mine = lax.dynamic_slice_in_dim(pole_coefficients, first_chan, narrow, 1)
    decay_mine = lax.dynamic_slice_in_dim(pole_damping, first_chan, narrow, 1)
    skip_mine = lax.dynamic_slice_in_dim(direct_coefficient, first_chan, narrow, 0)
    hidden = long_mix(queries, gated_prod, residue_mine, decay_mine, skip_mine)
    new_end = running_ends(updated_piece_sizes)
    new_start = new_end - updated_piece_sizes
    device_names = jnp.arange(seq_count, dtype=jnp.int32)
    partner_table = (remaining_indices[None, :] == device_names[:, None]).astype(jnp.int32)
    start_dev = jnp.sum(partner_table * new_start[None, :], axis=1)
    count_dev = jnp.sum(partner_table * updated_piece_sizes[None, :], axis=1)
    offsets = jnp.arange(capacity, dtype=jnp.int32)
    hidden_padded = jnp.concatenate(
        [hidden, jnp.zeros((hidden.shape[0], capacity), hidden.dtype)], axis=1
    )
    outgoing_init = jnp.zeros((hidden.shape[0], capacity * seq_count), hidden.dtype)

    def pick(target, current):
        piece = lax.dynamic_slice_in_dim(hidden_padded, start_dev[target], capacity, 1)
        kept = jnp.where((offsets < count_dev[target])[None, :], piece, jnp.zeros_like(piece))
        return lax.dynamic_update_slice_in_dim(current, kept, target * capacity, 1)

    outgoing = lax.fori_loop(0, seq_count, pick, outgoing_init)
    arrived = lax.all_to_all(outgoing, "seq", split_axis=1, concat_axis=0, tiled=True)
    all_channels = lax.all_gather(arrived, "chan", axis=0, tiled=True)
    projected = lax.dot_general(
        all_channels,
        lax.all_gather(final_projector, "seq", axis=0, tiled=True),
        (((0,), (0,)), ((), ())),
        preferred_element_type=jnp.float32,
    )
    return projected.astype(jnp.bfloat16)


def solution(mesh):
    return jax.shard_map(
        shards,
        mesh=mesh,
        in_specs=(
            P("seq", None, "chan"),
            P(),
            P(),
            P(),
            P(None, None, "chan"),
            P(None, "chan"),
            P(None, "chan"),
            P("chan"),
            P("seq", "chan"),
        ),
        out_specs=P("seq", "chan"),
        check_vma=False,
    )
```

```python
import functools

import jax
import jax.numpy as jnp
from jax import lax
from jax.experimental import pallas as pl
from jax.experimental.pallas import tpu as pltpu
from jax.sharding import Mesh
from jax.sharding import PartitionSpec as P

MESH = pl.DeviceIdType.MESH
LANES = 128
SUBS = 8
AXES = ("x", "z", "y", "core")


def shift_down(value, by):
    row = lax.broadcasted_iota(jnp.int32, value.shape, 0)
    return jnp.where(row >= by, pltpu.roll(value, by, 0), 0.0)


def tree_sum(terms):
    while len(terms) > 1:
        terms = [a + b for a, b in zip(terms[::2], terms[1::2], strict=True)]
    return terms[0]


def conv_kernel(
    x_count, z_count,
    sizes, streams, tail, taps, residue, damping, damping_tiles, direct,
    gathered,
    padded, query, gated, mixed, partial, ends, end_in, carry_out, carry_in, hidden, halo,
    halo_send, halo_recv, end_send, end_recv, carry_send, carry_recv,
    z_send, z_recv, right_send, right_recv, left_send, left_recv,
    far_a_send, far_a_recv, far_b_send, far_b_recv, local_sem,
):
    modes = residue.shape[0]
    cap = streams.shape[1]
    groups = z_count
    step_rows = cap // SUBS
    seq_count = x_count * z_count
    per_owner = max(1, modes // seq_count)
    owners = modes // per_owner
    my_x, my_z = lax.axis_index("x"), lax.axis_index("z")
    me = my_x * z_count + my_z
    valid = sizes[me]

    def seq_device(index):
        return {"x": index // z_count, "z": lax.rem(index, z_count)}

    barrier = pltpu.get_barrier_semaphore()

    @pl.loop(1, seq_count)
    def _(k):
        pl.semaphore_signal(
            barrier, inc=1, device_id=seq_device(lax.rem(me + k, seq_count)), device_id_type=MESH
        )

    pl.semaphore_wait(barrier, seq_count - 1)

    def halo_copy(distance):
        target = lax.rem(me + distance, seq_count)
        return pltpu.make_async_remote_copy(
            src_ref=tail, dst_ref=halo.at[distance - 1], send_sem=halo_send.at[distance - 1],
            recv_sem=halo_recv.at[distance - 1], device_id=seq_device(target), device_id_type=MESH,
        )

    for distance in (1, 2):
        halo_copy(distance).start()
    for distance in (1, 2):
        halo_copy(distance).wait_recv()

    row = lax.broadcasted_iota(jnp.int32, (cap, LANES), 0)
    before_size = sizes[lax.rem(me + seq_count - 1, seq_count)]

    def lanes(g):
        return pl.ds(pl.multiple_of(g * LANES, LANES), LANES)

    @pl.loop(0, groups)
    def _(g):
        at = lanes(g)
        features = []
        for p in range(3):
            last_one = jnp.where(me >= 1, halo[0, p : p + 1, at], 0.0)
            own_second = halo[0, 3 + p : 4 + p, at]
            far_last = jnp.where(me >= 2, halo[1, p : p + 1, at], 0.0)
            last_two = jnp.where(me >= 1, jnp.where(before_size >= 2, own_second, far_last), 0.0)
            padded[p, 6:7, :] = last_two
            padded[p, 7:8, :] = last_one
            padded[p, 8 : 8 + cap, :] = streams[p, :, at].astype(jnp.float32)
            features.append(
                taps[3 * p : 3 * p + 1, at] * padded[p, 8 : 8 + cap, :]
                + taps[3 * p + 1 : 3 * p + 2, at] * padded[p, 7 : 7 + cap, :]
                + taps[3 * p + 2 : 3 * p + 3, at] * padded[p, 6 : 6 + cap, :]
            )
        query[g] = features[0].astype(jnp.bfloat16).astype(jnp.float32)
        product = (features[1] * features[2]).astype(jnp.bfloat16).astype(jnp.float32)
        gated[g] = jnp.where(row < valid, product, 0.0)

    def mode_rows(ref, at):
        return [jnp.broadcast_to(ref[m : m + 1, at], (SUBS, LANES)) for m in range(modes)]

    @pl.loop(0, groups)
    def _(g):
        at = lanes(g)
        decay = [jnp.exp(-d) for d in mode_rows(damping, at)]
        weight = mode_rows(residue, at)

        def step(i, states):
            u = gated[g, pl.ds(i, SUBS, stride=step_rows), :]
            return tuple(a * h + r * u for a, h, r in zip(decay, states, weight, strict=True))

        zero = jnp.zeros((SUBS, LANES), jnp.float32)
        states = lax.fori_loop(0, step_rows, step, (zero,) * modes, unroll=4)
        left_over = (cap - valid).astype(jnp.float32)
        for m in range(modes):
            rate = damping[m : m + 1, at]
            total = states[m]
            for by in (1, 2, 4):
                total = total + jnp.exp(-rate * (step_rows * by)) * shift_down(total, by)
            partial[g, m] = shift_down(total, 1)
            ends[m, pl.ds(g, 1), :] = total[SUBS - 1 : SUBS, :] * jnp.exp(rate * left_over)

    def end_copy(owner):
        return pltpu.make_async_remote_copy(
            src_ref=ends.at[pl.ds(owner * per_owner, per_owner)], dst_ref=end_in.at[me],
            send_sem=end_send.at[owner], recv_sem=end_recv.at[me],
            device_id=seq_device(owner), device_id_type=MESH,
        )

    def end_arrival(source):
        return pltpu.make_async_remote_copy(
            src_ref=ends.at[pl.ds(0, per_owner)], dst_ref=end_in.at[source],
            send_sem=end_send.at[0], recv_sem=end_recv.at[source],
            device_id=seq_device(source), device_id_type=MESH,
        )

    def carry_copy(target):
        return pltpu.make_async_remote_copy(
            src_ref=carry_out.at[target], dst_ref=carry_in.at[me],
            send_sem=carry_send.at[target], recv_sem=carry_recv.at[me],
            device_id=seq_device(target), device_id_type=MESH,
        )

    def carry_arrival(owner):
        return pltpu.make_async_remote_copy(
            src_ref=carry_out.at[0], dst_ref=carry_in.at[owner],
            send_sem=carry_send.at[0], recv_sem=carry_recv.at[owner],
            device_id=seq_device(owner), device_id_type=MESH,
        )

    @pl.loop(0, owners)
    def _(k):
        owner = lax.rem(me + k, owners)

        @pl.when(owner != me)
        def _():
            end_copy(owner).start()

    @pl.when(me < owners)
    def _():
        end_in[me] = ends[pl.ds(me * per_owner, per_owner)]

        @pl.loop(0, seq_count)
        def _(source):
            @pl.when(source != me)
            def _():
                end_arrival(source).wait_recv()

        rate = damping_tiles[pl.ds(me * per_owner, per_owner)]

        def advance(source, carry):
            carry_out[source] = carry
            return jnp.exp(-rate * sizes[source].astype(jnp.float32)) * carry + end_in[source]

        lax.fori_loop(0, seq_count, advance, jnp.zeros_like(rate))
        carry_in[me] = carry_out[me]

        @pl.loop(0, seq_count)
        def _(target):
            @pl.when(target != me)
            def _():
                carry_copy(target).start()

    @pl.loop(0, owners)
    def _(owner):
        @pl.when(owner != me)
        def _():
            carry_arrival(owner).wait_recv()

    def z_copy(g):
        return pltpu.make_async_remote_copy(
            src_ref=hidden.at[g], dst_ref=gathered.at[me], send_sem=z_send.at[g],
            recv_sem=z_recv.at[my_z], device_id={"z": g}, device_id_type=MESH,
        )

    def z_arrival(z):
        return pltpu.make_async_remote_copy(
            src_ref=hidden.at[0], dst_ref=gathered.at[my_x * z_count + z], send_sem=z_send.at[0],
            recv_sem=z_recv.at[z], device_id={"z": z}, device_id_type=MESH,
        )

    own_copy = pltpu.make_async_copy(hidden.at[my_z], gathered.at[me], local_sem)

    @pl.loop(0, groups)
    def _(k):
        g = lax.rem(my_z + 1 + k, groups)
        at = lanes(g)
        rates = mode_rows(damping, at)
        decay = [jnp.exp(-d) for d in rates]
        weight = mode_rows(residue, at)
        sub = lax.broadcasted_iota(jnp.int32, (SUBS, LANES), 0).astype(jnp.float32) * step_rows
        start = tuple(
            partial[g, m]
            + jnp.exp(-rates[m] * sub)
            * carry_in[m // per_owner, m % per_owner, pl.ds(g, 1), :]
            for m in range(modes)
        )

        def step(i, states):
            rows = pl.ds(i, SUBS, stride=step_rows)
            u = gated[g, rows, :]
            states = tuple(a * h + r * u for a, h, r in zip(decay, states, weight, strict=True))
            mixed[rows, :] = tree_sum(list(states))
            return states

        lax.fori_loop(0, step_rows, step, start, unroll=4)
        conv = mixed[...] + direct[0:1, at] * gated[g]
        hidden[g] = (query[g] * conv).astype(jnp.bfloat16)

        @pl.when(g != my_z)
        def _():
            z_copy(g).start()

        @pl.when(g == my_z)
        def _():
            own_copy.start()

    right, left = lax.rem(my_x + 1, x_count), lax.rem(my_x + x_count - 1, x_count)
    half = cap // 2

    def x_copy(source_x, z, to, send, recv, first, rows):
        slot = source_x * z_count + z
        view = gathered.at[slot, pl.ds(first, rows)]
        return pltpu.make_async_remote_copy(
            src_ref=view, dst_ref=view, send_sem=send.at[z], recv_sem=recv.at[z],
            device_id={"x": to}, device_id_type=MESH,
        )

    def to_right(source_x, z):
        return x_copy(source_x, z, right, right_send, right_recv, 0, cap)

    def to_left(source_x, z):
        return x_copy(source_x, z, left, left_send, left_recv, 0, cap)

    def far_right(source_x, z):
        return x_copy(source_x, z, right, far_a_send, far_a_recv, 0, half)

    def far_left(source_x, z):
        return x_copy(source_x, z, left, far_b_send, far_b_recv, half, half)

    @pl.loop(0, z_count)
    def _(k):
        z = lax.rem(my_z + 2 * z_count - 1 - k, z_count)

        @pl.when(z != my_z)
        def _():
            z_arrival(z).wait_recv()

        @pl.when(z == my_z)
        def _():
            own_copy.wait()

        to_right(my_x, z).start()
        to_left(my_x, z).start()

    @pl.loop(0, z_count)
    def _(k):
        z = lax.rem(my_z + 2 * z_count - 1 - k, z_count)
        to_right(left, z).wait_recv()
        far_right(left, z).start()
        to_left(right, z).wait_recv()
        far_left(right, z).start()

    opposite = lax.rem(my_x + 2, x_count)

    @pl.loop(0, z_count)
    def _(z):
        far_right(opposite, z).wait_recv()
        far_left(opposite, z).wait_recv()
        far_right(left, z).wait_send()
        far_left(right, z).wait_send()
        to_right(my_x, z).wait_send()
        to_left(my_x, z).wait_send()

        @pl.when(z != my_z)
        def _():
            z_copy(z).wait_send()

    for distance in (1, 2):
        halo_copy(distance).wait_send()

    @pl.loop(0, owners)
    def _(owner):
        @pl.when(owner != me)
        def _():
            end_copy(owner).wait_send()

    @pl.when(me < owners)
    def _():
        @pl.loop(0, seq_count)
        def _(target):
            @pl.when(target != me)
            def _():
                carry_copy(target).wait_send()


def conv_call(dims, streams, tail, sizes, taps, residue, damping, direct):
    x_count, z_count = dims["x"], dims["z"]
    cap, width = streams.shape[1:]
    modes = residue.shape[0]
    seq_count = x_count * z_count
    per_owner = max(1, modes // seq_count)
    owners = modes // per_owner
    f32, bf16 = jnp.float32, jnp.bfloat16
    dma = pltpu.SemaphoreType.DMA
    vmem = pl.BlockSpec(memory_space=pltpu.VMEM)
    return pl.pallas_call(
        functools.partial(conv_kernel, x_count, z_count),
        out_shape=jax.ShapeDtypeStruct((seq_count, cap, LANES), bf16),
        in_specs=[pl.BlockSpec(memory_space=pltpu.SMEM)] + [vmem] * 7,
        out_specs=pl.BlockSpec(memory_space=pl.ANY),
        scratch_shapes=[
            pltpu.VMEM((3, cap + SUBS, LANES), f32),
            pltpu.VMEM((z_count, cap, LANES), f32),
            pltpu.VMEM((z_count, cap, LANES), f32),
            pltpu.VMEM((cap, LANES), f32),
            pltpu.VMEM((z_count, modes, SUBS, LANES), f32),
            pltpu.VMEM((modes, z_count, LANES), f32),
            pltpu.VMEM((seq_count, per_owner, z_count, LANES), f32),
            pltpu.VMEM((seq_count, per_owner, z_count, LANES), f32),
            pltpu.VMEM((owners, per_owner, z_count, LANES), f32),
            pltpu.VMEM((z_count, cap, LANES), bf16),
            pltpu.VMEM((2,) + tail.shape, f32),
            dma((2,)), dma((2,)),
            dma((owners,)), dma((seq_count,)), dma((seq_count,)), dma((owners,)),
        ]
        + [dma((z_count,))] * 10
        + [dma],
        compiler_params=pltpu.CompilerParams(
            collective_id=0, has_side_effects=True, vmem_limit_bytes=24 << 20
        ),
        name="conv_shuffle",
    )(
        sizes, streams, tail, taps, residue, damping,
        damping.reshape(modes, width // LANES, LANES), direct,
    )


def select_kernel(old_start, new_start, counts, pieces, chosen, sequence):
    seq_count, cap, _ = pieces.shape

    @pl.loop(0, seq_count)
    def _(s):
        sequence[pl.ds(old_start[s], cap), :] = pieces[s].astype(jnp.float32)

    row = lax.broadcasted_iota(jnp.int32, (cap, LANES), 0)

    @pl.loop(0, chosen.shape[0])
    def _(k):
        rows = sequence[pl.ds(new_start[k], cap), :]
        chosen[k] = jnp.where(row < counts[k], rows, 0.0).astype(jnp.bfloat16)


def select_call(dims, seq_len, pieces, old_start, new_start, counts):
    cap = pieces.shape[1]
    smem = pl.BlockSpec(memory_space=pltpu.SMEM)
    vmem = pl.BlockSpec(memory_space=pltpu.VMEM)
    return pl.pallas_call(
        select_kernel,
        out_shape=jax.ShapeDtypeStruct((dims["z"], cap, LANES), jnp.bfloat16),
        in_specs=[smem] * 3 + [vmem],
        out_specs=vmem,
        scratch_shapes=[pltpu.VMEM((seq_len + cap, LANES), jnp.float32)],
        compiler_params=pltpu.CompilerParams(vmem_limit_bytes=24 << 20),
        name="reorder_rows",
    )(old_start, new_start, counts, pieces)


def spread_kernel(
    x_count, z_count, y_count,
    chosen, rows_out,
    z_send, z_recv, right_send, right_recv, left_send, left_recv,
    far_a_send, far_a_recv, far_b_send, far_b_recv, core_send, core_recv, local_sem,
):
    cap = rows_out.shape[0]
    my_z, my_y, my_core = lax.axis_index("z"), lax.axis_index("y"), lax.axis_index("core")
    right, left = lax.rem(my_y + 1, y_count), lax.rem(my_y + y_count - 1, y_count)
    opposite = lax.rem(my_y + 2, y_count)
    other = 1 - my_core
    half = cap // 2

    barrier = pltpu.get_barrier_semaphore()

    @pl.loop(1, z_count)
    def _(k):
        pl.semaphore_signal(
            barrier, inc=1, device_id={"z": lax.rem(my_z + k, z_count)}, device_id_type=MESH
        )

    for to in ({"y": right}, {"y": left}, {"core": other}):
        pl.semaphore_signal(barrier, inc=1, device_id=to, device_id_type=MESH)
    pl.semaphore_wait(barrier, z_count + 2)

    def columns(y, core, z):
        return pl.ds(pl.multiple_of(((y * 2 + core) * z_count + z) * LANES, LANES), LANES)

    def z_copy(z):
        return pltpu.make_async_remote_copy(
            src_ref=chosen.at[z], dst_ref=rows_out.at[:, columns(my_y, my_core, my_z)],
            send_sem=z_send.at[z], recv_sem=z_recv.at[my_z], device_id={"z": z}, device_id_type=MESH,
        )

    def z_arrival(z):
        return pltpu.make_async_remote_copy(
            src_ref=chosen.at[0], dst_ref=rows_out.at[:, columns(my_y, my_core, z)],
            send_sem=z_send.at[0], recv_sem=z_recv.at[z], device_id={"z": z}, device_id_type=MESH,
        )

    own_copy = pltpu.make_async_copy(
        chosen.at[my_z], rows_out.at[:, columns(my_y, my_core, my_z)], local_sem
    )
    own_copy.start()

    @pl.loop(1, z_count)
    def _(k):
        z_copy(lax.rem(my_z + k, z_count)).start()

    def onward(y, core, z, to, send, recv, first, rows):
        view = rows_out.at[pl.ds(first, rows), columns(y, core, z)]
        return pltpu.make_async_remote_copy(
            src_ref=view, dst_ref=view, send_sem=send, recv_sem=recv,
            device_id=to, device_id_type=MESH,
        )

    def to_right(y, z):
        return onward(y, my_core, z, {"y": right}, right_send.at[z], right_recv.at[z], 0, cap)

    def to_left(y, z):
        return onward(y, my_core, z, {"y": left}, left_send.at[z], left_recv.at[z], 0, cap)

    def far_right(y, z):
        return onward(y, my_core, z, {"y": right}, far_a_send.at[z], far_a_recv.at[z], 0, half)

    def far_left(y, z):
        return onward(y, my_core, z, {"y": left}, far_b_send.at[z], far_b_recv.at[z], half, half)

    def to_core(y, core, z):
        return onward(y, core, z, {"core": other}, core_send.at[y, z], core_recv.at[y, z], 0, cap)

    def arrival_order(k):
        return lax.rem(my_z + z_count - k, z_count)

    @pl.loop(0, z_count)
    def _(k):
        z = arrival_order(k)

        @pl.when(z != my_z)
        def _():
            z_arrival(z).wait_recv()

        @pl.when(z == my_z)
        def _():
            own_copy.wait()

        to_right(my_y, z).start()
        to_left(my_y, z).start()
        to_core(my_y, my_core, z).start()

    @pl.loop(0, z_count)
    def _(k):
        z = arrival_order(k)
        to_right(left, z).wait_recv()
        far_right(left, z).start()
        to_core(left, my_core, z).start()
        to_left(right, z).wait_recv()
        far_left(right, z).start()
        to_core(right, my_core, z).start()

    @pl.loop(0, z_count)
    def _(k):
        z = arrival_order(k)
        far_right(opposite, z).wait_recv()
        far_left(opposite, z).wait_recv()
        to_core(opposite, my_core, z).start()

    @pl.loop(0, z_count)
    def _(z):
        for y in range(y_count):
            to_core(y, other, z).wait_recv()
            to_core(y, my_core, z).wait_send()
        to_right(my_y, z).wait_send()
        to_left(my_y, z).wait_send()
        far_right(left, z).wait_send()
        far_left(right, z).wait_send()

        @pl.when(z != my_z)
        def _():
            z_copy(z).wait_send()


def spread_call(dims, chosen):
    z_count, cap, _ = chosen.shape
    y_count = dims["y"]
    dma = pltpu.SemaphoreType.DMA
    return pl.pallas_call(
        functools.partial(spread_kernel, dims["x"], z_count, y_count),
        out_shape=jax.ShapeDtypeStruct((cap, y_count * 2 * z_count * LANES), jnp.bfloat16),
        in_specs=[pl.BlockSpec(memory_space=pltpu.VMEM)],
        out_specs=pl.BlockSpec(memory_space=pl.ANY),
        scratch_shapes=[dma((z_count,))] * 10 + [dma((y_count, z_count))] * 2 + [dma],
        compiler_params=pltpu.CompilerParams(collective_id=1, has_side_effects=True),
        name="spread_rows",
    )(chosen)


def running_ends(sizes):
    index = jnp.arange(sizes.shape[0], dtype=jnp.int32)
    return jnp.sum(jnp.where(index[None, :] <= index[:, None], sizes[None, :], 0), axis=1)


def shards(
    dims,
    input_triple_streams,
    former_piece_sizes,
    updated_piece_sizes,
    remaining_indices,
    short_causal_filters,
    pole_coefficients,
    pole_damping,
    direct_coefficient,
    final_projector,
):
    x_count, z_count = dims["x"], dims["z"]
    seq_count = x_count * z_count
    my_x = lax.axis_index("x")
    me = my_x * z_count + lax.axis_index("z")
    cap, _, width = input_triple_streams.shape
    seq_len = cap * 4 // 5 * seq_count

    projector = lax.all_gather(final_projector, ("x", "z"), axis=0, tiled=True)

    last = former_piece_sizes[me] - 1
    last_row = lax.dynamic_slice_in_dim(input_triple_streams, last, 1, 0)[0]
    second_row = lax.dynamic_slice_in_dim(input_triple_streams, jnp.maximum(last - 1, 0), 1, 0)[0]
    tail = jnp.concatenate([last_row, second_row, last_row[:2]], axis=0).astype(jnp.float32)

    pieces = conv_call(
        dims,
        jnp.transpose(input_triple_streams, (1, 0, 2)),
        tail,
        former_piece_sizes,
        short_causal_filters.reshape(9, width),
        pole_coefficients,
        pole_damping,
        direct_coefficient[None, :],
    )

    old_start = running_ends(former_piece_sizes) - former_piece_sizes
    new_start = running_ends(updated_piece_sizes) - updated_piece_sizes
    device_names = my_x * z_count + jnp.arange(z_count, dtype=jnp.int32)
    partner_table = (remaining_indices[None, :] == device_names[:, None]).astype(jnp.int32)
    start_dev = jnp.sum(partner_table * new_start[None, :], axis=1)
    count_dev = jnp.sum(partner_table * updated_piece_sizes[None, :], axis=1)
    chosen = select_call(dims, seq_len, pieces, old_start, start_dev, count_dev)

    hidden = spread_call(dims, chosen)
    projected = jnp.dot(hidden, projector, preferred_element_type=jnp.float32)
    return projected.astype(jnp.bfloat16)


def solution(mesh):
    grid = (4, mesh.shape["seq"] // 4, mesh.shape["chan"] // 2, 2)
    dims = dict(zip(AXES, grid, strict=True))
    rows, channels = ("x", "z"), ("y", "core")
    return jax.shard_map(
        functools.partial(shards, dims),
        mesh=Mesh(mesh.devices.reshape(grid), AXES),
        in_specs=(
            P(rows, None, channels),
            P(),
            P(),
            P(),
            P(None, None, channels),
            P(None, channels),
            P(None, channels),
            P(channels),
            P(rows, channels),
        ),
        out_specs=P(rows, channels),
        check_vma=False,
    )
```

```python
import functools

import jax
import jax.numpy as jnp
from jax import lax
from jax.experimental import pallas as pl
from jax.experimental.pallas import tpu as pltpu
from jax.sharding import Mesh
from jax.sharding import PartitionSpec as P

MESH = pl.DeviceIdType.MESH
LANES = 128
SUBS = 8
AXES = ("x", "z", "y", "core")


def shift_down(value, by):
    row = lax.broadcasted_iota(jnp.int32, value.shape, 0)
    return jnp.where(row >= by, pltpu.roll(value, by, 0), 0.0)


def tree_sum(terms):
    while len(terms) > 1:
        terms = [a + b for a, b in zip(terms[::2], terms[1::2], strict=True)]
    return terms[0]


def conv_kernel(
    x_count, z_count,
    sizes, streams, taps, residue, damping, direct,
    gathered,
    padded, tail, rates_own, query, gated, mixed, partial, ends, end_in, carry_out, carry_in, hidden, halo,
    halo_send, halo_recv, end_send, end_recv, carry_send, carry_recv,
    z_send, z_recv, right_send, right_recv, left_send, left_recv,
    far_a_send, far_a_recv, far_b_send, far_b_recv, local_sem,
):
    modes = residue.shape[0]
    cap = streams.shape[1]
    groups = z_count
    step_rows = cap // SUBS
    seq_count = x_count * z_count
    per_owner = max(1, modes // seq_count)
    owners = modes // per_owner
    my_x, my_z = lax.axis_index("x"), lax.axis_index("z")
    me = my_x * z_count + my_z
    valid = sizes[me]

    def seq_device(index):
        return {"x": index // z_count, "z": lax.rem(index, z_count)}

    def lanes(g):
        return pl.ds(pl.multiple_of(g * LANES, LANES), LANES)

    barrier = pltpu.get_barrier_semaphore()

    @pl.loop(1, seq_count)
    def _(k):
        pl.semaphore_signal(
            barrier, inc=1, device_id=seq_device(lax.rem(me + k, seq_count)), device_id_type=MESH
        )

    last = SUBS - 1 + valid
    second = jnp.maximum(last - 1, SUBS)

    @pl.loop(0, groups)
    def _(g):
        for p in range(3):
            padded[p, g, SUBS : SUBS + cap, :] = streams[p, :, lanes(g)].astype(jnp.float32)
            tail[g, p : p + 1, :] = padded[p, g, pl.ds(last, 1), :]
            tail[g, 3 + p : 4 + p, :] = padded[p, g, pl.ds(second, 1), :]
        tail[g, 6:8, :] = jnp.zeros((2, LANES), jnp.float32)

    pl.semaphore_wait(barrier, seq_count - 1)

    def halo_copy(distance):
        target = lax.rem(me + distance, seq_count)
        return pltpu.make_async_remote_copy(
            src_ref=tail, dst_ref=halo.at[distance - 1], send_sem=halo_send.at[distance - 1],
            recv_sem=halo_recv.at[distance - 1], device_id=seq_device(target), device_id_type=MESH,
        )

    for distance in (1, 2):
        halo_copy(distance).start()
    for distance in (1, 2):
        halo_copy(distance).wait_recv()

    row = lax.broadcasted_iota(jnp.int32, (cap, LANES), 0)
    before_size = sizes[lax.rem(me + seq_count - 1, seq_count)]

    @pl.loop(0, groups)
    def _(g):
        at = lanes(g)
        features = []
        for p in range(3):
            last_one = jnp.where(me >= 1, halo[0, g, p : p + 1, :], 0.0)
            own_second = halo[0, g, 3 + p : 4 + p, :]
            far_last = jnp.where(me >= 2, halo[1, g, p : p + 1, :], 0.0)
            last_two = jnp.where(me >= 1, jnp.where(before_size >= 2, own_second, far_last), 0.0)
            padded[p, g, 6:7, :] = last_two
            padded[p, g, 7:8, :] = last_one
            features.append(
                taps[p, 0:1, at] * padded[p, g, 8 : 8 + cap, :]
                + taps[p, 1:2, at] * padded[p, g, 7 : 7 + cap, :]
                + taps[p, 2:3, at] * padded[p, g, 6 : 6 + cap, :]
            )
        query[g] = features[0].astype(jnp.bfloat16).astype(jnp.float32)
        product = (features[1] * features[2]).astype(jnp.bfloat16).astype(jnp.float32)
        gated[g] = jnp.where(row < valid, product, 0.0)

    def mode_rows(ref, at):
        return [jnp.broadcast_to(ref[m : m + 1, at], (SUBS, LANES)) for m in range(modes)]

    @pl.loop(0, groups)
    def _(g):
        at = lanes(g)
        decay = [jnp.exp(-d) for d in mode_rows(damping, at)]
        weight = mode_rows(residue, at)

        def step(i, states):
            u = gated[g, pl.ds(i, SUBS, stride=step_rows), :]
            return tuple(a * h + r * u for a, h, r in zip(decay, states, weight, strict=True))

        zero = jnp.zeros((SUBS, LANES), jnp.float32)
        states = lax.fori_loop(0, step_rows, step, (zero,) * modes, unroll=4)
        left_over = (cap - valid).astype(jnp.float32)
        for m in range(modes):
            rate = damping[m : m + 1, at]
            total = states[m]
            for by in (1, 2, 4):
                total = total + jnp.exp(-rate * (step_rows * by)) * shift_down(total, by)
            partial[g, m] = shift_down(total, 1)
            ends[m, pl.ds(g, 1), :] = total[SUBS - 1 : SUBS, :] * jnp.exp(rate * left_over)

    def end_copy(owner):
        return pltpu.make_async_remote_copy(
            src_ref=ends.at[pl.ds(owner * per_owner, per_owner)], dst_ref=end_in.at[me],
            send_sem=end_send.at[owner], recv_sem=end_recv.at[me],
            device_id=seq_device(owner), device_id_type=MESH,
        )

    def end_arrival(source):
        return pltpu.make_async_remote_copy(
            src_ref=ends.at[pl.ds(0, per_owner)], dst_ref=end_in.at[source],
            send_sem=end_send.at[0], recv_sem=end_recv.at[source],
            device_id=seq_device(source), device_id_type=MESH,
        )

    def carry_copy(target):
        return pltpu.make_async_remote_copy(
            src_ref=carry_out.at[target], dst_ref=carry_in.at[me],
            send_sem=carry_send.at[target], recv_sem=carry_recv.at[me],
            device_id=seq_device(target), device_id_type=MESH,
        )

    def carry_arrival(owner):
        return pltpu.make_async_remote_copy(
            src_ref=carry_out.at[0], dst_ref=carry_in.at[owner],
            send_sem=carry_send.at[0], recv_sem=carry_recv.at[owner],
            device_id=seq_device(owner), device_id_type=MESH,
        )

    @pl.loop(0, owners)
    def _(k):
        owner = lax.rem(me + k, owners)

        @pl.when(owner != me)
        def _():
            end_copy(owner).start()

    @pl.when(me < owners)
    def _():
        end_in[me] = ends[pl.ds(me * per_owner, per_owner)]
        mode = lax.broadcasted_iota(jnp.int32, (modes, LANES), 0)
        for j in range(per_owner):
            for g in range(groups):
                block = damping[:, g * LANES : (g + 1) * LANES]
                rates_own[j, g : g + 1, :] = jnp.sum(
                    jnp.where(mode == me * per_owner + j, block, 0.0), axis=0, keepdims=True
                )

        @pl.loop(0, seq_count)
        def _(source):
            @pl.when(source != me)
            def _():
                end_arrival(source).wait_recv()

        rate = rates_own[...]

        def advance(source, carry):
            carry_out[source] = carry
            return jnp.exp(-rate * sizes[source].astype(jnp.float32)) * carry + end_in[source]

        lax.fori_loop(0, seq_count, advance, jnp.zeros_like(rate), unroll=8)
        carry_in[me] = carry_out[me]

        @pl.loop(0, seq_count)
        def _(target):
            @pl.when(target != me)
            def _():
                carry_copy(target).start()

    @pl.loop(0, owners)
    def _(owner):
        @pl.when(owner != me)
        def _():
            carry_arrival(owner).wait_recv()

    def z_copy(g):
        return pltpu.make_async_remote_copy(
            src_ref=hidden.at[g], dst_ref=gathered.at[me], send_sem=z_send.at[g],
            recv_sem=z_recv.at[my_z], device_id={"z": g}, device_id_type=MESH,
        )

    def z_arrival(z):
        return pltpu.make_async_remote_copy(
            src_ref=hidden.at[0], dst_ref=gathered.at[my_x * z_count + z], send_sem=z_send.at[0],
            recv_sem=z_recv.at[z], device_id={"z": z}, device_id_type=MESH,
        )

    own_copy = pltpu.make_async_copy(hidden.at[my_z], gathered.at[me], local_sem)

    @pl.loop(0, groups)
    def _(k):
        g = lax.rem(my_z + 1 + k, groups)
        at = lanes(g)
        rates = mode_rows(damping, at)
        decay = [jnp.exp(-d) for d in rates]
        weight = mode_rows(residue, at)
        sub = lax.broadcasted_iota(jnp.int32, (SUBS, LANES), 0).astype(jnp.float32) * step_rows
        start = tuple(
            partial[g, m]
            + jnp.exp(-rates[m] * sub)
            * carry_in[m // per_owner, m % per_owner, pl.ds(g, 1), :]
            for m in range(modes)
        )

        def step(i, states):
            rows = pl.ds(i, SUBS, stride=step_rows)
            u = gated[g, rows, :]
            states = tuple(a * h + r * u for a, h, r in zip(decay, states, weight, strict=True))
            mixed[rows, :] = tree_sum(list(states))
            return states

        lax.fori_loop(0, step_rows, step, start, unroll=4)
        conv = mixed[...] + direct[0:1, at] * gated[g]
        hidden[g] = (query[g] * conv).astype(jnp.bfloat16)

        @pl.when(g != my_z)
        def _():
            z_copy(g).start()

        @pl.when(g == my_z)
        def _():
            own_copy.start()

    right, left = lax.rem(my_x + 1, x_count), lax.rem(my_x + x_count - 1, x_count)
    half = cap // 2

    def x_copy(source_x, z, to, send, recv, first, rows):
        slot = source_x * z_count + z
        view = gathered.at[slot, pl.ds(first, rows)]
        return pltpu.make_async_remote_copy(
            src_ref=view, dst_ref=view, send_sem=send.at[z], recv_sem=recv.at[z],
            device_id={"x": to}, device_id_type=MESH,
        )

    def to_right(source_x, z):
        return x_copy(source_x, z, right, right_send, right_recv, 0, cap)

    def to_left(source_x, z):
        return x_copy(source_x, z, left, left_send, left_recv, 0, cap)

    def far_right(source_x, z):
        return x_copy(source_x, z, right, far_a_send, far_a_recv, 0, half)

    def far_left(source_x, z):
        return x_copy(source_x, z, left, far_b_send, far_b_recv, half, half)

    def arrival_order(k):
        return lax.rem(my_z + 2 * z_count - 1 - k, z_count)

    lag = min(2, z_count)

    @pl.loop(0, z_count + lag)
    def _(k):
        @pl.when(k < z_count)
        def _():
            z = arrival_order(k)

            @pl.when(z != my_z)
            def _():
                z_arrival(z).wait_recv()

            @pl.when(z == my_z)
            def _():
                own_copy.wait()

            to_right(my_x, z).start()
            to_left(my_x, z).start()

        @pl.when(k >= lag)
        def _():
            z = arrival_order(k - lag)
            to_right(left, z).wait_recv()
            far_right(left, z).start()
            to_left(right, z).wait_recv()
            far_left(right, z).start()

    opposite = lax.rem(my_x + 2, x_count)

    @pl.loop(0, z_count)
    def _(z):
        far_right(opposite, z).wait_recv()
        far_left(opposite, z).wait_recv()
        far_right(left, z).wait_send()
        far_left(right, z).wait_send()
        to_right(my_x, z).wait_send()
        to_left(my_x, z).wait_send()

        @pl.when(z != my_z)
        def _():
            z_copy(z).wait_send()

    for distance in (1, 2):
        halo_copy(distance).wait_send()

    @pl.loop(0, owners)
    def _(owner):
        @pl.when(owner != me)
        def _():
            end_copy(owner).wait_send()

    @pl.when(me < owners)
    def _():
        @pl.loop(0, seq_count)
        def _(target):
            @pl.when(target != me)
            def _():
                carry_copy(target).wait_send()


def conv_call(dims, streams, sizes, taps, residue, damping, direct):
    x_count, z_count = dims["x"], dims["z"]
    cap, width = streams.shape[1:]
    modes = residue.shape[0]
    seq_count = x_count * z_count
    per_owner = max(1, modes // seq_count)
    owners = modes // per_owner
    f32, bf16 = jnp.float32, jnp.bfloat16
    dma = pltpu.SemaphoreType.DMA
    vmem = pl.BlockSpec(memory_space=pltpu.VMEM)
    return pl.pallas_call(
        functools.partial(conv_kernel, x_count, z_count),
        out_shape=jax.ShapeDtypeStruct((seq_count, cap, LANES), bf16),
        in_specs=[pl.BlockSpec(memory_space=pltpu.SMEM)] + [vmem] * 5,
        out_specs=pl.BlockSpec(memory_space=pl.ANY),
        scratch_shapes=[
            pltpu.VMEM((3, z_count, cap + SUBS, LANES), f32),
            pltpu.VMEM((z_count, SUBS, LANES), f32),
            pltpu.VMEM((per_owner, z_count, LANES), f32),
            pltpu.VMEM((z_count, cap, LANES), f32),
            pltpu.VMEM((z_count, cap, LANES), f32),
            pltpu.VMEM((cap, LANES), f32),
            pltpu.VMEM((z_count, modes, SUBS, LANES), f32),
            pltpu.VMEM((modes, z_count, LANES), f32),
            pltpu.VMEM((seq_count, per_owner, z_count, LANES), f32),
            pltpu.VMEM((seq_count, per_owner, z_count, LANES), f32),
            pltpu.VMEM((owners, per_owner, z_count, LANES), f32),
            pltpu.VMEM((z_count, cap, LANES), bf16),
            pltpu.VMEM((2, z_count, SUBS, LANES), f32),
            dma((2,)), dma((2,)),
            dma((owners,)), dma((seq_count,)), dma((seq_count,)), dma((owners,)),
        ]
        + [dma((z_count,))] * 10
        + [dma],
        compiler_params=pltpu.CompilerParams(
            collective_id=0, has_side_effects=True, vmem_limit_bytes=24 << 20
        ),
        name="conv_shuffle",
    )(sizes, streams, taps, residue, damping, direct)


def select_kernel(z_count, former, updated, remaining, pieces, chosen, sequence):
    seq_count, cap, _ = pieces.shape

    def place(s, start):
        sequence[pl.ds(start, cap), :] = pieces[s].astype(jnp.float32)
        return start + former[s]

    lax.fori_loop(0, seq_count, place, 0)
    row = lax.broadcasted_iota(jnp.int32, (cap, LANES), 0)
    first = lax.axis_index("x") * z_count
    chosen[...] = jnp.zeros_like(chosen)

    def pick(k, start):
        own = remaining[k] - first

        @pl.when(jnp.logical_and(own >= 0, own < z_count))
        def _():
            rows = sequence[pl.ds(start, cap), :]
            chosen[own] = jnp.where(row < updated[k], rows, 0.0).astype(jnp.bfloat16)

        return start + updated[k]

    lax.fori_loop(0, updated.shape[0], pick, 0)


def select_call(dims, seq_len, pieces, former, updated, remaining):
    cap = pieces.shape[1]
    smem = pl.BlockSpec(memory_space=pltpu.SMEM)
    vmem = pl.BlockSpec(memory_space=pltpu.VMEM)
    return pl.pallas_call(
        functools.partial(select_kernel, dims["z"]),
        out_shape=jax.ShapeDtypeStruct((dims["z"], cap, LANES), jnp.bfloat16),
        in_specs=[smem] * 3 + [vmem],
        out_specs=vmem,
        scratch_shapes=[pltpu.VMEM((seq_len + cap, LANES), jnp.float32)],
        compiler_params=pltpu.CompilerParams(vmem_limit_bytes=24 << 20),
        name="reorder_rows",
    )(former, updated, remaining, pieces)


def project_kernel(
    x_count, z_count, y_count,
    chosen, projector, out,
    rows_in, own_sum, partial_out, partial_in,
    z_send, z_recv, right_send, right_recv, left_send, left_recv,
    far_a_send, far_a_recv, far_b_send, far_b_recv, core_send, core_recv,
    sum_send, sum_recv, local_sem,
):
    cap = out.shape[0]
    parts, tile = partial_out.shape[1], partial_out.shape[3]
    my_x, my_z = lax.axis_index("x"), lax.axis_index("z")
    my_y, my_core = lax.axis_index("y"), lax.axis_index("core")
    right, left = lax.rem(my_y + 1, y_count), lax.rem(my_y + y_count - 1, y_count)
    opposite = lax.rem(my_y + 2, y_count)
    other = 1 - my_core
    half = cap // 2
    diagonal = my_x == my_y

    def crossed(z):
        return {"x": my_y, "y": my_x, "z": z}

    def is_me(z):
        return jnp.logical_and(diagonal, z == my_z)

    barrier = pltpu.get_barrier_semaphore()

    @pl.loop(0, z_count)
    def _(k):
        z = lax.rem(my_z + k, z_count)

        @pl.when(jnp.logical_not(is_me(z)))
        def _():
            pl.semaphore_signal(barrier, inc=1, device_id=crossed(z), device_id_type=MESH)

    for to in ({"y": right}, {"y": left}, {"core": other}):
        pl.semaphore_signal(barrier, inc=1, device_id=to, device_id_type=MESH)
    for k in range(1, x_count):
        to = {"x": lax.rem(my_x + k, x_count)}
        pl.semaphore_signal(barrier, inc=1, device_id=to, device_id_type=MESH)

    @pl.when(diagonal)
    def _():
        pl.semaphore_wait(barrier, z_count - 1 + 3 + x_count - 1)

    @pl.when(jnp.logical_not(diagonal))
    def _():
        pl.semaphore_wait(barrier, z_count + 3 + x_count - 1)

    def columns(core, z):
        return pl.ds(pl.multiple_of((core * z_count + z) * LANES, LANES), LANES)

    def z_copy(z):
        return pltpu.make_async_remote_copy(
            src_ref=chosen.at[z], dst_ref=rows_in.at[my_x, :, columns(my_core, my_z)],
            send_sem=z_send.at[z], recv_sem=z_recv.at[my_z],
            device_id=crossed(z), device_id_type=MESH,
        )

    def z_arrival(z):
        return pltpu.make_async_remote_copy(
            src_ref=chosen.at[0], dst_ref=rows_in.at[my_y, :, columns(my_core, z)],
            send_sem=z_send.at[0], recv_sem=z_recv.at[z],
            device_id=crossed(z), device_id_type=MESH,
        )

    own_copy = pltpu.make_async_copy(
        chosen.at[my_z], rows_in.at[my_x, :, columns(my_core, my_z)], local_sem
    )

    @pl.when(diagonal)
    def _():
        own_copy.start()

    @pl.loop(0, z_count)
    def _(k):
        z = lax.rem(my_z + k, z_count)

        @pl.when(jnp.logical_not(is_me(z)))
        def _():
            z_copy(z).start()

    def onward(y, core, z, to, send, recv, first, rows):
        view = rows_in.at[y, pl.ds(first, rows), columns(core, z)]
        return pltpu.make_async_remote_copy(
            src_ref=view, dst_ref=view, send_sem=send, recv_sem=recv,
            device_id=to, device_id_type=MESH,
        )

    def to_right(y, z):
        return onward(y, my_core, z, {"y": right}, right_send.at[z], right_recv.at[z], 0, cap)

    def to_left(y, z):
        return onward(y, my_core, z, {"y": left}, left_send.at[z], left_recv.at[z], 0, cap)

    def far_right(y, z):
        return onward(y, my_core, z, {"y": right}, far_a_send.at[z], far_a_recv.at[z], 0, half)

    def far_left(y, z):
        return onward(y, my_core, z, {"y": left}, far_b_send.at[z], far_b_recv.at[z], half, half)

    def to_core(y, core, z):
        return onward(y, core, z, {"core": other}, core_send.at[y, z], core_recv.at[y, z], 0, cap)

    def sum_copy(owner, part):
        return pltpu.make_async_remote_copy(
            src_ref=partial_out.at[owner, part], dst_ref=partial_in.at[my_x, part],
            send_sem=sum_send.at[owner, part], recv_sem=sum_recv.at[my_x, part],
            device_id={"x": owner}, device_id_type=MESH,
        )

    def sum_arrival(source, part):
        return pltpu.make_async_remote_copy(
            src_ref=partial_out.at[0, part], dst_ref=partial_in.at[source, part],
            send_sem=sum_send.at[0, part], recv_sem=sum_recv.at[source, part],
            device_id={"x": source}, device_id_type=MESH,
        )

    def project(owner):
        @pl.loop(0, z_count)
        def _(z):
            to_core(owner, other, z).wait_recv()

        @pl.loop(0, parts)
        def _(part):
            at = pl.ds(pl.multiple_of(part * tile, tile), tile)
            total = jnp.dot(
                rows_in[owner], projector[:, at], preferred_element_type=jnp.float32
            )

            @pl.when(owner == my_x)
            def _():
                own_sum[:, at] = total

            @pl.when(owner != my_x)
            def _():
                partial_out[owner, part] = total.astype(jnp.bfloat16)
                sum_copy(owner, part).start()

    def arrival_order(k):
        return lax.rem(my_z + z_count - k, z_count)

    lag = min(2, z_count)

    @pl.loop(0, z_count + lag)
    def _(k):
        @pl.when(k < z_count)
        def _():
            z = arrival_order(k)

            @pl.when(jnp.logical_not(is_me(z)))
            def _():
                z_arrival(z).wait_recv()

            @pl.when(is_me(z))
            def _():
                own_copy.wait()

            to_right(my_y, z).start()
            to_left(my_y, z).start()
            to_core(my_y, my_core, z).start()

        @pl.when(k >= lag)
        def _():
            z = arrival_order(k - lag)
            to_right(left, z).wait_recv()
            far_right(left, z).start()
            to_core(left, my_core, z).start()
            to_left(right, z).wait_recv()
            far_left(right, z).start()
            to_core(right, my_core, z).start()

    project(my_y)
    project(left)
    project(right)

    @pl.loop(0, z_count)
    def _(k):
        z = arrival_order(k)
        far_right(opposite, z).wait_recv()
        far_left(opposite, z).wait_recv()
        to_core(opposite, my_core, z).start()

    project(opposite)

    @pl.loop(0, parts)
    def _(part):
        at = pl.ds(pl.multiple_of(part * tile, tile), tile)
        total = own_sum[:, at]
        for k in range(1, x_count):
            source = lax.rem(my_x + k, x_count)
            sum_arrival(source, part).wait_recv()
            total = total + partial_in[source, part].astype(jnp.float32)
        out[:, at] = total.astype(jnp.bfloat16)
        for k in range(1, x_count):
            sum_copy(lax.rem(my_x + k, x_count), part).wait_send()

    @pl.loop(0, z_count)
    def _(z):
        for y in range(y_count):
            to_core(y, my_core, z).wait_send()
        to_right(my_y, z).wait_send()
        to_left(my_y, z).wait_send()
        far_right(left, z).wait_send()
        far_left(right, z).wait_send()

        @pl.when(jnp.logical_not(is_me(z)))
        def _():
            z_copy(z).wait_send()


def project_call(dims, chosen, projector):
    x_count, y_count = dims["x"], dims["y"]
    z_count, cap, _ = chosen.shape
    depth, width = projector.shape
    tile = min(256, width)
    parts = width // tile
    f32, bf16 = jnp.float32, jnp.bfloat16
    dma = pltpu.SemaphoreType.DMA
    vmem = pl.BlockSpec(memory_space=pltpu.VMEM)
    return pl.pallas_call(
        functools.partial(project_kernel, x_count, z_count, y_count),
        out_shape=jax.ShapeDtypeStruct((cap, width), bf16),
        in_specs=[vmem, vmem],
        out_specs=vmem,
        scratch_shapes=[
            pltpu.VMEM((y_count, cap, depth), bf16),
            pltpu.VMEM((cap, width), f32),
            pltpu.VMEM((x_count, parts, cap, tile), bf16),
            pltpu.VMEM((x_count, parts, cap, tile), bf16),
        ]
        + [dma((z_count,))] * 10
        + [dma((y_count, z_count))] * 2
        + [dma((x_count, parts))] * 2
        + [dma],
        compiler_params=pltpu.CompilerParams(
            collective_id=1, has_side_effects=True, vmem_limit_bytes=40 << 20
        ),
        name="project_rows",
    )(chosen, projector)


def shards(
    dims,
    input_triple_streams,
    former_piece_sizes,
    updated_piece_sizes,
    remaining_indices,
    short_causal_filters,
    pole_coefficients,
    pole_damping,
    direct_coefficient,
    final_projector,
):
    cap = input_triple_streams.shape[0]
    seq_len = cap * 4 // 5 * dims["x"] * dims["z"]

    projector = lax.all_gather(final_projector, "z", axis=0, tiled=True)
    pieces = conv_call(
        dims,
        jnp.transpose(input_triple_streams, (1, 0, 2)),
        former_piece_sizes,
        short_causal_filters,
        pole_coefficients,
        pole_damping,
        direct_coefficient[None, :],
    )
    chosen = select_call(
        dims, seq_len, pieces, former_piece_sizes, updated_piece_sizes, remaining_indices
    )
    return project_call(dims, chosen, projector)


def solution(mesh):
    grid = (4, mesh.shape["seq"] // 4, mesh.shape["chan"] // 2, 2)
    dims = dict(zip(AXES, grid, strict=True))
    rows, channels = ("x", "z"), ("y", "core")
    return jax.shard_map(
        functools.partial(shards, dims),
        mesh=Mesh(mesh.devices.reshape(grid), AXES),
        in_specs=(
            P(rows, None, channels),
            P(),
            P(),
            P(),
            P(None, None, channels),
            P(None, channels),
            P(None, channels),
            P(channels),
            P(rows, channels),
        ),
        out_specs=P(rows, channels),
        check_vma=False,
    )
```

```python
import functools

import jax
import jax.numpy as jnp
from jax import lax
from jax.experimental import pallas as pl
from jax.experimental.pallas import tpu as pltpu
from jax.sharding import Mesh
from jax.sharding import PartitionSpec as P

MESH = pl.DeviceIdType.MESH
LANES = 128
SUBS = 8
AXES = ("x_high", "x_low", "z", "y", "core")
SEQ = ("x_high", "x_low", "z")


def x_index():
    return lax.axis_index("x_high") * 2 + lax.axis_index("x_low")


def at_x(x):
    return {"x_high": x // 2, "x_low": lax.rem(x, 2)}


def shift_down(value, by):
    row = lax.broadcasted_iota(jnp.int32, value.shape, 0)
    return jnp.where(row >= by, pltpu.roll(value, by, 0), 0.0)


def tree_sum(terms):
    while len(terms) > 1:
        terms = [a + b for a, b in zip(terms[::2], terms[1::2], strict=True)]
    return terms[0]


def conv_kernel(
    x_count, z_count,
    sizes, streams, taps, residue, damping, direct,
    gathered,
    padded, tail, rates_own, query, gated, mixed, partial, ends, end_in, carry_out, carry_in, hidden, halo,
    halo_send, halo_recv, end_send, end_recv, carry_send, carry_recv,
    z_send, z_recv, right_send, right_recv, left_send, left_recv,
    far_a_send, far_a_recv, far_b_send, far_b_recv, local_sem,
):
    modes = residue.shape[0]
    cap = streams.shape[1]
    groups = z_count
    step_rows = cap // SUBS
    seq_count = x_count * z_count
    per_owner = max(1, modes // seq_count)
    owners = modes // per_owner
    my_x, my_z = x_index(), lax.axis_index("z")
    me = my_x * z_count + my_z
    valid = sizes[me]

    def seq_device(index):
        return {**at_x(index // z_count), "z": lax.rem(index, z_count)}

    def lanes(g):
        return pl.ds(pl.multiple_of(g * LANES, LANES), LANES)

    barrier = pltpu.get_barrier_semaphore()

    @pl.loop(1, seq_count)
    def _(k):
        pl.semaphore_signal(
            barrier, inc=1, device_id=seq_device(lax.rem(me + k, seq_count)), device_id_type=MESH
        )

    last = SUBS - 1 + valid
    second = jnp.maximum(last - 1, SUBS)

    @pl.loop(0, groups)
    def _(g):
        for p in range(3):
            padded[p, g, SUBS : SUBS + cap, :] = streams[p, :, lanes(g)].astype(jnp.float32)
            tail[g, p : p + 1, :] = padded[p, g, pl.ds(last, 1), :]
            tail[g, 3 + p : 4 + p, :] = padded[p, g, pl.ds(second, 1), :]
        tail[g, 6:8, :] = jnp.zeros((2, LANES), jnp.float32)

    pl.semaphore_wait(barrier, seq_count - 1)

    def halo_copy(distance):
        target = lax.rem(me + distance, seq_count)
        return pltpu.make_async_remote_copy(
            src_ref=tail, dst_ref=halo.at[distance - 1], send_sem=halo_send.at[distance - 1],
            recv_sem=halo_recv.at[distance - 1], device_id=seq_device(target), device_id_type=MESH,
        )

    for distance in (1, 2):
        halo_copy(distance).start()
    for distance in (1, 2):
        halo_copy(distance).wait_recv()

    row = lax.broadcasted_iota(jnp.int32, (cap, LANES), 0)
    before_size = sizes[lax.rem(me + seq_count - 1, seq_count)]

    @pl.loop(0, groups)
    def _(g):
        at = lanes(g)
        features = []
        for p in range(3):
            last_one = jnp.where(me >= 1, halo[0, g, p : p + 1, :], 0.0)
            own_second = halo[0, g, 3 + p : 4 + p, :]
            far_last = jnp.where(me >= 2, halo[1, g, p : p + 1, :], 0.0)
            last_two = jnp.where(me >= 1, jnp.where(before_size >= 2, own_second, far_last), 0.0)
            padded[p, g, 6:7, :] = last_two
            padded[p, g, 7:8, :] = last_one
            features.append(
                taps[p, 0:1, at] * padded[p, g, 8 : 8 + cap, :]
                + taps[p, 1:2, at] * padded[p, g, 7 : 7 + cap, :]
                + taps[p, 2:3, at] * padded[p, g, 6 : 6 + cap, :]
            )
        query[g] = features[0].astype(jnp.bfloat16).astype(jnp.float32)
        product = (features[1] * features[2]).astype(jnp.bfloat16).astype(jnp.float32)
        gated[g] = jnp.where(row < valid, product, 0.0)

    def mode_rows(ref, at):
        return [jnp.broadcast_to(ref[m : m + 1, at], (SUBS, LANES)) for m in range(modes)]

    @pl.loop(0, groups)
    def _(g):
        at = lanes(g)
        decay = [jnp.exp(-d) for d in mode_rows(damping, at)]
        weight = mode_rows(residue, at)

        def step(i, states):
            u = gated[g, pl.ds(i, SUBS, stride=step_rows), :]
            return tuple(a * h + r * u for a, h, r in zip(decay, states, weight, strict=True))

        zero = jnp.zeros((SUBS, LANES), jnp.float32)
        states = lax.fori_loop(0, step_rows, step, (zero,) * modes, unroll=4)
        left_over = (cap - valid).astype(jnp.float32)
        for m in range(modes):
            rate = damping[m : m + 1, at]
            total = states[m]
            for by in (1, 2, 4):
                total = total + jnp.exp(-rate * (step_rows * by)) * shift_down(total, by)
            partial[g, m] = shift_down(total, 1)
            ends[m, pl.ds(g, 1), :] = total[SUBS - 1 : SUBS, :] * jnp.exp(rate * left_over)

    def end_copy(owner):
        return pltpu.make_async_remote_copy(
            src_ref=ends.at[pl.ds(owner * per_owner, per_owner)], dst_ref=end_in.at[me],
            send_sem=end_send.at[owner], recv_sem=end_recv.at[me],
            device_id=seq_device(owner), device_id_type=MESH,
        )

    def end_arrival(source):
        return pltpu.make_async_remote_copy(
            src_ref=ends.at[pl.ds(0, per_owner)], dst_ref=end_in.at[source],
            send_sem=end_send.at[0], recv_sem=end_recv.at[source],
            device_id=seq_device(source), device_id_type=MESH,
        )

    def carry_copy(target):
        return pltpu.make_async_remote_copy(
            src_ref=carry_out.at[target], dst_ref=carry_in.at[me],
            send_sem=carry_send.at[target], recv_sem=carry_recv.at[me],
            device_id=seq_device(target), device_id_type=MESH,
        )

    def carry_arrival(owner):
        return pltpu.make_async_remote_copy(
            src_ref=carry_out.at[0], dst_ref=carry_in.at[owner],
            send_sem=carry_send.at[0], recv_sem=carry_recv.at[owner],
            device_id=seq_device(owner), device_id_type=MESH,
        )

    @pl.loop(0, owners)
    def _(k):
        owner = lax.rem(me + k, owners)

        @pl.when(owner != me)
        def _():
            end_copy(owner).start()

    @pl.when(me < owners)
    def _():
        end_in[me] = ends[pl.ds(me * per_owner, per_owner)]
        mode = lax.broadcasted_iota(jnp.int32, (modes, LANES), 0)
        for j in range(per_owner):
            for g in range(groups):
                block = damping[:, g * LANES : (g + 1) * LANES]
                rates_own[j, g : g + 1, :] = jnp.sum(
                    jnp.where(mode == me * per_owner + j, block, 0.0), axis=0, keepdims=True
                )

        @pl.loop(0, seq_count)
        def _(source):
            @pl.when(source != me)
            def _():
                end_arrival(source).wait_recv()

        rate = rates_own[...]

        def advance(source, carry):
            carry_out[source] = carry
            return jnp.exp(-rate * sizes[source].astype(jnp.float32)) * carry + end_in[source]

        lax.fori_loop(0, seq_count, advance, jnp.zeros_like(rate), unroll=8)
        carry_in[me] = carry_out[me]

        @pl.loop(0, seq_count)
        def _(target):
            @pl.when(target != me)
            def _():
                carry_copy(target).start()

    @pl.loop(0, owners)
    def _(owner):
        @pl.when(owner != me)
        def _():
            carry_arrival(owner).wait_recv()

    def z_copy(g):
        return pltpu.make_async_remote_copy(
            src_ref=hidden.at[g], dst_ref=gathered.at[me], send_sem=z_send.at[g],
            recv_sem=z_recv.at[my_z], device_id={"z": g}, device_id_type=MESH,
        )

    def z_arrival(z):
        return pltpu.make_async_remote_copy(
            src_ref=hidden.at[0], dst_ref=gathered.at[my_x * z_count + z], send_sem=z_send.at[0],
            recv_sem=z_recv.at[z], device_id={"z": z}, device_id_type=MESH,
        )

    own_copy = pltpu.make_async_copy(hidden.at[my_z], gathered.at[me], local_sem)

    @pl.loop(0, groups)
    def _(k):
        g = lax.rem(my_z + 1 + k, groups)
        at = lanes(g)
        rates = mode_rows(damping, at)
        decay = [jnp.exp(-d) for d in rates]
        weight = mode_rows(residue, at)
        sub = lax.broadcasted_iota(jnp.int32, (SUBS, LANES), 0).astype(jnp.float32) * step_rows
        start = tuple(
            partial[g, m]
            + jnp.exp(-rates[m] * sub)
            * carry_in[m // per_owner, m % per_owner, pl.ds(g, 1), :]
            for m in range(modes)
        )

        def step(i, states):
            rows = pl.ds(i, SUBS, stride=step_rows)
            u = gated[g, rows, :]
            states = tuple(a * h + r * u for a, h, r in zip(decay, states, weight, strict=True))
            mixed[rows, :] = tree_sum(list(states))
            return states

        lax.fori_loop(0, step_rows, step, start, unroll=4)
        conv = mixed[...] + direct[0:1, at] * gated[g]
        hidden[g] = (query[g] * conv).astype(jnp.bfloat16)

        @pl.when(g != my_z)
        def _():
            z_copy(g).start()

        @pl.when(g == my_z)
        def _():
            own_copy.start()

    right, left = lax.rem(my_x + 1, x_count), lax.rem(my_x + x_count - 1, x_count)
    half = cap // 2

    def x_copy(source_x, z, to, send, recv, first, rows):
        slot = source_x * z_count + z
        view = gathered.at[slot, pl.ds(first, rows)]
        return pltpu.make_async_remote_copy(
            src_ref=view, dst_ref=view, send_sem=send.at[z], recv_sem=recv.at[z],
            device_id=at_x(to), device_id_type=MESH,
        )

    def to_right(source_x, z):
        return x_copy(source_x, z, right, right_send, right_recv, 0, cap)

    def to_left(source_x, z):
        return x_copy(source_x, z, left, left_send, left_recv, 0, cap)

    def far_right(source_x, z):
        return x_copy(source_x, z, right, far_a_send, far_a_recv, 0, half)

    def far_left(source_x, z):
        return x_copy(source_x, z, left, far_b_send, far_b_recv, half, half)

    def arrival_order(k):
        return lax.rem(my_z + 2 * z_count - 1 - k, z_count)

    lag = min(2, z_count)

    @pl.loop(0, z_count + lag)
    def _(k):
        @pl.when(k < z_count)
        def _():
            z = arrival_order(k)

            @pl.when(z != my_z)
            def _():
                z_arrival(z).wait_recv()

            @pl.when(z == my_z)
            def _():
                own_copy.wait()

            to_right(my_x, z).start()
            to_left(my_x, z).start()

        @pl.when(k >= lag)
        def _():
            z = arrival_order(k - lag)
            to_right(left, z).wait_recv()
            far_right(left, z).start()
            to_left(right, z).wait_recv()
            far_left(right, z).start()

    opposite = lax.rem(my_x + 2, x_count)

    @pl.loop(0, z_count)
    def _(z):
        far_right(opposite, z).wait_recv()
        far_left(opposite, z).wait_recv()
        far_right(left, z).wait_send()
        far_left(right, z).wait_send()
        to_right(my_x, z).wait_send()
        to_left(my_x, z).wait_send()

        @pl.when(z != my_z)
        def _():
            z_copy(z).wait_send()

    for distance in (1, 2):
        halo_copy(distance).wait_send()

    @pl.loop(0, owners)
    def _(owner):
        @pl.when(owner != me)
        def _():
            end_copy(owner).wait_send()

    @pl.when(me < owners)
    def _():
        @pl.loop(0, seq_count)
        def _(target):
            @pl.when(target != me)
            def _():
                carry_copy(target).wait_send()


def conv_call(dims, streams, sizes, taps, residue, damping, direct):
    x_count, z_count = dims["x"], dims["z"]
    cap, width = streams.shape[1:]
    modes = residue.shape[0]
    seq_count = x_count * z_count
    per_owner = max(1, modes // seq_count)
    owners = modes // per_owner
    f32, bf16 = jnp.float32, jnp.bfloat16
    dma = pltpu.SemaphoreType.DMA
    vmem = pl.BlockSpec(memory_space=pltpu.VMEM)
    return pl.pallas_call(
        functools.partial(conv_kernel, x_count, z_count),
        out_shape=jax.ShapeDtypeStruct((seq_count, cap, LANES), bf16),
        in_specs=[pl.BlockSpec(memory_space=pltpu.SMEM)] + [vmem] * 5,
        out_specs=pl.BlockSpec(memory_space=pl.ANY),
        scratch_shapes=[
            pltpu.VMEM((3, z_count, cap + SUBS, LANES), f32),
            pltpu.VMEM((z_count, SUBS, LANES), f32),
            pltpu.VMEM((per_owner, z_count, LANES), f32),
            pltpu.VMEM((z_count, cap, LANES), f32),
            pltpu.VMEM((z_count, cap, LANES), f32),
            pltpu.VMEM((cap, LANES), f32),
            pltpu.VMEM((z_count, modes, SUBS, LANES), f32),
            pltpu.VMEM((modes, z_count, LANES), f32),
            pltpu.VMEM((seq_count, per_owner, z_count, LANES), f32),
            pltpu.VMEM((seq_count, per_owner, z_count, LANES), f32),
            pltpu.VMEM((owners, per_owner, z_count, LANES), f32),
            pltpu.VMEM((z_count, cap, LANES), bf16),
            pltpu.VMEM((2, z_count, SUBS, LANES), f32),
            dma((2,)), dma((2,)),
            dma((owners,)), dma((seq_count,)), dma((seq_count,)), dma((owners,)),
        ]
        + [dma((z_count,))] * 10
        + [dma],
        compiler_params=pltpu.CompilerParams(
            collective_id=0, has_side_effects=True, vmem_limit_bytes=24 << 20
        ),
        name="conv_shuffle",
    )(sizes, streams, taps, residue, damping, direct)


def select_kernel(z_count, former, updated, remaining, pieces, chosen, sequence):
    seq_count, cap, _ = pieces.shape

    def place(s, start):
        sequence[pl.ds(start, cap), :] = pieces[s].astype(jnp.float32)
        return start + former[s]

    lax.fori_loop(0, seq_count, place, 0)
    row = lax.broadcasted_iota(jnp.int32, (cap, LANES), 0)
    first = x_index() * z_count
    chosen[...] = jnp.zeros_like(chosen)

    def pick(k, start):
        own = remaining[k] - first

        @pl.when(jnp.logical_and(own >= 0, own < z_count))
        def _():
            rows = sequence[pl.ds(start, cap), :]
            chosen[own] = jnp.where(row < updated[k], rows, 0.0).astype(jnp.bfloat16)

        return start + updated[k]

    lax.fori_loop(0, updated.shape[0], pick, 0)


def select_call(dims, seq_len, pieces, former, updated, remaining):
    cap = pieces.shape[1]
    smem = pl.BlockSpec(memory_space=pltpu.SMEM)
    vmem = pl.BlockSpec(memory_space=pltpu.VMEM)
    return pl.pallas_call(
        functools.partial(select_kernel, dims["z"]),
        out_shape=jax.ShapeDtypeStruct((dims["z"], cap, LANES), jnp.bfloat16),
        in_specs=[smem] * 3 + [vmem],
        out_specs=vmem,
        scratch_shapes=[pltpu.VMEM((seq_len + cap, LANES), jnp.float32)],
        compiler_params=pltpu.CompilerParams(vmem_limit_bytes=24 << 20),
        name="reorder_rows",
    )(former, updated, remaining, pieces)


def spread_kernel(
    z_count, y_count,
    chosen, rows_in,
    z_send, z_recv, right_send, right_recv, left_send, left_recv,
    far_a_send, far_a_recv, far_b_send, far_b_recv, core_send, core_recv,
    local_sem,
):
    cap = rows_in.shape[1]
    my_x, my_z = x_index(), lax.axis_index("z")
    my_y, my_core = lax.axis_index("y"), lax.axis_index("core")
    right, left = lax.rem(my_y + 1, y_count), lax.rem(my_y + y_count - 1, y_count)
    opposite = lax.rem(my_y + 2, y_count)
    other = 1 - my_core
    half = cap // 2
    stays = my_x // 2 == my_y // 2
    target_x = jnp.where(stays, my_x, 3 - my_x)
    target_y = jnp.where(stays, my_y, 3 - my_y)

    def crossed(z):
        return {**at_x(target_x), "y": target_y, "z": z}

    def is_me(z):
        return jnp.logical_and(stays, z == my_z)

    barrier = pltpu.get_barrier_semaphore()

    @pl.loop(0, z_count)
    def _(k):
        z = lax.rem(my_z + k, z_count)

        @pl.when(jnp.logical_not(is_me(z)))
        def _():
            pl.semaphore_signal(barrier, inc=1, device_id=crossed(z), device_id_type=MESH)

    for to in ({"y": right}, {"y": left}, {"core": other}):
        pl.semaphore_signal(barrier, inc=1, device_id=to, device_id_type=MESH)
    @pl.when(stays)
    def _():
        pl.semaphore_wait(barrier, z_count - 1 + 3)

    @pl.when(jnp.logical_not(stays))
    def _():
        pl.semaphore_wait(barrier, z_count + 3)

    def columns(source_y, core, z):
        block = (lax.rem(source_y, 2) * 2 + core) * z_count + z
        return pl.ds(pl.multiple_of(block * LANES, LANES), LANES)

    def place(y, core, z, first, rows):
        native = y // 2 == my_x // 2
        source_y = jnp.where(native, y, 3 - y)
        return rows_in.at[
            jnp.where(native, 0, 1), pl.ds(first, rows), columns(source_y, core, z)
        ]

    def z_copy(z):
        return pltpu.make_async_remote_copy(
            src_ref=chosen.at[z], dst_ref=rows_in.at[jnp.where(stays, 0, 1), :, columns(my_y, my_core, my_z)],
            send_sem=z_send.at[z], recv_sem=z_recv.at[my_z],
            device_id=crossed(z), device_id_type=MESH,
        )

    def z_arrival(z):
        return pltpu.make_async_remote_copy(
            src_ref=chosen.at[0], dst_ref=place(my_y, my_core, z, 0, cap),
            send_sem=z_send.at[0], recv_sem=z_recv.at[z],
            device_id=crossed(z), device_id_type=MESH,
        )

    own_copy = pltpu.make_async_copy(
        chosen.at[my_z], rows_in.at[0, :, columns(my_y, my_core, my_z)], local_sem
    )

    @pl.when(stays)
    def _():
        own_copy.start()

    @pl.loop(0, z_count)
    def _(k):
        z = lax.rem(my_z + k, z_count)

        @pl.when(jnp.logical_not(is_me(z)))
        def _():
            z_copy(z).start()

    def onward(y, core, z, to, send, recv, first, rows):
        view = place(y, core, z, first, rows)
        return pltpu.make_async_remote_copy(
            src_ref=view, dst_ref=view, send_sem=send, recv_sem=recv,
            device_id=to, device_id_type=MESH,
        )

    def to_right(y, z):
        return onward(y, my_core, z, {"y": right}, right_send.at[z], right_recv.at[z], 0, cap)

    def to_left(y, z):
        return onward(y, my_core, z, {"y": left}, left_send.at[z], left_recv.at[z], 0, cap)

    def far_right(y, z):
        return onward(y, my_core, z, {"y": right}, far_a_send.at[z], far_a_recv.at[z], 0, half)

    def far_left(y, z):
        return onward(y, my_core, z, {"y": left}, far_b_send.at[z], far_b_recv.at[z], half, half)

    def to_core(y, core, z):
        return onward(y, core, z, {"core": other}, core_send.at[y, z], core_recv.at[y, z], 0, cap)

    def arrival_order(k):
        return lax.rem(my_z + z_count - k, z_count)

    lag = min(2, z_count)

    @pl.loop(0, z_count + lag)
    def _(k):
        @pl.when(k < z_count)
        def _():
            z = arrival_order(k)

            @pl.when(jnp.logical_not(is_me(z)))
            def _():
                z_arrival(z).wait_recv()

            @pl.when(is_me(z))
            def _():
                own_copy.wait()

            to_right(my_y, z).start()
            to_left(my_y, z).start()
            to_core(my_y, my_core, z).start()

        @pl.when(k >= lag)
        def _():
            z = arrival_order(k - lag)
            to_right(left, z).wait_recv()
            far_right(left, z).start()
            to_core(left, my_core, z).start()
            to_left(right, z).wait_recv()
            far_left(right, z).start()
            to_core(right, my_core, z).start()

    @pl.loop(0, z_count)
    def _(k):
        z = arrival_order(k)
        far_right(opposite, z).wait_recv()
        far_left(opposite, z).wait_recv()
        to_core(opposite, my_core, z).start()

    @pl.loop(0, z_count)
    def _(z):
        for y in range(y_count):
            to_core(y, other, z).wait_recv()
            to_core(y, my_core, z).wait_send()
        to_right(my_y, z).wait_send()
        to_left(my_y, z).wait_send()
        far_right(left, z).wait_send()
        far_left(right, z).wait_send()

        @pl.when(jnp.logical_not(is_me(z)))
        def _():
            z_copy(z).wait_send()


def spread_call(dims, chosen):
    z_count, cap, _ = chosen.shape
    y_count = dims["y"]
    dma = pltpu.SemaphoreType.DMA
    return pl.pallas_call(
        functools.partial(spread_kernel, z_count, y_count),
        out_shape=jax.ShapeDtypeStruct((2, cap, y_count * z_count * LANES), jnp.bfloat16),
        in_specs=[pl.BlockSpec(memory_space=pltpu.VMEM)],
        out_specs=pl.BlockSpec(memory_space=pl.ANY),
        scratch_shapes=[dma((z_count,))] * 10 + [dma((y_count, z_count))] * 2 + [dma],
        compiler_params=pltpu.CompilerParams(
            collective_id=1, has_side_effects=True, vmem_limit_bytes=16 << 20
        ),
        name="spread_rows",
    )(chosen)


def project_kernel(
    rows, projector, out,
    weights, own_sum, partial_out, partial_in,
    load_sem, sum_send, sum_recv,
):
    parts, _, tile = weights.shape
    partner = at_x(3 - x_index())

    barrier = pltpu.get_barrier_semaphore()
    pl.semaphore_signal(barrier, inc=1, device_id=partner, device_id_type=MESH)

    def span(part):
        return pl.ds(pl.multiple_of(part * tile, tile), tile)

    def load(part):
        return pltpu.make_async_copy(
            projector.at[:, span(part)], weights.at[part], load_sem.at[part]
        )

    def exchange(part):
        return pltpu.make_async_remote_copy(
            src_ref=partial_out.at[part], dst_ref=partial_in.at[part],
            send_sem=sum_send.at[part], recv_sem=sum_recv.at[part],
            device_id=partner, device_id_type=MESH,
        )

    @pl.loop(0, parts)
    def _(part):
        load(part).start()

    pl.semaphore_wait(barrier, 1)

    @pl.loop(0, parts)
    def _(part):
        load(part).wait()
        partial_out[part] = jnp.dot(
            rows[1], weights[part], preferred_element_type=jnp.float32
        ).astype(jnp.bfloat16)
        exchange(part).start()

    @pl.loop(0, parts)
    def _(part):
        own_sum[part] = jnp.dot(rows[0], weights[part], preferred_element_type=jnp.float32)

    @pl.loop(0, parts)
    def _(part):
        exchange(part).wait_recv()
        total = own_sum[part] + partial_in[part].astype(jnp.float32)
        out[:, span(part)] = total.astype(jnp.bfloat16)

    @pl.loop(0, parts)
    def _(part):
        exchange(part).wait_send()


def project_call(rows, projector):
    cap = rows.shape[1]
    depth, width = projector.shape
    tile = min(256, width)
    parts = width // tile
    f32, bf16 = jnp.float32, jnp.bfloat16
    dma = pltpu.SemaphoreType.DMA
    vmem = pl.BlockSpec(memory_space=pltpu.VMEM)
    return pl.pallas_call(
        project_kernel,
        out_shape=jax.ShapeDtypeStruct((cap, width), bf16),
        in_specs=[vmem, pl.BlockSpec(memory_space=pl.ANY)],
        out_specs=vmem,
        scratch_shapes=[
            pltpu.VMEM((parts, depth, tile), bf16),
            pltpu.VMEM((parts, cap, tile), f32),
            pltpu.VMEM((parts, cap, tile), bf16),
            pltpu.VMEM((parts, cap, tile), bf16),
            dma((parts,)), dma((parts,)), dma((parts,)),
        ],
        compiler_params=pltpu.CompilerParams(
            collective_id=2, has_side_effects=True, vmem_limit_bytes=32 << 20
        ),
        name="project_rows",
    )(rows, projector)


def shards(
    dims,
    input_triple_streams,
    former_piece_sizes,
    updated_piece_sizes,
    remaining_indices,
    short_causal_filters,
    pole_coefficients,
    pole_damping,
    direct_coefficient,
    final_projector,
):
    cap = input_triple_streams.shape[0]
    seq_len = cap * 4 // 5 * dims["x"] * dims["z"]

    projector = lax.all_gather(final_projector, ("x_low", "z"), axis=0, tiled=True)
    pieces = conv_call(
        dims,
        jnp.transpose(input_triple_streams, (1, 0, 2)),
        former_piece_sizes,
        short_causal_filters,
        pole_coefficients,
        pole_damping,
        direct_coefficient[None, :],
    )
    chosen = select_call(
        dims, seq_len, pieces, former_piece_sizes, updated_piece_sizes, remaining_indices
    )
    return project_call(spread_call(dims, chosen), projector)


def solution(mesh):
    grid = (2, 2, mesh.shape["seq"] // 4, mesh.shape["chan"] // 2, 2)
    dims = {"x": 4, "z": grid[2], "y": grid[3]}
    rows, channels = SEQ, ("y", "core")
    return jax.shard_map(
        functools.partial(shards, dims),
        mesh=Mesh(mesh.devices.reshape(grid), AXES),
        in_specs=(
            P(rows, None, channels),
            P(),
            P(),
            P(),
            P(None, None, channels),
            P(None, channels),
            P(None, channels),
            P(channels),
            P(rows, channels),
        ),
        out_specs=P(rows, channels),
        check_vma=False,
    )
```

```python
import functools

import jax
import jax.numpy as jnp
from jax import lax
from jax.experimental import pallas as pl
from jax.experimental.pallas import tpu as pltpu
from jax.sharding import Mesh
from jax.sharding import PartitionSpec as P

MESH = pl.DeviceIdType.MESH
LANES = 128
VMEM = 56 << 20
SUBS = 8
AXES = ("x_high", "x_low", "z", "y", "core")
SEQ = ("x_high", "x_low", "z")


def x_index():
    return lax.axis_index("x_high") * 2 + lax.axis_index("x_low")


def at_x(x):
    return {"x_high": x // 2, "x_low": lax.rem(x, 2)}


def shift_down(value, by):
    row = lax.broadcasted_iota(jnp.int32, value.shape, 0)
    return jnp.where(row >= by, pltpu.roll(value, by, 0), 0.0)


def tree_sum(terms):
    while len(terms) > 1:
        terms = [a + b for a, b in zip(terms[::2], terms[1::2], strict=True)]
    return terms[0]


def conv_kernel(
    x_count, z_count,
    sizes, streams_far, taps_far, residue_far, damping_far, direct_far, block,
    gathered, swapped,
    streams, taps, residue, damping, direct, padded, tail, rates_own, query, gated, mixed, partial, ends, end_in, carry_out, carry_in, hidden, halo,
    halo_send, halo_recv, end_send, end_recv, carry_send, carry_recv,
    z_send, z_recv, swap_send, swap_recv, load_sem, local_sem,
):
    modes = residue.shape[0]
    cap = streams.shape[1]
    groups = z_count
    step_rows = cap // SUBS
    seq_count = x_count * z_count
    per_owner = max(1, modes // seq_count)
    owners = modes // per_owner
    my_x, my_z = x_index(), lax.axis_index("z")
    me = my_x * z_count + my_z
    valid = sizes[me]

    loads = [
        pltpu.make_async_copy(far, near, load_sem.at[i])
        for i, (far, near) in enumerate((
            (streams_far, streams), (taps_far, taps), (residue_far, residue),
            (damping_far, damping), (direct_far, direct),
        ))
    ]
    for load in loads:
        load.start()

    def seq_device(index):
        return {**at_x(index // z_count), "z": lax.rem(index, z_count)}

    def lanes(g):
        return pl.ds(pl.multiple_of(g * LANES, LANES), LANES)

    barrier = pltpu.get_barrier_semaphore()

    @pl.loop(1, seq_count)
    def _(k):
        pl.semaphore_signal(
            barrier, inc=1, device_id=seq_device(lax.rem(me + k, seq_count)), device_id_type=MESH
        )

    for load in loads:
        load.wait()
    last = SUBS - 1 + valid
    second = jnp.maximum(last - 1, SUBS)

    @pl.loop(0, groups)
    def _(g):
        for p in range(3):
            padded[p, g, SUBS : SUBS + cap, :] = streams[p, :, lanes(g)].astype(jnp.float32)
            tail[g, p : p + 1, :] = padded[p, g, pl.ds(last, 1), :]
            tail[g, 3 + p : 4 + p, :] = padded[p, g, pl.ds(second, 1), :]
        tail[g, 6:8, :] = jnp.zeros((2, LANES), jnp.float32)

    pl.semaphore_wait(barrier, seq_count - 1)

    def halo_copy(distance):
        target = lax.rem(me + distance, seq_count)
        return pltpu.make_async_remote_copy(
            src_ref=tail, dst_ref=halo.at[distance - 1], send_sem=halo_send.at[distance - 1],
            recv_sem=halo_recv.at[distance - 1], device_id=seq_device(target), device_id_type=MESH,
        )

    swap = pltpu.make_async_remote_copy(
        src_ref=block, dst_ref=swapped, send_sem=swap_send, recv_sem=swap_recv,
        device_id={"x_low": 1 - lax.axis_index("x_low")}, device_id_type=MESH,
    )
    for distance in (1, 2):
        halo_copy(distance).start()
    swap.start()
    for distance in (1, 2):
        halo_copy(distance).wait_recv()

    row = lax.broadcasted_iota(jnp.int32, (cap, LANES), 0)
    before_size = sizes[lax.rem(me + seq_count - 1, seq_count)]

    @pl.loop(0, groups)
    def _(g):
        at = lanes(g)
        features = []
        for p in range(3):
            last_one = jnp.where(me >= 1, halo[0, g, p : p + 1, :], 0.0)
            own_second = halo[0, g, 3 + p : 4 + p, :]
            far_last = jnp.where(me >= 2, halo[1, g, p : p + 1, :], 0.0)
            last_two = jnp.where(me >= 1, jnp.where(before_size >= 2, own_second, far_last), 0.0)
            padded[p, g, 6:7, :] = last_two
            padded[p, g, 7:8, :] = last_one
            features.append(
                taps[p, 0:1, at] * padded[p, g, 8 : 8 + cap, :]
                + taps[p, 1:2, at] * padded[p, g, 7 : 7 + cap, :]
                + taps[p, 2:3, at] * padded[p, g, 6 : 6 + cap, :]
            )
        query[g] = features[0].astype(jnp.bfloat16).astype(jnp.float32)
        product = (features[1] * features[2]).astype(jnp.bfloat16).astype(jnp.float32)
        gated[g] = jnp.where(row < valid, product, 0.0)

    def mode_rows(ref, at):
        return [jnp.broadcast_to(ref[m : m + 1, at], (SUBS, LANES)) for m in range(modes)]

    @pl.loop(0, groups)
    def _(g):
        at = lanes(g)
        decay = [jnp.exp(-d) for d in mode_rows(damping, at)]
        weight = mode_rows(residue, at)

        def step(i, states):
            u = gated[g, pl.ds(i, SUBS, stride=step_rows), :]
            return tuple(a * h + r * u for a, h, r in zip(decay, states, weight, strict=True))

        zero = jnp.zeros((SUBS, LANES), jnp.float32)
        states = lax.fori_loop(0, step_rows, step, (zero,) * modes, unroll=4)
        left_over = (cap - valid).astype(jnp.float32)
        for m in range(modes):
            rate = damping[m : m + 1, at]
            total = states[m]
            for by in (1, 2, 4):
                total = total + jnp.exp(-rate * (step_rows * by)) * shift_down(total, by)
            partial[g, m] = shift_down(total, 1)
            ends[m, pl.ds(g, 1), :] = total[SUBS - 1 : SUBS, :] * jnp.exp(rate * left_over)

    def end_copy(owner):
        return pltpu.make_async_remote_copy(
            src_ref=ends.at[pl.ds(owner * per_owner, per_owner)], dst_ref=end_in.at[me],
            send_sem=end_send.at[owner], recv_sem=end_recv.at[me],
            device_id=seq_device(owner), device_id_type=MESH,
        )

    def end_arrival(source):
        return pltpu.make_async_remote_copy(
            src_ref=ends.at[pl.ds(0, per_owner)], dst_ref=end_in.at[source],
            send_sem=end_send.at[0], recv_sem=end_recv.at[source],
            device_id=seq_device(source), device_id_type=MESH,
        )

    def carry_copy(target):
        return pltpu.make_async_remote_copy(
            src_ref=carry_out.at[target], dst_ref=carry_in.at[me],
            send_sem=carry_send.at[target], recv_sem=carry_recv.at[me],
            device_id=seq_device(target), device_id_type=MESH,
        )

    def carry_arrival(owner):
        return pltpu.make_async_remote_copy(
            src_ref=carry_out.at[0], dst_ref=carry_in.at[owner],
            send_sem=carry_send.at[0], recv_sem=carry_recv.at[owner],
            device_id=seq_device(owner), device_id_type=MESH,
        )

    @pl.loop(0, owners)
    def _(k):
        owner = lax.rem(me + k, owners)

        @pl.when(owner != me)
        def _():
            end_copy(owner).start()

    @pl.when(me < owners)
    def _():
        end_in[me] = ends[pl.ds(me * per_owner, per_owner)]
        mode = lax.broadcasted_iota(jnp.int32, (modes, LANES), 0)
        for j in range(per_owner):
            for g in range(groups):
                block = damping[:, g * LANES : (g + 1) * LANES]
                rates_own[j, g : g + 1, :] = jnp.sum(
                    jnp.where(mode == me * per_owner + j, block, 0.0), axis=0, keepdims=True
                )

        @pl.loop(0, seq_count)
        def _(source):
            @pl.when(source != me)
            def _():
                end_arrival(source).wait_recv()

        rate = rates_own[...]

        def advance(source, carry):
            carry_out[source] = carry
            return jnp.exp(-rate * sizes[source].astype(jnp.float32)) * carry + end_in[source]

        lax.fori_loop(0, seq_count, advance, jnp.zeros_like(rate), unroll=8)
        carry_in[me] = carry_out[me]

        @pl.loop(0, seq_count)
        def _(target):
            @pl.when(target != me)
            def _():
                carry_copy(target).start()

    @pl.loop(0, owners)
    def _(owner):
        @pl.when(owner != me)
        def _():
            carry_arrival(owner).wait_recv()

    def z_copy(g):
        return pltpu.make_async_remote_copy(
            src_ref=hidden.at[g], dst_ref=gathered.at[my_z], send_sem=z_send.at[g],
            recv_sem=z_recv.at[my_z], device_id={"z": g}, device_id_type=MESH,
        )

    def z_arrival(z):
        return pltpu.make_async_remote_copy(
            src_ref=hidden.at[0], dst_ref=gathered.at[z], send_sem=z_send.at[0],
            recv_sem=z_recv.at[z], device_id={"z": z}, device_id_type=MESH,
        )

    own_copy = pltpu.make_async_copy(hidden.at[my_z], gathered.at[my_z], local_sem)

    @pl.loop(0, groups)
    def _(k):
        g = lax.rem(my_z + 1 + k, groups)
        at = lanes(g)
        rates = mode_rows(damping, at)
        decay = [jnp.exp(-d) for d in rates]
        weight = mode_rows(residue, at)
        sub = lax.broadcasted_iota(jnp.int32, (SUBS, LANES), 0).astype(jnp.float32) * step_rows
        start = tuple(
            partial[g, m]
            + jnp.exp(-rates[m] * sub)
            * carry_in[m // per_owner, m % per_owner, pl.ds(g, 1), :]
            for m in range(modes)
        )

        def step(i, states):
            rows = pl.ds(i, SUBS, stride=step_rows)
            u = gated[g, rows, :]
            states = tuple(a * h + r * u for a, h, r in zip(decay, states, weight, strict=True))
            mixed[rows, :] = tree_sum(list(states))
            return states

        lax.fori_loop(0, step_rows, step, start, unroll=4)
        conv = mixed[...] + direct[0:1, at] * gated[g]
        hidden[g] = (query[g] * conv).astype(jnp.bfloat16)

        @pl.when(g != my_z)
        def _():
            z_copy(g).start()

        @pl.when(g == my_z)
        def _():
            own_copy.start()

    own_copy.wait()

    @pl.loop(0, z_count)
    def _(z):
        @pl.when(z != my_z)
        def _():
            z_arrival(z).wait_recv()
            z_copy(z).wait_send()

    swap.wait()
    for distance in (1, 2):
        halo_copy(distance).wait_send()

    @pl.loop(0, owners)
    def _(owner):
        @pl.when(owner != me)
        def _():
            end_copy(owner).wait_send()

    @pl.when(me < owners)
    def _():
        @pl.loop(0, seq_count)
        def _(target):
            @pl.when(target != me)
            def _():
                carry_copy(target).wait_send()


def conv_call(dims, streams, sizes, taps, residue, damping, direct, block):
    x_count, z_count = dims["x"], dims["z"]
    cap, width = streams.shape[1:]
    modes = residue.shape[0]
    seq_count = x_count * z_count
    per_owner = max(1, modes // seq_count)
    owners = modes // per_owner
    f32, bf16 = jnp.float32, jnp.bfloat16
    dma = pltpu.SemaphoreType.DMA
    vmem = pl.BlockSpec(memory_space=pltpu.VMEM)
    far = pl.BlockSpec(memory_space=pl.ANY)
    return pl.pallas_call(
        functools.partial(conv_kernel, x_count, z_count),
        out_shape=[
            jax.ShapeDtypeStruct((z_count, cap, LANES), bf16),
            jax.ShapeDtypeStruct(block.shape, bf16),
        ],
        in_specs=[pl.BlockSpec(memory_space=pltpu.SMEM)] + [far] * 6,
        out_specs=[far, far],
        scratch_shapes=[
            pltpu.VMEM(streams.shape, bf16),
            pltpu.VMEM(taps.shape, f32),
            pltpu.VMEM(residue.shape, f32),
            pltpu.VMEM(damping.shape, f32),
            pltpu.VMEM(direct.shape, f32),
            pltpu.VMEM((3, z_count, cap + SUBS, LANES), f32),
            pltpu.VMEM((z_count, SUBS, LANES), f32),
            pltpu.VMEM((per_owner, z_count, LANES), f32),
            pltpu.VMEM((z_count, cap, LANES), f32),
            pltpu.VMEM((z_count, cap, LANES), f32),
            pltpu.VMEM((cap, LANES), f32),
            pltpu.VMEM((z_count, modes, SUBS, LANES), f32),
            pltpu.VMEM((modes, z_count, LANES), f32),
            pltpu.VMEM((seq_count, per_owner, z_count, LANES), f32),
            pltpu.VMEM((seq_count, per_owner, z_count, LANES), f32),
            pltpu.VMEM((owners, per_owner, z_count, LANES), f32),
            pltpu.VMEM((z_count, cap, LANES), bf16),
            pltpu.VMEM((2, z_count, SUBS, LANES), f32),
            dma((2,)), dma((2,)),
            dma((owners,)), dma((seq_count,)), dma((seq_count,)), dma((owners,)),
        ]
        + [dma((z_count,))] * 2
        + [dma, dma, dma((5,)), dma],
        compiler_params=pltpu.CompilerParams(
            collective_id=0, has_side_effects=True, vmem_limit_bytes=VMEM
        ),
        name="convolve",
    )(sizes, streams, taps, residue, damping, direct, block)


def ring_kernel(
    x_count, z_count,
    own, gathered,
    right_send, right_recv, left_send, left_recv,
    far_a_send, far_a_recv, far_b_send, far_b_recv, local_sem,
):
    my_x = x_index()
    cap = own.shape[1]
    half = cap // 2
    right, left = lax.rem(my_x + 1, x_count), lax.rem(my_x + x_count - 1, x_count)
    opposite = lax.rem(my_x + 2, x_count)
    local = pltpu.make_async_copy(
        own, gathered.at[pl.ds(my_x * z_count, z_count)], local_sem
    )
    local.start()
    barrier = pltpu.get_barrier_semaphore()
    for to in (right, left):
        pl.semaphore_signal(barrier, inc=1, device_id=at_x(to), device_id_type=MESH)
    pl.semaphore_wait(barrier, 2)

    def x_copy(source, source_x, z, to, send, recv, first, rows):
        at = pl.ds(first, rows)
        return pltpu.make_async_remote_copy(
            src_ref=source.at[at], dst_ref=gathered.at[source_x * z_count + z, at],
            send_sem=send.at[z], recv_sem=recv.at[z], device_id=at_x(to), device_id_type=MESH,
        )

    def to_right(source_x, z):
        return x_copy(own.at[z], source_x, z, right, right_send, right_recv, 0, cap)

    def to_left(source_x, z):
        return x_copy(own.at[z], source_x, z, left, left_send, left_recv, 0, cap)

    def onward(source_x, z):
        return gathered.at[source_x * z_count + z]

    def far_right(source_x, z):
        return x_copy(
            onward(source_x, z), source_x, z, right, far_a_send, far_a_recv, 0, half
        )

    def far_left(source_x, z):
        return x_copy(
            onward(source_x, z), source_x, z, left, far_b_send, far_b_recv, half, half
        )

    @pl.loop(0, z_count)
    def _(z):
        to_right(my_x, z).start()
        to_left(my_x, z).start()

    @pl.loop(0, z_count)
    def _(z):
        to_right(left, z).wait_recv()
        far_right(left, z).start()
        to_left(right, z).wait_recv()
        far_left(right, z).start()

    local.wait()

    @pl.loop(0, z_count)
    def _(z):
        far_right(opposite, z).wait_recv()
        far_left(opposite, z).wait_recv()
        far_right(left, z).wait_send()
        far_left(right, z).wait_send()
        to_right(my_x, z).wait_send()
        to_left(my_x, z).wait_send()


def ring_call(dims, own):
    x_count, z_count = dims["x"], dims["z"]
    dma = pltpu.SemaphoreType.DMA
    far = pl.BlockSpec(memory_space=pl.ANY)
    return pl.pallas_call(
        functools.partial(ring_kernel, x_count, z_count),
        out_shape=jax.ShapeDtypeStruct((x_count * z_count,) + own.shape[1:], own.dtype),
        in_specs=[far],
        out_specs=far,
        scratch_shapes=[dma((z_count,))] * 8 + [dma],
        compiler_params=pltpu.CompilerParams(collective_id=3, has_side_effects=True),
        name="ring_rows",
    )(own)


def select_kernel(z_count, former, updated, remaining, pieces, chosen, sequence):
    seq_count, cap, _ = pieces.shape

    def place(s, start):
        sequence[pl.ds(start, cap), :] = pieces[s].astype(jnp.float32)
        return start + former[s]

    lax.fori_loop(0, seq_count, place, 0)
    row = lax.broadcasted_iota(jnp.int32, (cap, LANES), 0)
    first = x_index() * z_count
    chosen[...] = jnp.zeros_like(chosen)

    def pick(k, start):
        own = remaining[k] - first

        @pl.when(jnp.logical_and(own >= 0, own < z_count))
        def _():
            rows = sequence[pl.ds(start, cap), :]
            chosen[own] = jnp.where(row < updated[k], rows, 0.0).astype(jnp.bfloat16)

        return start + updated[k]

    lax.fori_loop(0, updated.shape[0], pick, 0)


def select_call(dims, seq_len, pieces, former, updated, remaining):
    cap = pieces.shape[1]
    smem = pl.BlockSpec(memory_space=pltpu.SMEM)
    vmem = pl.BlockSpec(memory_space=pltpu.VMEM)
    return pl.pallas_call(
        functools.partial(select_kernel, dims["z"]),
        out_shape=jax.ShapeDtypeStruct((dims["z"], cap, LANES), jnp.bfloat16),
        in_specs=[smem] * 3 + [vmem],
        out_specs=vmem,
        scratch_shapes=[pltpu.VMEM((seq_len + cap, LANES), jnp.float32)],
        compiler_params=pltpu.CompilerParams(vmem_limit_bytes=24 << 20),
        name="reorder_rows",
    )(former, updated, remaining, pieces)


def spread_kernel(
    z_count, y_count,
    chosen, rows_in,
    z_send, z_recv, right_send, right_recv, left_send, left_recv,
    far_a_send, far_a_recv, far_b_send, far_b_recv, core_send, core_recv,
    local_sem,
):
    cap = rows_in.shape[1]
    my_x, my_z = x_index(), lax.axis_index("z")
    my_y, my_core = lax.axis_index("y"), lax.axis_index("core")
    right, left = lax.rem(my_y + 1, y_count), lax.rem(my_y + y_count - 1, y_count)
    opposite = lax.rem(my_y + 2, y_count)
    other = 1 - my_core
    half = cap // 2
    stays = my_x // 2 == my_y // 2
    target_x = jnp.where(stays, my_x, 3 - my_x)
    target_y = jnp.where(stays, my_y, 3 - my_y)

    def crossed(z):
        return {**at_x(target_x), "y": target_y, "z": z}

    def is_me(z):
        return jnp.logical_and(stays, z == my_z)

    barrier = pltpu.get_barrier_semaphore()

    @pl.loop(0, z_count)
    def _(k):
        z = lax.rem(my_z + k, z_count)

        @pl.when(jnp.logical_not(is_me(z)))
        def _():
            pl.semaphore_signal(barrier, inc=1, device_id=crossed(z), device_id_type=MESH)

    for to in ({"y": right}, {"y": left}, {"core": other}):
        pl.semaphore_signal(barrier, inc=1, device_id=to, device_id_type=MESH)
    @pl.when(stays)
    def _():
        pl.semaphore_wait(barrier, z_count - 1 + 3)

    @pl.when(jnp.logical_not(stays))
    def _():
        pl.semaphore_wait(barrier, z_count + 3)

    def columns(source_y, core, z):
        block = (lax.rem(source_y, 2) * 2 + core) * z_count + z
        return pl.ds(pl.multiple_of(block * LANES, LANES), LANES)

    def place(y, core, z, first, rows):
        native = y // 2 == my_x // 2
        source_y = jnp.where(native, y, 3 - y)
        return rows_in.at[
            jnp.where(native, 0, 1), pl.ds(first, rows), columns(source_y, core, z)
        ]

    def z_copy(z):
        return pltpu.make_async_remote_copy(
            src_ref=chosen.at[z], dst_ref=rows_in.at[jnp.where(stays, 0, 1), :, columns(my_y, my_core, my_z)],
            send_sem=z_send.at[z], recv_sem=z_recv.at[my_z],
            device_id=crossed(z), device_id_type=MESH,
        )

    def z_arrival(z):
        return pltpu.make_async_remote_copy(
            src_ref=chosen.at[0], dst_ref=place(my_y, my_core, z, 0, cap),
            send_sem=z_send.at[0], recv_sem=z_recv.at[z],
            device_id=crossed(z), device_id_type=MESH,
        )

    own_copy = pltpu.make_async_copy(
        chosen.at[my_z], rows_in.at[0, :, columns(my_y, my_core, my_z)], local_sem
    )

    @pl.when(stays)
    def _():
        own_copy.start()

    @pl.loop(0, z_count)
    def _(k):
        z = lax.rem(my_z + k, z_count)

        @pl.when(jnp.logical_not(is_me(z)))
        def _():
            z_copy(z).start()

    def onward(y, core, z, to, send, recv, first, rows):
        view = place(y, core, z, first, rows)
        return pltpu.make_async_remote_copy(
            src_ref=view, dst_ref=view, send_sem=send, recv_sem=recv,
            device_id=to, device_id_type=MESH,
        )

    def to_right(y, z):
        return onward(y, my_core, z, {"y": right}, right_send.at[z], right_recv.at[z], 0, cap)

    def to_left(y, z):
        return onward(y, my_core, z, {"y": left}, left_send.at[z], left_recv.at[z], 0, cap)

    def far_right(y, z):
        return onward(y, my_core, z, {"y": right}, far_a_send.at[z], far_a_recv.at[z], 0, half)

    def far_left(y, z):
        return onward(y, my_core, z, {"y": left}, far_b_send.at[z], far_b_recv.at[z], half, half)

    def to_core(y, core, z):
        return onward(y, core, z, {"core": other}, core_send.at[y, z], core_recv.at[y, z], 0, cap)

    def arrival_order(k):
        return lax.rem(my_z + z_count - k, z_count)

    lag = min(2, z_count)

    @pl.loop(0, z_count + lag)
    def _(k):
        @pl.when(k < z_count)
        def _():
            z = arrival_order(k)

            @pl.when(jnp.logical_not(is_me(z)))
            def _():
                z_arrival(z).wait_recv()

            @pl.when(is_me(z))
            def _():
                own_copy.wait()

            to_right(my_y, z).start()
            to_left(my_y, z).start()
            to_core(my_y, my_core, z).start()

        @pl.when(k >= lag)
        def _():
            z = arrival_order(k - lag)
            to_right(left, z).wait_recv()
            far_right(left, z).start()
            to_core(left, my_core, z).start()
            to_left(right, z).wait_recv()
            far_left(right, z).start()
            to_core(right, my_core, z).start()

    @pl.loop(0, z_count)
    def _(k):
        z = arrival_order(k)
        far_right(opposite, z).wait_recv()
        far_left(opposite, z).wait_recv()
        to_core(opposite, my_core, z).start()

    @pl.loop(0, z_count)
    def _(z):
        for y in range(y_count):
            to_core(y, other, z).wait_recv()
            to_core(y, my_core, z).wait_send()
        to_right(my_y, z).wait_send()
        to_left(my_y, z).wait_send()
        far_right(left, z).wait_send()
        far_left(right, z).wait_send()

        @pl.when(jnp.logical_not(is_me(z)))
        def _():
            z_copy(z).wait_send()


def spread_call(dims, chosen):
    z_count, cap, _ = chosen.shape
    y_count = dims["y"]
    dma = pltpu.SemaphoreType.DMA
    return pl.pallas_call(
        functools.partial(spread_kernel, z_count, y_count),
        out_shape=jax.ShapeDtypeStruct((2, cap, y_count * z_count * LANES), jnp.bfloat16),
        in_specs=[pl.BlockSpec(memory_space=pltpu.VMEM)],
        out_specs=pl.BlockSpec(memory_space=pl.ANY),
        scratch_shapes=[dma((z_count,))] * 10 + [dma((y_count, z_count))] * 2 + [dma],
        compiler_params=pltpu.CompilerParams(
            collective_id=1, has_side_effects=True, vmem_limit_bytes=VMEM
        ),
        name="spread_rows",
    )(chosen)


def project_kernel(
    rows_far, near_block, far_block, out,
    rows, weights, own_sum, partial_out, partial_in,
    rows_sem, load_sem, sum_send, sum_recv,
):
    parts, depth, tile = weights.shape
    half = depth // 2
    my_low = lax.axis_index("x_low")
    partner = at_x(3 - x_index())

    barrier = pltpu.get_barrier_semaphore()
    pl.semaphore_signal(barrier, inc=1, device_id=partner, device_id_type=MESH)

    def span(part):
        return pl.ds(pl.multiple_of(part * tile, tile), tile)

    def load(block, low, part, sem):
        first = pl.multiple_of(low * half, half)
        return pltpu.make_async_copy(
            block.at[:, span(part)], weights.at[part, pl.ds(first, half)], sem.at[part]
        )

    def near(part):
        return load(near_block, my_low, part, load_sem.at[0])

    def far(part):
        return load(far_block, 1 - my_low, part, load_sem.at[1])

    def row_load(k):
        return pltpu.make_async_copy(rows_far.at[k], rows.at[k], rows_sem.at[k])

    row_load(1).start()

    def exchange(part):
        return pltpu.make_async_remote_copy(
            src_ref=partial_out.at[part], dst_ref=partial_in.at[part],
            send_sem=sum_send.at[part], recv_sem=sum_recv.at[part],
            device_id=partner, device_id_type=MESH,
        )

    @pl.loop(0, parts)
    def _(part):
        near(part).start()
        far(part).start()

    row_load(0).start()
    row_load(1).wait()
    pl.semaphore_wait(barrier, 1)

    @pl.loop(0, parts)
    def _(part):
        near(part).wait()
        far(part).wait()
        partial_out[part] = jnp.dot(
            rows[1], weights[part], preferred_element_type=jnp.float32
        ).astype(jnp.bfloat16)
        exchange(part).start()

    row_load(0).wait()

    @pl.loop(0, parts)
    def _(part):
        own_sum[part] = jnp.dot(rows[0], weights[part], preferred_element_type=jnp.float32)

    @pl.loop(0, parts)
    def _(part):
        exchange(part).wait_recv()
        total = own_sum[part] + partial_in[part].astype(jnp.float32)
        out[:, span(part)] = total.astype(jnp.bfloat16)

    @pl.loop(0, parts)
    def _(part):
        exchange(part).wait_send()


def project_call(rows, near_block, far_block):
    _, cap, depth = rows.shape
    width = near_block.shape[1]
    tile = min(256, width)
    parts = width // tile
    f32, bf16 = jnp.float32, jnp.bfloat16
    dma = pltpu.SemaphoreType.DMA
    vmem = pl.BlockSpec(memory_space=pltpu.VMEM)
    return pl.pallas_call(
        project_kernel,
        out_shape=jax.ShapeDtypeStruct((cap, width), bf16),
        in_specs=[pl.BlockSpec(memory_space=pl.ANY)] * 3,
        out_specs=vmem,
        scratch_shapes=[
            pltpu.VMEM(rows.shape, bf16),
            pltpu.VMEM((parts, depth, tile), bf16),
            pltpu.VMEM((parts, cap, tile), f32),
            pltpu.VMEM((parts, cap, tile), bf16),
            pltpu.VMEM((parts, cap, tile), bf16),
            dma((2,)), dma((2, parts)), dma((parts,)), dma((parts,)),
        ],
        compiler_params=pltpu.CompilerParams(
            collective_id=2, has_side_effects=True, vmem_limit_bytes=VMEM
        ),
        name="project_rows",
    )(rows, near_block, far_block)


def shards(
    dims,
    input_triple_streams,
    former_piece_sizes,
    updated_piece_sizes,
    remaining_indices,
    short_causal_filters,
    pole_coefficients,
    pole_damping,
    direct_coefficient,
    final_projector,
):
    cap = input_triple_streams.shape[0]
    seq_len = cap * 4 // 5 * dims["x"] * dims["z"]

    near_block = lax.all_gather(final_projector, "z", axis=0, tiled=True)
    own, swapped = conv_call(
        dims,
        jnp.transpose(input_triple_streams, (1, 0, 2)),
        former_piece_sizes,
        short_causal_filters,
        pole_coefficients,
        pole_damping,
        direct_coefficient[None, :],
        final_projector,
    )
    far_block = lax.all_gather(swapped, "z", axis=0, tiled=True)
    pieces = ring_call(dims, own)
    chosen = select_call(
        dims, seq_len, pieces, former_piece_sizes, updated_piece_sizes, remaining_indices
    )
    return project_call(spread_call(dims, chosen), near_block, far_block)


def solution(mesh):
    grid = (2, 2, mesh.shape["seq"] // 4, mesh.shape["chan"] // 2, 2)
    dims = {"x": 4, "z": grid[2], "y": grid[3]}
    rows, channels = SEQ, ("y", "core")
    return jax.shard_map(
        functools.partial(shards, dims),
        mesh=Mesh(mesh.devices.reshape(grid), AXES),
        in_specs=(
            P(rows, None, channels),
            P(),
            P(),
            P(),
            P(None, None, channels),
            P(None, channels),
            P(None, channels),
            P(channels),
            P(rows, channels),
        ),
        out_specs=P(rows, channels),
        check_vma=False,
    )
```

```python
import functools

import jax
import jax.numpy as jnp
from jax import lax
from jax.experimental import pallas as pl
from jax.experimental.pallas import tpu as pltpu
from jax.sharding import Mesh
from jax.sharding import PartitionSpec as P

MESH = pl.DeviceIdType.MESH
LANES = 128
VMEM = 56 << 20
SUBS = 8
AXES = ("x_high", "x_low", "z", "y", "core")
SEQ = ("x_high", "x_low", "z")


def x_index():
    return lax.axis_index("x_high") * 2 + lax.axis_index("x_low")


def at_x(x):
    return {"x_high": x // 2, "x_low": lax.rem(x, 2)}


def repack(quarters, k):
    group = lax.broadcasted_iota(jnp.int32, quarters[0].shape, 1) // (LANES // 4)
    result = jnp.zeros_like(quarters[0])
    for q in range(4):
        turned = pltpu.roll(quarters[q], ((q - k) % 4) * (LANES // 4), 1)
        result = jnp.where(group == q, turned, result)
    return result


def block_step(step, z_count, my_z, held, passed, sems):
    up_send, up_recv, down_send, down_recv = sems
    rows = held.shape[1]
    last = step == z_count // 2
    half = rows // 2
    copies = []
    for source, to, first, send, recv in (
        (my_z + 1 - step, my_z + 1, 0, up_send, up_recv),
        (my_z - 1 + step, my_z - 1, half, down_send, down_recv),
    ):
        source = lax.rem(source + z_count, z_count)
        at = pl.ds(first, half) if last else pl.ds(0, rows)
        copies.append(
            pltpu.make_async_remote_copy(
                src_ref=held.at[source, at], dst_ref=passed.at[source, at],
                send_sem=send.at[step - 1], recv_sem=recv.at[step - 1],
                device_id={"z": lax.rem(to + z_count, z_count)}, device_id_type=MESH,
            )
        )
    return copies


def shift_down(value, by):
    row = lax.broadcasted_iota(jnp.int32, value.shape, 0)
    return jnp.where(row >= by, pltpu.roll(value, by, 0), 0.0)


def tree_sum(terms):
    while len(terms) > 1:
        terms = [a + b for a, b in zip(terms[::2], terms[1::2], strict=True)]
    return terms[0]


def conv_kernel(
    x_count, z_count,
    sizes, streams_far, taps_far, residue_far, damping_far, direct_far, block,
    gathered, blocks,
    streams, taps, residue, damping, direct, padded, tail, rates_own, query, gated, mixed, partial, ends, end_in, carry_out, carry_in, hidden, halo,
    halo_send, halo_recv, end_send, end_recv, carry_send, carry_recv,
    piece_send, piece_recv, swap_send, swap_recv, up_send, up_recv, down_send, down_recv,
    load_sem, local_sem,
):
    modes = residue.shape[0]
    cap = streams.shape[1]
    groups = z_count
    step_rows = cap // SUBS
    seq_count = x_count * z_count
    per_owner = max(1, modes // seq_count)
    owners = modes // per_owner
    my_x, my_z = x_index(), lax.axis_index("z")
    me = my_x * z_count + my_z
    valid = sizes[me]

    loads = [
        pltpu.make_async_copy(far, near, load_sem.at[i])
        for i, (far, near) in enumerate((
            (streams_far, streams), (taps_far, taps), (residue_far, residue),
            (damping_far, damping), (direct_far, direct),
        ))
    ]
    for load in loads:
        load.start()

    def seq_device(index):
        return {**at_x(index // z_count), "z": lax.rem(index, z_count)}

    def lanes(g):
        return pl.ds(pl.multiple_of(g * LANES, LANES), LANES)

    barrier = pltpu.get_barrier_semaphore()

    @pl.loop(1, seq_count)
    def _(k):
        pl.semaphore_signal(
            barrier, inc=1, device_id=seq_device(lax.rem(me + k, seq_count)), device_id_type=MESH
        )

    for load in loads:
        load.wait()
    last = SUBS - 1 + valid
    second = jnp.maximum(last - 1, SUBS)

    @pl.loop(0, groups)
    def _(g):
        for p in range(3):
            padded[p, g, SUBS : SUBS + cap, :] = streams[p, :, lanes(g)].astype(jnp.float32)
            tail[g, p : p + 1, :] = padded[p, g, pl.ds(last, 1), :]
            tail[g, 3 + p : 4 + p, :] = padded[p, g, pl.ds(second, 1), :]
        tail[g, 6:8, :] = jnp.zeros((2, LANES), jnp.float32)

    pl.semaphore_wait(barrier, seq_count - 1)

    def halo_copy(distance):
        target = lax.rem(me + distance, seq_count)
        return pltpu.make_async_remote_copy(
            src_ref=tail, dst_ref=halo.at[distance - 1], send_sem=halo_send.at[distance - 1],
            recv_sem=halo_recv.at[distance - 1], device_id=seq_device(target), device_id_type=MESH,
        )

    swap = pltpu.make_async_remote_copy(
        src_ref=block, dst_ref=blocks.at[my_z], send_sem=swap_send, recv_sem=swap_recv,
        device_id={"x_low": 1 - lax.axis_index("x_low")}, device_id_type=MESH,
    )
    for distance in (1, 2):
        halo_copy(distance).start()
    swap.start()
    for distance in (1, 2):
        halo_copy(distance).wait_recv()

    row = lax.broadcasted_iota(jnp.int32, (cap, LANES), 0)
    before_size = sizes[lax.rem(me + seq_count - 1, seq_count)]

    @pl.loop(0, groups)
    def _(g):
        at = lanes(g)
        features = []
        for p in range(3):
            last_one = jnp.where(me >= 1, halo[0, g, p : p + 1, :], 0.0)
            own_second = halo[0, g, 3 + p : 4 + p, :]
            far_last = jnp.where(me >= 2, halo[1, g, p : p + 1, :], 0.0)
            last_two = jnp.where(me >= 1, jnp.where(before_size >= 2, own_second, far_last), 0.0)
            padded[p, g, 6:7, :] = last_two
            padded[p, g, 7:8, :] = last_one
            features.append(
                taps[p, 0:1, at] * padded[p, g, 8 : 8 + cap, :]
                + taps[p, 1:2, at] * padded[p, g, 7 : 7 + cap, :]
                + taps[p, 2:3, at] * padded[p, g, 6 : 6 + cap, :]
            )
        query[g] = features[0].astype(jnp.bfloat16).astype(jnp.float32)
        product = (features[1] * features[2]).astype(jnp.bfloat16).astype(jnp.float32)
        gated[g] = jnp.where(row < valid, product, 0.0)

    def mode_rows(ref, at):
        return [jnp.broadcast_to(ref[m : m + 1, at], (SUBS, LANES)) for m in range(modes)]

    @pl.loop(0, groups)
    def _(g):
        at = lanes(g)
        decay = [jnp.exp(-d) for d in mode_rows(damping, at)]
        weight = mode_rows(residue, at)

        def step(i, states):
            u = gated[g, pl.ds(i, SUBS, stride=step_rows), :]
            return tuple(a * h + r * u for a, h, r in zip(decay, states, weight, strict=True))

        zero = jnp.zeros((SUBS, LANES), jnp.float32)
        states = lax.fori_loop(0, step_rows, step, (zero,) * modes, unroll=4)
        left_over = (cap - valid).astype(jnp.float32)
        for m in range(modes):
            rate = damping[m : m + 1, at]
            total = states[m]
            for by in (1, 2, 4):
                total = total + jnp.exp(-rate * (step_rows * by)) * shift_down(total, by)
            partial[g, m] = shift_down(total, 1)
            ends[m, pl.ds(g, 1), :] = total[SUBS - 1 : SUBS, :] * jnp.exp(rate * left_over)

    swap.wait_recv()
    block_sems = (up_send, up_recv, down_send, down_recv)
    for copy in block_step(1, z_count, my_z, blocks, blocks, block_sems):
        copy.start()

    def end_copy(owner):
        return pltpu.make_async_remote_copy(
            src_ref=ends.at[pl.ds(owner * per_owner, per_owner)], dst_ref=end_in.at[me],
            send_sem=end_send.at[owner], recv_sem=end_recv.at[me],
            device_id=seq_device(owner), device_id_type=MESH,
        )

    def end_arrival(source):
        return pltpu.make_async_remote_copy(
            src_ref=ends.at[pl.ds(0, per_owner)], dst_ref=end_in.at[source],
            send_sem=end_send.at[0], recv_sem=end_recv.at[source],
            device_id=seq_device(source), device_id_type=MESH,
        )

    def carry_copy(target):
        return pltpu.make_async_remote_copy(
            src_ref=carry_out.at[target], dst_ref=carry_in.at[me],
            send_sem=carry_send.at[target], recv_sem=carry_recv.at[me],
            device_id=seq_device(target), device_id_type=MESH,
        )

    def carry_arrival(owner):
        return pltpu.make_async_remote_copy(
            src_ref=carry_out.at[0], dst_ref=carry_in.at[owner],
            send_sem=carry_send.at[0], recv_sem=carry_recv.at[owner],
            device_id=seq_device(owner), device_id_type=MESH,
        )

    @pl.loop(0, owners)
    def _(k):
        owner = lax.rem(me + k, owners)

        @pl.when(owner != me)
        def _():
            end_copy(owner).start()

    @pl.when(me < owners)
    def _():
        end_in[me] = ends[pl.ds(me * per_owner, per_owner)]
        mode = lax.broadcasted_iota(jnp.int32, (modes, LANES), 0)
        for j in range(per_owner):
            for g in range(groups):
                block = damping[:, g * LANES : (g + 1) * LANES]
                rates_own[j, g : g + 1, :] = jnp.sum(
                    jnp.where(mode == me * per_owner + j, block, 0.0), axis=0, keepdims=True
                )

        @pl.loop(0, seq_count)
        def _(source):
            @pl.when(source != me)
            def _():
                end_arrival(source).wait_recv()

        rate = rates_own[...]

        def advance(source, carry):
            carry_out[source] = carry
            return jnp.exp(-rate * sizes[source].astype(jnp.float32)) * carry + end_in[source]

        lax.fori_loop(0, seq_count, advance, jnp.zeros_like(rate), unroll=8)
        carry_in[me] = carry_out[me]

        @pl.loop(0, seq_count)
        def _(target):
            @pl.when(target != me)
            def _():
                carry_copy(target).start()

    @pl.loop(0, owners)
    def _(owner):
        @pl.when(owner != me)
        def _():
            carry_arrival(owner).wait_recv()

    def piece_copy(x, z):
        return pltpu.make_async_remote_copy(
            src_ref=hidden.at[z, x], dst_ref=gathered.at[me], send_sem=piece_send.at[x, z],
            recv_sem=piece_recv.at[me], device_id={**at_x(x), "z": z}, device_id_type=MESH,
        )

    def piece_arrival(source):
        return pltpu.make_async_remote_copy(
            src_ref=hidden.at[0, 0], dst_ref=gathered.at[source], send_sem=piece_send.at[0, 0],
            recv_sem=piece_recv.at[source], device_id=seq_device(source), device_id_type=MESH,
        )

    own_copy = pltpu.make_async_copy(hidden.at[my_z, my_x], gathered.at[me], local_sem)
    quarter = cap // 4

    @pl.loop(0, groups)
    def _(k):
        g = lax.rem(my_z + 1 + k, groups)
        at = lanes(g)
        rates = mode_rows(damping, at)
        decay = [jnp.exp(-d) for d in rates]
        weight = mode_rows(residue, at)
        sub = lax.broadcasted_iota(jnp.int32, (SUBS, LANES), 0).astype(jnp.float32) * step_rows
        start = tuple(
            partial[g, m]
            + jnp.exp(-rates[m] * sub)
            * carry_in[m // per_owner, m % per_owner, pl.ds(g, 1), :]
            for m in range(modes)
        )

        def step(i, states):
            rows = pl.ds(i, SUBS, stride=step_rows)
            u = gated[g, rows, :]
            states = tuple(a * h + r * u for a, h, r in zip(decay, states, weight, strict=True))
            mixed[rows, :] = tree_sum(list(states))
            return states

        lax.fori_loop(0, step_rows, step, start, unroll=4)
        conv = mixed[...] + direct[0:1, at] * gated[g]
        value = query[g] * conv
        quarters = [value[q * quarter : (q + 1) * quarter] for q in range(4)]
        for x in range(x_count):
            hidden[g, x] = repack(quarters, x).astype(jnp.bfloat16)

            @pl.when(jnp.logical_or(g != my_z, x != my_x))
            def _():
                piece_copy(x, g).start()

            @pl.when(jnp.logical_and(g == my_z, x == my_x))
            def _():
                own_copy.start()

    own_copy.wait()

    @pl.loop(0, seq_count)
    def _(other):
        @pl.when(other != me)
        def _():
            piece_arrival(other).wait_recv()
            piece_copy(other // z_count, lax.rem(other, z_count)).wait_send()

    for copy in block_step(1, z_count, my_z, blocks, blocks, block_sems):
        copy.wait()
    swap.wait_send()
    for distance in (1, 2):
        halo_copy(distance).wait_send()

    @pl.loop(0, owners)
    def _(owner):
        @pl.when(owner != me)
        def _():
            end_copy(owner).wait_send()

    @pl.when(me < owners)
    def _():
        @pl.loop(0, seq_count)
        def _(target):
            @pl.when(target != me)
            def _():
                carry_copy(target).wait_send()


def conv_call(dims, streams, sizes, taps, residue, damping, direct, block):
    x_count, z_count = dims["x"], dims["z"]
    cap, width = streams.shape[1:]
    modes = residue.shape[0]
    seq_count = x_count * z_count
    per_owner = max(1, modes // seq_count)
    owners = modes // per_owner
    f32, bf16 = jnp.float32, jnp.bfloat16
    dma = pltpu.SemaphoreType.DMA
    vmem = pl.BlockSpec(memory_space=pltpu.VMEM)
    far = pl.BlockSpec(memory_space=pl.ANY)
    return pl.pallas_call(
        functools.partial(conv_kernel, x_count, z_count),
        out_shape=[
            jax.ShapeDtypeStruct((seq_count, cap // 4, LANES), bf16),
            jax.ShapeDtypeStruct((z_count,) + block.shape, bf16),
        ],
        in_specs=[pl.BlockSpec(memory_space=pltpu.SMEM)] + [far] * 6,
        out_specs=[far, far],
        scratch_shapes=[
            pltpu.VMEM(streams.shape, bf16),
            pltpu.VMEM(taps.shape, f32),
            pltpu.VMEM(residue.shape, f32),
            pltpu.VMEM(damping.shape, f32),
            pltpu.VMEM(direct.shape, f32),
            pltpu.VMEM((3, z_count, cap + SUBS, LANES), f32),
            pltpu.VMEM((z_count, SUBS, LANES), f32),
            pltpu.VMEM((per_owner, z_count, LANES), f32),
            pltpu.VMEM((z_count, cap, LANES), f32),
            pltpu.VMEM((z_count, cap, LANES), f32),
            pltpu.VMEM((cap, LANES), f32),
            pltpu.VMEM((z_count, modes, SUBS, LANES), f32),
            pltpu.VMEM((modes, z_count, LANES), f32),
            pltpu.VMEM((seq_count, per_owner, z_count, LANES), f32),
            pltpu.VMEM((seq_count, per_owner, z_count, LANES), f32),
            pltpu.VMEM((owners, per_owner, z_count, LANES), f32),
            pltpu.VMEM((z_count, x_count, cap // 4, LANES), bf16),
            pltpu.VMEM((2, z_count, SUBS, LANES), f32),
            dma((2,)), dma((2,)),
            dma((owners,)), dma((seq_count,)), dma((seq_count,)), dma((owners,)),
        ]
        + [dma((x_count, z_count)), dma((seq_count,)), dma, dma]
        + [dma((1,))] * 4
        + [dma((5,)), dma],
        compiler_params=pltpu.CompilerParams(
            collective_id=0, has_side_effects=True, vmem_limit_bytes=VMEM
        ),
        name="convolve",
    )(sizes, streams, taps, residue, damping, direct, block)


def select_kernel(former, updated, remaining, pieces, chosen, sequence):
    seq_count, quarter, _ = pieces.shape
    lane_group = LANES // 4

    def place(s, start):
        piece = pieces[s].astype(jnp.float32)
        for q in range(4):
            turned = pltpu.roll(piece, (4 - q) % 4 * lane_group, 1)
            sequence[pl.ds(start + q * quarter, quarter), :] = turned
        return start + former[s]

    lax.fori_loop(0, seq_count, place, 0)
    row = lax.broadcasted_iota(jnp.int32, (quarter, LANES), 0)
    chosen[...] = jnp.zeros_like(chosen)

    def pick(k, start):
        quarters = []
        for q in range(4):
            rows = sequence[pl.ds(start + q * quarter, quarter), :]
            quarters.append(jnp.where(row + q * quarter < updated[k], rows, 0.0))
        chosen[remaining[k]] = repack(quarters, 0).astype(jnp.bfloat16)
        return start + updated[k]

    lax.fori_loop(0, updated.shape[0], pick, 0)


def select_call(seq_len, pieces, former, updated, remaining):
    smem = pl.BlockSpec(memory_space=pltpu.SMEM)
    vmem = pl.BlockSpec(memory_space=pltpu.VMEM)
    return pl.pallas_call(
        select_kernel,
        out_shape=jax.ShapeDtypeStruct(pieces.shape, jnp.bfloat16),
        in_specs=[smem] * 3 + [vmem],
        out_specs=vmem,
        scratch_shapes=[pltpu.VMEM((seq_len + 4 * pieces.shape[1], LANES), jnp.float32)],
        compiler_params=pltpu.CompilerParams(vmem_limit_bytes=24 << 20),
        name="reorder_rows",
    )(former, updated, remaining, pieces)


def spread_kernel(
    x_count, z_count, y_count,
    chosen, held, rows_in, passed,
    landing, pieces,
    piece_send, piece_recv, right_send, right_recv, left_send, left_recv,
    far_a_send, far_a_recv, far_b_send, far_b_recv, core_send, core_recv,
    up_send, up_recv, down_send, down_recv, own_sem, local_sem,
):
    cap = rows_in.shape[1]
    my_x, my_z = x_index(), lax.axis_index("z")
    my_y, my_core = lax.axis_index("y"), lax.axis_index("core")
    right, left = lax.rem(my_y + 1, y_count), lax.rem(my_y + y_count - 1, y_count)
    opposite = lax.rem(my_y + 2, y_count)
    other = 1 - my_core
    half, quarter = cap // 2, cap // 4
    stays = my_x // 2 == my_y // 2
    source_row = jnp.where(stays, my_y, 3 - my_y)

    def target(x, z):
        native = x // 2 == my_y // 2
        return {
            **at_x(jnp.where(native, x, 3 - x)),
            "y": jnp.where(native, my_y, 3 - my_y),
            "z": z,
        }

    def is_me(x, z):
        return jnp.logical_and(stays, jnp.logical_and(x == my_x, z == my_z))

    barrier = pltpu.get_barrier_semaphore()

    @pl.loop(0, z_count)
    def _(k):
        z = lax.rem(my_z + k, z_count)
        for x in range(x_count):

            @pl.when(jnp.logical_not(is_me(x, z)))
            def _():
                pl.semaphore_signal(
                    barrier, inc=1, device_id={**at_x(x), "y": source_row, "z": z},
                    device_id_type=MESH,
                )

    up, down = lax.rem(my_z + 1, z_count), lax.rem(my_z + z_count - 1, z_count)
    for to in ({"y": right}, {"y": left}, {"core": other}, {"z": up}, {"z": down}):
        pl.semaphore_signal(barrier, inc=1, device_id=to, device_id_type=MESH)

    @pl.when(stays)
    def _():
        pl.semaphore_wait(barrier, x_count * z_count - 1 + 5)

    @pl.when(jnp.logical_not(stays))
    def _():
        pl.semaphore_wait(barrier, x_count * z_count + 5)

    block_sems = (up_send, up_recv, down_send, down_recv)

    def steps(step):
        return block_step(step, z_count, my_z, held if step == 2 else passed, passed, block_sems)

    last_step = z_count // 2
    if last_step >= 2:
        for copy in steps(2):
            copy.start()

    def columns(source_y, core, z):
        block = (lax.rem(source_y, 2) * 2 + core) * z_count + z
        return pl.ds(pl.multiple_of(block * LANES, LANES), LANES)

    def place(y, core, z, first, rows):
        native = y // 2 == my_x // 2
        source_y = jnp.where(native, y, 3 - y)
        return rows_in.at[
            jnp.where(native, 0, 1), pl.ds(first, rows), columns(source_y, core, z)
        ]

    def piece_copy(x, z):
        owner = x * z_count + z
        return pltpu.make_async_remote_copy(
            src_ref=chosen.at[owner], dst_ref=landing.at[my_x, my_z],
            send_sem=piece_send.at[owner], recv_sem=piece_recv.at[my_x, my_z],
            device_id=target(x, z), device_id_type=MESH,
        )

    def piece_arrival(x, z):
        return pltpu.make_async_remote_copy(
            src_ref=chosen.at[0], dst_ref=landing.at[x, z],
            send_sem=piece_send.at[0], recv_sem=piece_recv.at[x, z],
            device_id={**at_x(x), "y": source_row, "z": z}, device_id_type=MESH,
        )

    own_copy = pltpu.make_async_copy(
        chosen.at[my_x * z_count + my_z], landing.at[my_x, my_z], own_sem
    )

    @pl.when(stays)
    def _():
        own_copy.start()

    @pl.loop(0, z_count)
    def _(k):
        z = lax.rem(my_z + k, z_count)
        for x in range(x_count):

            @pl.when(jnp.logical_not(is_me(x, z)))
            def _():
                piece_copy(x, z).start()

    def onward(y, core, z, to, send, recv, first, rows, source=None):
        view = place(y, core, z, first, rows)
        return pltpu.make_async_remote_copy(
            src_ref=view if source is None else source, dst_ref=view, send_sem=send,
            recv_sem=recv, device_id=to, device_id_type=MESH,
        )

    def to_right(y, z):
        return onward(
            y, my_core, z, {"y": right}, right_send.at[z], right_recv.at[z], 0, cap, pieces.at[z]
        )

    def to_left(y, z):
        return onward(
            y, my_core, z, {"y": left}, left_send.at[z], left_recv.at[z], 0, cap, pieces.at[z]
        )

    def far_right(y, z):
        return onward(y, my_core, z, {"y": right}, far_a_send.at[z], far_a_recv.at[z], 0, half)

    def far_left(y, z):
        return onward(y, my_core, z, {"y": left}, far_b_send.at[z], far_b_recv.at[z], half, half)

    def to_core(y, core, z, source=None):
        return onward(
            y, core, z, {"core": other}, core_send.at[y, z], core_recv.at[y, z], 0, cap, source
        )

    def keep(z):
        return pltpu.make_async_copy(
            pieces.at[z], place(my_y, my_core, z, 0, cap), local_sem.at[z]
        )

    def arrival_order(k):
        return lax.rem(my_z + z_count - k, z_count)

    lag = min(2, z_count)

    @pl.loop(0, z_count + lag)
    def _(k):
        @pl.when(k < z_count)
        def _():
            z = arrival_order(k)

            for x in range(x_count):

                @pl.when(jnp.logical_not(is_me(x, z)))
                def _():
                    piece_arrival(x, z).wait_recv()

                @pl.when(is_me(x, z))
                def _():
                    own_copy.wait()

            packed = [landing[x, z].astype(jnp.float32) for x in range(x_count)]
            for q in range(4):
                pieces[z, q * quarter : (q + 1) * quarter] = repack(packed, q).astype(jnp.bfloat16)
            to_right(my_y, z).start()
            to_left(my_y, z).start()
            to_core(my_y, my_core, z, pieces.at[z]).start()
            keep(z).start()

        @pl.when(k >= lag)
        def _():
            z = arrival_order(k - lag)
            to_right(left, z).wait_recv()
            far_right(left, z).start()
            to_core(left, my_core, z).start()
            to_left(right, z).wait_recv()
            far_left(right, z).start()
            to_core(right, my_core, z).start()

    if last_step >= 3:
        for copy in steps(2):
            copy.wait_recv()
        for copy in steps(3):
            copy.start()

    @pl.loop(0, z_count)
    def _(k):
        z = arrival_order(k)
        far_right(opposite, z).wait_recv()
        far_left(opposite, z).wait_recv()
        to_core(opposite, my_core, z).start()

    if last_step >= 4:
        for copy in steps(3):
            copy.wait_recv()
        for copy in steps(4):
            copy.start()

    @pl.loop(0, z_count)
    def _(z):
        for y in range(y_count):
            to_core(y, other, z).wait_recv()
            to_core(y, my_core, z).wait_send()
        to_right(my_y, z).wait_send()
        to_left(my_y, z).wait_send()
        far_right(left, z).wait_send()
        far_left(right, z).wait_send()

        keep(z).wait()
        for x in range(x_count):

            @pl.when(jnp.logical_not(is_me(x, z)))
            def _():
                piece_copy(x, z).wait_send()

    for step in range(2, last_step + 1):
        for copy in steps(step):
            copy.wait_send()
            if step == last_step:
                copy.wait_recv()


def spread_call(dims, chosen, held):
    x_count, y_count, z_count = dims["x"], dims["y"], dims["z"]
    cap = chosen.shape[1] * 4
    bf16 = jnp.bfloat16
    dma = pltpu.SemaphoreType.DMA
    far = pl.BlockSpec(memory_space=pl.ANY)
    return pl.pallas_call(
        functools.partial(spread_kernel, x_count, z_count, y_count),
        out_shape=[
            jax.ShapeDtypeStruct((2, cap, y_count * z_count * LANES), bf16),
            jax.ShapeDtypeStruct(held.shape, bf16),
        ],
        in_specs=[pl.BlockSpec(memory_space=pltpu.VMEM), far],
        out_specs=[far, far],
        scratch_shapes=[
            pltpu.VMEM((x_count, z_count, cap // 4, LANES), bf16),
            pltpu.VMEM((z_count, cap, LANES), bf16),
            dma((x_count * z_count,)), dma((x_count, z_count)),
        ]
        + [dma((z_count,))] * 8
        + [dma((y_count, z_count))] * 2
        + [dma((max(1, z_count // 2),))] * 4
        + [dma, dma((z_count,))],
        compiler_params=pltpu.CompilerParams(
            collective_id=1, has_side_effects=True, vmem_limit_bytes=VMEM
        ),
        name="spread_rows",
    )(chosen, held)


def project_kernel(
    rows_far, near_block, held, passed, out,
    rows, weights, own_sum, partial_out, partial_in,
    rows_sem, load_sem, sum_send, sum_recv,
):
    depth, width = weights.shape
    parts, _, tile = partial_out.shape
    half = depth // 2
    z_count, block_rows, _ = held.shape
    my_low, my_z = lax.axis_index("x_low"), lax.axis_index("z")
    partner = at_x(3 - x_index())

    barrier = pltpu.get_barrier_semaphore()
    pl.semaphore_signal(barrier, inc=1, device_id=partner, device_id_type=MESH)

    def span(part):
        return pl.ds(pl.multiple_of(part * tile, tile), tile)

    loads = [
        pltpu.make_async_copy(
            near_block, weights.at[pl.ds(pl.multiple_of(my_low * half, half), half)],
            load_sem.at[z_count],
        )
    ]
    for d in range(z_count):
        z = lax.rem(my_z + d, z_count)
        first = pl.multiple_of((1 - my_low) * half + z * block_rows, block_rows)
        loads.append(
            pltpu.make_async_copy(
                (held if min(d, z_count - d) <= 1 and 2 * d != z_count or z_count == 2 else passed).at[z],
                weights.at[pl.ds(first, block_rows)], load_sem.at[d],
            )
        )

    def row_load(k):
        return pltpu.make_async_copy(rows_far.at[k], rows.at[k], rows_sem.at[k])

    row_load(1).start()
    for load in loads:
        load.start()

    def exchange(part):
        return pltpu.make_async_remote_copy(
            src_ref=partial_out.at[part], dst_ref=partial_in.at[part],
            send_sem=sum_send.at[part], recv_sem=sum_recv.at[part],
            device_id=partner, device_id_type=MESH,
        )

    row_load(0).start()
    row_load(1).wait()
    for load in loads:
        load.wait()
    pl.semaphore_wait(barrier, 1)

    @pl.loop(0, parts)
    def _(part):
        partial_out[part] = jnp.dot(
            rows[1], weights[:, span(part)], preferred_element_type=jnp.float32
        ).astype(jnp.bfloat16)
        exchange(part).start()

    row_load(0).wait()

    @pl.loop(0, parts)
    def _(part):
        own_sum[part] = jnp.dot(
            rows[0], weights[:, span(part)], preferred_element_type=jnp.float32
        )

    @pl.loop(0, parts)
    def _(part):
        exchange(part).wait_recv()
        total = own_sum[part] + partial_in[part].astype(jnp.float32)
        out[:, span(part)] = total.astype(jnp.bfloat16)

    @pl.loop(0, parts)
    def _(part):
        exchange(part).wait_send()


def project_call(rows, near_block, held, passed):
    _, cap, depth = rows.shape
    width = near_block.shape[1]
    tile = min(256, width)
    parts = width // tile
    f32, bf16 = jnp.float32, jnp.bfloat16
    dma = pltpu.SemaphoreType.DMA
    vmem = pl.BlockSpec(memory_space=pltpu.VMEM)
    return pl.pallas_call(
        project_kernel,
        out_shape=jax.ShapeDtypeStruct((cap, width), bf16),
        in_specs=[pl.BlockSpec(memory_space=pl.ANY)] * 4,
        out_specs=vmem,
        scratch_shapes=[
            pltpu.VMEM(rows.shape, bf16),
            pltpu.VMEM((depth, width), bf16),
            pltpu.VMEM((parts, cap, tile), f32),
            pltpu.VMEM((parts, cap, tile), bf16),
            pltpu.VMEM((parts, cap, tile), bf16),
            dma((2,)), dma((held.shape[0] + 1,)), dma((parts,)), dma((parts,)),
        ],
        compiler_params=pltpu.CompilerParams(
            collective_id=2, has_side_effects=True, vmem_limit_bytes=VMEM
        ),
        name="project_rows",
    )(rows, near_block, held, passed)


def shards(
    dims,
    input_triple_streams,
    former_piece_sizes,
    updated_piece_sizes,
    remaining_indices,
    short_causal_filters,
    pole_coefficients,
    pole_damping,
    direct_coefficient,
    final_projector,
):
    cap = input_triple_streams.shape[0]
    seq_len = cap * 4 // 5 * dims["x"] * dims["z"]

    near_block = lax.all_gather(final_projector, "z", axis=0, tiled=True)
    pieces, held = conv_call(
        dims,
        jnp.transpose(input_triple_streams, (1, 0, 2)),
        former_piece_sizes,
        short_causal_filters,
        pole_coefficients,
        pole_damping,
        direct_coefficient[None, :],
        final_projector,
    )
    chosen = select_call(
        seq_len, pieces, former_piece_sizes, updated_piece_sizes, remaining_indices
    )
    rows, passed = spread_call(dims, chosen, held)
    return project_call(rows, near_block, held, passed)


def solution(mesh):
    grid = (2, 2, mesh.shape["seq"] // 4, mesh.shape["chan"] // 2, 2)
    dims = {"x": 4, "z": grid[2], "y": grid[3]}
    rows, channels = SEQ, ("y", "core")
    return jax.shard_map(
        functools.partial(shards, dims),
        mesh=Mesh(mesh.devices.reshape(grid), AXES),
        in_specs=(
            P(rows, None, channels),
            P(),
            P(),
            P(),
            P(None, None, channels),
            P(None, channels),
            P(None, channels),
            P(channels),
            P(rows, channels),
        ),
        out_specs=P(rows, channels),
        check_vma=False,
    )
```

```python
import functools

import jax
import jax.numpy as jnp
from jax import lax
from jax.experimental import pallas as pl
from jax.experimental.pallas import tpu as pltpu
from jax.sharding import Mesh
from jax.sharding import PartitionSpec as P

MESH = pl.DeviceIdType.MESH
LANES = 128
VMEM = 56 << 20
SUBS = 8
AXES = ("x_high", "x_low", "z", "y", "core")
SEQ = ("x_high", "x_low", "z")


def x_index():
    return lax.axis_index("x_high") * 2 + lax.axis_index("x_low")


def at_x(x):
    return {"x_high": x // 2, "x_low": lax.rem(x, 2)}


def repack(quarters, k):
    group = lax.broadcasted_iota(jnp.int32, quarters[0].shape, 1) // (LANES // 4)
    result = jnp.zeros_like(quarters[0])
    for q in range(4):
        turned = pltpu.roll(quarters[q], ((q - k) % 4) * (LANES // 4), 1)
        result = jnp.where(group == q, turned, result)
    return result


def shift_down(value, by):
    row = lax.broadcasted_iota(jnp.int32, value.shape, 0)
    return jnp.where(row >= by, pltpu.roll(value, by, 0), 0.0)


def tree_sum(terms):
    while len(terms) > 1:
        terms = [a + b for a, b in zip(terms[::2], terms[1::2], strict=True)]
    return terms[0]


def conv_kernel(
    x_count, z_count,
    sizes, streams_far, taps_far, residue_far, damping_far, direct_far,
    gathered,
    streams, taps, residue, damping, direct, padded, tail, rates_own, query, gated, mixed, partial, ends, end_in, carry_out, carry_in, hidden, halo,
    halo_send, halo_recv, end_send, end_recv, carry_send, carry_recv,
    piece_send, piece_recv, load_sem, local_sem,
):
    modes = residue.shape[0]
    cap = streams.shape[1]
    groups = z_count
    step_rows = cap // SUBS
    seq_count = x_count * z_count
    per_owner = max(1, modes // seq_count)
    owners = modes // per_owner
    my_x, my_z, my_core = x_index(), lax.axis_index("z"), lax.axis_index("core")
    me = my_x * z_count + my_z
    valid = sizes[me]

    def seq_device(index):
        return {**at_x(index // z_count), "z": lax.rem(index, z_count)}

    source_core = my_z // (z_count // 2)

    @pl.when(source_core != lax.axis_index("core"))
    def _():
        @pl.loop(0, seq_count)
        def _(k):
            pl.semaphore_signal(
                pltpu.get_barrier_semaphore(), inc=1,
                device_id={**seq_device(lax.rem(me + k, seq_count)), "core": source_core},
                device_id_type=MESH,
            )

    loads = [
        pltpu.make_async_copy(far, near, load_sem.at[i])
        for i, (far, near) in enumerate((
            (streams_far, streams), (taps_far, taps), (residue_far, residue),
            (damping_far, damping), (direct_far, direct),
        ))
    ]
    for load in loads:
        load.start()

    def lanes(g):
        return pl.ds(pl.multiple_of(g * LANES, LANES), LANES)

    barrier = pltpu.get_barrier_semaphore()

    @pl.loop(1, seq_count)
    def _(k):
        pl.semaphore_signal(
            barrier, inc=1, device_id=seq_device(lax.rem(me + k, seq_count)), device_id_type=MESH
        )

    for load in loads:
        load.wait()
    last = SUBS - 1 + valid
    second = jnp.maximum(last - 1, SUBS)

    @pl.loop(0, groups)
    def _(g):
        for p in range(3):
            padded[p, g, SUBS : SUBS + cap, :] = streams[p, :, lanes(g)].astype(jnp.float32)
            tail[g, p : p + 1, :] = padded[p, g, pl.ds(last, 1), :]
            tail[g, 3 + p : 4 + p, :] = padded[p, g, pl.ds(second, 1), :]
        tail[g, 6:8, :] = jnp.zeros((2, LANES), jnp.float32)

    pl.semaphore_wait(barrier, seq_count - 1 + seq_count // 2)

    def halo_copy(distance):
        target = lax.rem(me + distance, seq_count)
        return pltpu.make_async_remote_copy(
            src_ref=tail, dst_ref=halo.at[distance - 1], send_sem=halo_send.at[distance - 1],
            recv_sem=halo_recv.at[distance - 1], device_id=seq_device(target), device_id_type=MESH,
        )

    for distance in (1, 2):
        halo_copy(distance).start()
    for distance in (1, 2):
        halo_copy(distance).wait_recv()

    row = lax.broadcasted_iota(jnp.int32, (cap, LANES), 0)
    before_size = sizes[lax.rem(me + seq_count - 1, seq_count)]

    @pl.loop(0, groups)
    def _(g):
        at = lanes(g)
        features = []
        for p in range(3):
            last_one = jnp.where(me >= 1, halo[0, g, p : p + 1, :], 0.0)
            own_second = halo[0, g, 3 + p : 4 + p, :]
            far_last = jnp.where(me >= 2, halo[1, g, p : p + 1, :], 0.0)
            last_two = jnp.where(me >= 1, jnp.where(before_size >= 2, own_second, far_last), 0.0)
            padded[p, g, 6:7, :] = last_two
            padded[p, g, 7:8, :] = last_one
            features.append(
                taps[p, 0:1, at] * padded[p, g, 8 : 8 + cap, :]
                + taps[p, 1:2, at] * padded[p, g, 7 : 7 + cap, :]
                + taps[p, 2:3, at] * padded[p, g, 6 : 6 + cap, :]
            )
        query[g] = features[0].astype(jnp.bfloat16).astype(jnp.float32)
        product = (features[1] * features[2]).astype(jnp.bfloat16).astype(jnp.float32)
        gated[g] = jnp.where(row < valid, product, 0.0)

    def mode_rows(ref, at):
        return [jnp.broadcast_to(ref[m : m + 1, at], (SUBS, LANES)) for m in range(modes)]

    @pl.loop(0, groups)
    def _(g):
        at = lanes(g)
        decay = [jnp.exp(-d) for d in mode_rows(damping, at)]
        weight = mode_rows(residue, at)

        def step(i, states):
            u = gated[g, pl.ds(i, SUBS, stride=step_rows), :]
            return tuple(a * h + r * u for a, h, r in zip(decay, states, weight, strict=True))

        zero = jnp.zeros((SUBS, LANES), jnp.float32)
        states = lax.fori_loop(0, step_rows, step, (zero,) * modes, unroll=4)
        left_over = (cap - valid).astype(jnp.float32)
        for m in range(modes):
            rate = damping[m : m + 1, at]
            total = states[m]
            for by in (1, 2, 4):
                total = total + jnp.exp(-rate * (step_rows * by)) * shift_down(total, by)
            partial[g, m] = shift_down(total, 1)
            ends[m, pl.ds(g, 1), :] = total[SUBS - 1 : SUBS, :] * jnp.exp(rate * left_over)

    def end_copy(owner):
        return pltpu.make_async_remote_copy(
            src_ref=ends.at[pl.ds(owner * per_owner, per_owner)], dst_ref=end_in.at[me],
            send_sem=end_send.at[owner], recv_sem=end_recv.at[me],
            device_id=seq_device(owner), device_id_type=MESH,
        )

    def end_arrival(source):
        return pltpu.make_async_remote_copy(
            src_ref=ends.at[pl.ds(0, per_owner)], dst_ref=end_in.at[source],
            send_sem=end_send.at[0], recv_sem=end_recv.at[source],
            device_id=seq_device(source), device_id_type=MESH,
        )

    def carry_copy(target):
        return pltpu.make_async_remote_copy(
            src_ref=carry_out.at[target], dst_ref=carry_in.at[me],
            send_sem=carry_send.at[target], recv_sem=carry_recv.at[me],
            device_id=seq_device(target), device_id_type=MESH,
        )

    def carry_arrival(owner):
        return pltpu.make_async_remote_copy(
            src_ref=carry_out.at[0], dst_ref=carry_in.at[owner],
            send_sem=carry_send.at[0], recv_sem=carry_recv.at[owner],
            device_id=seq_device(owner), device_id_type=MESH,
        )

    @pl.loop(0, owners)
    def _(k):
        owner = lax.rem(me + k, owners)

        @pl.when(owner != me)
        def _():
            end_copy(owner).start()

    @pl.when(me < owners)
    def _():
        end_in[me] = ends[pl.ds(me * per_owner, per_owner)]
        mode = lax.broadcasted_iota(jnp.int32, (modes, LANES), 0)
        for j in range(per_owner):
            for g in range(groups):
                block = damping[:, g * LANES : (g + 1) * LANES]
                rates_own[j, g : g + 1, :] = jnp.sum(
                    jnp.where(mode == me * per_owner + j, block, 0.0), axis=0, keepdims=True
                )

        @pl.loop(0, seq_count)
        def _(source):
            @pl.when(source != me)
            def _():
                end_arrival(source).wait_recv()

        rate = rates_own[...]

        def advance(source, carry):
            carry_out[source] = carry
            return jnp.exp(-rate * sizes[source].astype(jnp.float32)) * carry + end_in[source]

        lax.fori_loop(0, seq_count, advance, jnp.zeros_like(rate), unroll=8)
        carry_in[me] = carry_out[me]

        @pl.loop(0, seq_count)
        def _(target):
            @pl.when(target != me)
            def _():
                carry_copy(target).start()

    @pl.loop(0, owners)
    def _(owner):
        @pl.when(owner != me)
        def _():
            carry_arrival(owner).wait_recv()

    def goes_to(g):
        return my_core * (z_count // 2) + g // 2, lax.rem(g, 2)

    def is_me(x, g):
        z, core = goes_to(g)
        return jnp.logical_and(jnp.logical_and(x == my_x, z == my_z), core == my_core)

    def piece_copy(x, g):
        z, core = goes_to(g)
        return pltpu.make_async_remote_copy(
            src_ref=hidden.at[g, x], dst_ref=gathered.at[me], send_sem=piece_send.at[x, g],
            recv_sem=piece_recv.at[me], device_id={**at_x(x), "z": z, "core": core},
            device_id_type=MESH,
        )

    def piece_arrival(source):
        return pltpu.make_async_remote_copy(
            src_ref=hidden.at[0, 0], dst_ref=gathered.at[source], send_sem=piece_send.at[0, 0],
            recv_sem=piece_recv.at[source],
            device_id={**seq_device(source), "core": source_core}, device_id_type=MESH,
        )

    own_group = lax.rem(my_z, z_count // 2) * 2 + my_core
    own_copy = pltpu.make_async_copy(hidden.at[own_group, my_x], gathered.at[me], local_sem)
    quarter = cap // 4

    @pl.loop(0, groups)
    def _(k):
        g = lax.rem(my_z + 1 + k, groups)
        at = lanes(g)
        rates = mode_rows(damping, at)
        decay = [jnp.exp(-d) for d in rates]
        weight = mode_rows(residue, at)
        sub = lax.broadcasted_iota(jnp.int32, (SUBS, LANES), 0).astype(jnp.float32) * step_rows
        start = tuple(
            partial[g, m]
            + jnp.exp(-rates[m] * sub)
            * carry_in[m // per_owner, m % per_owner, pl.ds(g, 1), :]
            for m in range(modes)
        )

        def step(i, states):
            rows = pl.ds(i, SUBS, stride=step_rows)
            u = gated[g, rows, :]
            states = tuple(a * h + r * u for a, h, r in zip(decay, states, weight, strict=True))
            mixed[rows, :] = tree_sum(list(states))
            return states

        lax.fori_loop(0, step_rows, step, start, unroll=4)
        conv = mixed[...] + direct[0:1, at] * gated[g]
        value = query[g] * conv
        quarters = [value[q * quarter : (q + 1) * quarter] for q in range(4)]
        for x in range(x_count):
            hidden[g, x] = repack(quarters, x).astype(jnp.bfloat16)

            @pl.when(jnp.logical_not(is_me(x, g)))
            def _():
                piece_copy(x, g).start()

            @pl.when(is_me(x, g))
            def _():
                own_copy.start()

    from_self = source_core == my_core

    @pl.when(from_self)
    def _():
        own_copy.wait()

    @pl.loop(0, seq_count)
    def _(other):
        @pl.when(jnp.logical_not(jnp.logical_and(from_self, other == me)))
        def _():
            piece_arrival(other).wait_recv()

        x, g = other // z_count, lax.rem(other, z_count)

        @pl.when(jnp.logical_not(is_me(x, g)))
        def _():
            piece_copy(x, g).wait_send()

    for distance in (1, 2):
        halo_copy(distance).wait_send()

    @pl.loop(0, owners)
    def _(owner):
        @pl.when(owner != me)
        def _():
            end_copy(owner).wait_send()

    @pl.when(me < owners)
    def _():
        @pl.loop(0, seq_count)
        def _(target):
            @pl.when(target != me)
            def _():
                carry_copy(target).wait_send()


def conv_call(dims, streams, sizes, taps, residue, damping, direct):
    x_count, z_count = dims["x"], dims["z"]
    cap, width = streams.shape[1:]
    modes = residue.shape[0]
    seq_count = x_count * z_count
    per_owner = max(1, modes // seq_count)
    owners = modes // per_owner
    f32, bf16 = jnp.float32, jnp.bfloat16
    dma = pltpu.SemaphoreType.DMA
    vmem = pl.BlockSpec(memory_space=pltpu.VMEM)
    far = pl.BlockSpec(memory_space=pl.ANY)
    return pl.pallas_call(
        functools.partial(conv_kernel, x_count, z_count),
        out_shape=jax.ShapeDtypeStruct((seq_count, cap // 4, LANES), bf16),
        in_specs=[pl.BlockSpec(memory_space=pltpu.SMEM)] + [far] * 5,
        out_specs=far,
        scratch_shapes=[
            pltpu.VMEM(streams.shape, bf16),
            pltpu.VMEM(taps.shape, f32),
            pltpu.VMEM(residue.shape, f32),
            pltpu.VMEM(damping.shape, f32),
            pltpu.VMEM(direct.shape, f32),
            pltpu.VMEM((3, z_count, cap + SUBS, LANES), f32),
            pltpu.VMEM((z_count, SUBS, LANES), f32),
            pltpu.VMEM((per_owner, z_count, LANES), f32),
            pltpu.VMEM((z_count, cap, LANES), f32),
            pltpu.VMEM((z_count, cap, LANES), f32),
            pltpu.VMEM((cap, LANES), f32),
            pltpu.VMEM((z_count, modes, SUBS, LANES), f32),
            pltpu.VMEM((modes, z_count, LANES), f32),
            pltpu.VMEM((seq_count, per_owner, z_count, LANES), f32),
            pltpu.VMEM((seq_count, per_owner, z_count, LANES), f32),
            pltpu.VMEM((owners, per_owner, z_count, LANES), f32),
            pltpu.VMEM((z_count, x_count, cap // 4, LANES), bf16),
            pltpu.VMEM((2, z_count, SUBS, LANES), f32),
            dma((2,)), dma((2,)),
            dma((owners,)), dma((seq_count,)), dma((seq_count,)), dma((owners,)),
        ]
        + [dma((x_count, z_count)), dma((seq_count,)), dma((5,)), dma],
        compiler_params=pltpu.CompilerParams(
            collective_id=0, has_side_effects=True, vmem_limit_bytes=VMEM
        ),
        name="convolve",
    )(sizes, streams, taps, residue, damping, direct)


def select_kernel(former, updated, remaining, pieces, chosen, sequence):
    seq_count, quarter, _ = pieces.shape
    lane_group = LANES // 4

    def place(s, start):
        piece = pieces[s].astype(jnp.float32)
        for q in range(4):
            turned = pltpu.roll(piece, (4 - q) % 4 * lane_group, 1)
            sequence[pl.ds(start + q * quarter, quarter), :] = turned
        return start + former[s]

    lax.fori_loop(0, seq_count, place, 0)
    row = lax.broadcasted_iota(jnp.int32, (quarter, LANES), 0)
    chosen[...] = jnp.zeros_like(chosen)

    def pick(k, start):
        quarters = []
        for q in range(4):
            rows = sequence[pl.ds(start + q * quarter, quarter), :]
            quarters.append(jnp.where(row + q * quarter < updated[k], rows, 0.0))
        chosen[remaining[k]] = repack(quarters, 0).astype(jnp.bfloat16)
        return start + updated[k]

    lax.fori_loop(0, updated.shape[0], pick, 0)


def select_call(seq_len, pieces, former, updated, remaining):
    smem = pl.BlockSpec(memory_space=pltpu.SMEM)
    vmem = pl.BlockSpec(memory_space=pltpu.VMEM)
    return pl.pallas_call(
        select_kernel,
        out_shape=jax.ShapeDtypeStruct(pieces.shape, jnp.bfloat16),
        in_specs=[smem] * 3 + [vmem],
        out_specs=vmem,
        scratch_shapes=[pltpu.VMEM((seq_len + 4 * pieces.shape[1], LANES), jnp.float32)],
        compiler_params=pltpu.CompilerParams(vmem_limit_bytes=24 << 20),
        name="reorder_rows",
    )(former, updated, remaining, pieces)


def project_kernel(
    x_count, z_count, y_count,
    chosen, block, out,
    landing, rows_in, weights, sum_out, sum_in,
    load_sem, own_sem, piece_send, piece_recv,
    right_send, right_recv, left_send, left_recv,
    far_a_send, far_a_recv, far_b_send, far_b_recv, core_send, core_recv,
    sum_send, sum_recv,
):
    cap, width = out.shape
    part_width = width // 2
    half, quarter = cap // 2, cap // 4
    reach = z_count // 2
    my_x, my_z = x_index(), lax.axis_index("z")
    my_y, my_core = lax.axis_index("y"), lax.axis_index("core")
    right, left = lax.rem(my_y + 1, y_count), lax.rem(my_y + y_count - 1, y_count)
    opposite = lax.rem(my_y + 2, y_count)
    other = 1 - my_core
    above, below = lax.rem(my_z + 1, z_count), lax.rem(my_z + z_count - 1, z_count)

    load = pltpu.make_async_copy(block, weights, load_sem)
    load.start()
    own_copy = pltpu.make_async_copy(
        chosen.at[pl.ds(my_x * z_count, z_count)], landing.at[my_x], own_sem
    )
    own_copy.start()

    barrier = pltpu.get_barrier_semaphore()
    for k in range(1, x_count):
        pl.semaphore_signal(
            barrier, inc=1, device_id=at_x(lax.rem(my_x + k, x_count)), device_id_type=MESH
        )
    for to in ({"y": right}, {"y": left}, {"core": other}, {"z": above}, {"z": below}):
        pl.semaphore_signal(barrier, inc=1, device_id=to, device_id_type=MESH)
    pl.semaphore_wait(barrier, x_count - 1 + 5)

    def piece_copy(x):
        return pltpu.make_async_remote_copy(
            src_ref=chosen.at[pl.ds(x * z_count, z_count)], dst_ref=landing.at[my_x],
            send_sem=piece_send.at[x], recv_sem=piece_recv.at[my_x],
            device_id=at_x(x), device_id_type=MESH,
        )

    def piece_arrival(x):
        return pltpu.make_async_remote_copy(
            src_ref=chosen.at[pl.ds(0, z_count)], dst_ref=landing.at[x],
            send_sem=piece_send.at[x], recv_sem=piece_recv.at[x],
            device_id=at_x(x), device_id_type=MESH,
        )

    others = [lax.rem(my_x + k, x_count) for k in (1, 3, 2)]
    for x in others:
        piece_copy(x).start()

    def columns(y, core):
        return pl.ds(pl.multiple_of((y * 2 + core) * LANES, LANES), LANES)

    def onward(y, core, owner, to, send, recv, first, rows):
        view = rows_in.at[owner, pl.ds(first, rows), columns(y, core)]
        return pltpu.make_async_remote_copy(
            src_ref=view, dst_ref=view, send_sem=send, recv_sem=recv,
            device_id=to, device_id_type=MESH,
        )

    def to_right(y, o):
        return onward(y, my_core, o, {"y": right}, right_send.at[o], right_recv.at[o], 0, cap)

    def to_left(y, o):
        return onward(y, my_core, o, {"y": left}, left_send.at[o], left_recv.at[o], 0, cap)

    def far_right(y, o):
        return onward(y, my_core, o, {"y": right}, far_a_send.at[o], far_a_recv.at[o], 0, half)

    def far_left(y, o):
        return onward(y, my_core, o, {"y": left}, far_b_send.at[o], far_b_recv.at[o], half, half)

    def to_core(y, core, o):
        return onward(y, core, o, {"core": other}, core_send.at[y, o], core_recv.at[y, o], 0, cap)

    def travels(way, distance, part):
        return distance < reach or part == way

    def slot(distance, part):
        return (distance - 1) * 2 + part

    def sum_copy(way, distance, part):
        at = slot(distance, part)
        return pltpu.make_async_remote_copy(
            src_ref=sum_out.at[way, at], dst_ref=sum_in.at[way, at],
            send_sem=sum_send.at[way, at], recv_sem=sum_recv.at[way, at],
            device_id={"z": below if way else above}, device_id_type=MESH,
        )

    def partial(owner, part):
        return jnp.dot(
            rows_in[owner], weights[:, part * part_width : (part + 1) * part_width],
            preferred_element_type=jnp.float32,
        )

    def ready(owner):
        @pl.loop(0, y_count)
        def _(y):
            to_core(y, other, owner).wait_recv()

    def send_sums(distance):
        owners = [lax.rem(my_z + d, z_count) for d in (distance, z_count - distance)]
        for owner in owners[: 1 if distance == reach else 2]:
            ready(owner)
        for part in range(2):
            for way in range(2):
                if travels(way, distance, part):
                    total = partial(owners[way], part)
                    if distance < reach and travels(way, distance + 1, part):
                        sum_copy(way, distance + 1, part).wait_recv()
                        total = total + sum_in[way, slot(distance + 1, part)].astype(jnp.float32)
                    sum_out[way, slot(distance, part)] = total.astype(jnp.bfloat16)
                    sum_copy(way, distance, part).start()

    order = [reach]
    for distance in range(reach - 1, 0, -1):
        order += [distance, z_count - distance]
    order = [lax.rem(my_z + d, z_count) for d in order + [0]]

    own_copy.wait()
    for x in others:
        piece_arrival(x).wait_recv()
    for owner in order:
        packed = [landing[x, owner].astype(jnp.float32) for x in range(x_count)]
        for q in range(4):
            rows_in[owner, q * quarter : (q + 1) * quarter, columns(my_y, my_core)] = repack(
                packed, q
            ).astype(jnp.bfloat16)
        to_right(my_y, owner).start()
        to_left(my_y, owner).start()
        to_core(my_y, my_core, owner).start()

    def finish(owner):
        far_right(opposite, owner).wait_recv()
        far_left(opposite, owner).wait_recv()
        to_core(opposite, my_core, owner).start()

    load.wait()
    for k, owner in enumerate(order):
        to_right(left, owner).wait_recv()
        far_right(left, owner).start()
        to_core(left, my_core, owner).start()
        to_left(right, owner).wait_recv()
        far_left(right, owner).start()
        to_core(right, my_core, owner).start()
        if k >= 1:
            finish(order[k - 1])
        if k == 2:
            send_sums(reach)
        if k == 5 and reach > 1:
            send_sums(reach - 1)
    finish(order[-1])
    if len(order) <= 2:
        send_sums(reach)
    for distance in range(reach - 2 if reach > 1 else 0, 0, -1):
        send_sums(distance)

    ready(my_z)
    for part in range(2):
        total = partial(my_z, part)
        for way in range(2):
            if travels(way, 1, part):
                sum_copy(way, 1, part).wait_recv()
                total = total + sum_in[way, slot(1, part)].astype(jnp.float32)
        out[:, part * part_width : (part + 1) * part_width] = total.astype(jnp.bfloat16)

    for distance in range(1, reach + 1):
        for part in range(2):
            for way in range(2):
                if travels(way, distance, part):
                    sum_copy(way, distance, part).wait_send()
    for x in others:
        piece_copy(x).wait_send()

    @pl.loop(0, z_count)
    def _(o):
        for y in range(y_count):
            to_core(y, my_core, o).wait_send()
        to_right(my_y, o).wait_send()
        to_left(my_y, o).wait_send()
        far_right(left, o).wait_send()
        far_left(right, o).wait_send()


def project_call(dims, chosen, block):
    x_count, y_count, z_count = dims["x"], dims["y"], dims["z"]
    cap = chosen.shape[1] * 4
    depth, width = block.shape
    reach = z_count // 2
    bf16 = jnp.bfloat16
    dma = pltpu.SemaphoreType.DMA
    vmem = pl.BlockSpec(memory_space=pltpu.VMEM)
    return pl.pallas_call(
        functools.partial(project_kernel, x_count, z_count, y_count),
        out_shape=jax.ShapeDtypeStruct((cap, width), bf16),
        in_specs=[vmem, pl.BlockSpec(memory_space=pl.ANY)],
        out_specs=vmem,
        scratch_shapes=[
            pltpu.VMEM((x_count, z_count, cap // 4, LANES), bf16),
            pltpu.VMEM((z_count, cap, depth), bf16),
            pltpu.VMEM((depth, width), bf16),
            pltpu.VMEM((2, 2 * reach, cap, width // 2), bf16),
            pltpu.VMEM((2, 2 * reach, cap, width // 2), bf16),
            dma, dma, dma((x_count,)), dma((x_count,)),
        ]
        + [dma((z_count,))] * 8
        + [dma((y_count, z_count))] * 2
        + [dma((2, 2 * reach))] * 2,
        compiler_params=pltpu.CompilerParams(
            collective_id=1, has_side_effects=True, vmem_limit_bytes=48 << 20
        ),
        name="project_rows",
    )(chosen, block)


def shards(
    dims,
    input_triple_streams,
    former_piece_sizes,
    updated_piece_sizes,
    remaining_indices,
    short_causal_filters,
    pole_coefficients,
    pole_damping,
    direct_coefficient,
    final_projector,
):
    cap = input_triple_streams.shape[0]
    seq_len = cap * 4 // 5 * dims["x"] * dims["z"]

    block = lax.all_gather(final_projector, ("x_high", "x_low"), axis=0, tiled=True)
    pieces = conv_call(
        dims,
        jnp.transpose(input_triple_streams, (1, 0, 2)),
        former_piece_sizes,
        short_causal_filters,
        pole_coefficients,
        pole_damping,
        direct_coefficient[None, :],
    )
    chosen = select_call(
        seq_len, pieces, former_piece_sizes, updated_piece_sizes, remaining_indices
    )
    return project_call(dims, chosen, block)


def solution(mesh):
    grid = (2, 2, mesh.shape["seq"] // 4, mesh.shape["chan"] // 2, 2)
    dims = {"x": 4, "z": grid[2], "y": grid[3]}
    rows, channels = SEQ, ("y", "core")
    return jax.shard_map(
        functools.partial(shards, dims),
        mesh=Mesh(mesh.devices.reshape(grid), AXES),
        in_specs=(
            P(rows, None, channels),
            P(),
            P(),
            P(),
            P(None, None, channels),
            P(None, channels),
            P(None, channels),
            P(channels),
            P(rows, channels),
        ),
        out_specs=P(rows, channels),
        check_vma=False,
    )
```

```python
import functools

import jax
import jax.numpy as jnp
from jax import lax
from jax.experimental import pallas as pl
from jax.experimental.pallas import tpu as pltpu
from jax.sharding import Mesh
from jax.sharding import PartitionSpec as P

MESH = pl.DeviceIdType.MESH
LANES = 128
SUBS = 8
AXES = ("x_high", "x_low", "z", "y", "core")
SEQ = ("x_high", "x_low", "z")


def x_index():
    return lax.axis_index("x_high") * 2 + lax.axis_index("x_low")


def at_x(x):
    return {"x_high": x // 2, "x_low": lax.rem(x, 2)}


def repack(quarters, k):
    group = lax.broadcasted_iota(jnp.int32, quarters[0].shape, 1) // (LANES // 4)
    result = jnp.zeros_like(quarters[0])
    for q in range(4):
        turned = pltpu.roll(quarters[q], ((q - k) % 4) * (LANES // 4), 1)
        result = jnp.where(group == q, turned, result)
    return result


def shift_down(value, by):
    row = lax.broadcasted_iota(jnp.int32, value.shape, 0)
    return jnp.where(row >= by, pltpu.roll(value, by, 0), 0.0)


def tree_sum(terms):
    while len(terms) > 1:
        terms = [a + b for a, b in zip(terms[::2], terms[1::2], strict=True)]
    return terms[0]


def conv_kernel(
    x_count, z_count,
    sizes, streams_far, taps_far, residue_far, damping_far, direct_far,
    gathered,
    streams, taps, residue, damping, direct, padded, tail, rates_own, query, gated, mixed, partial, ends, end_in, carry_out, carry_in, hidden, halo,
    halo_send, halo_recv, end_send, end_recv, carry_send, carry_recv,
    piece_send, piece_recv, load_sem, local_sem,
):
    modes = residue.shape[0]
    cap = streams.shape[1]
    groups = z_count
    step_rows = cap // SUBS
    seq_count = x_count * z_count
    per_owner = max(1, modes // seq_count)
    owners = modes // per_owner
    my_x, my_z, my_core = x_index(), lax.axis_index("z"), lax.axis_index("core")
    me = my_x * z_count + my_z
    valid = sizes[me]

    def seq_device(index):
        return {**at_x(index // z_count), "z": lax.rem(index, z_count)}

    source_core = my_z // (z_count // 2)

    @pl.when(source_core != lax.axis_index("core"))
    def _():
        @pl.loop(0, seq_count)
        def _(k):
            pl.semaphore_signal(
                pltpu.get_barrier_semaphore(), inc=1,
                device_id={**seq_device(lax.rem(me + k, seq_count)), "core": source_core},
                device_id_type=MESH,
            )

    loads = [
        pltpu.make_async_copy(far, near, load_sem.at[i])
        for i, (far, near) in enumerate((
            (streams_far, streams), (taps_far, taps), (residue_far, residue),
            (damping_far, damping), (direct_far, direct),
        ))
    ]
    for load in loads:
        load.start()

    def lanes(g):
        return pl.ds(pl.multiple_of(g * LANES, LANES), LANES)

    barrier = pltpu.get_barrier_semaphore()

    @pl.loop(1, seq_count)
    def _(k):
        pl.semaphore_signal(
            barrier, inc=1, device_id=seq_device(lax.rem(me + k, seq_count)), device_id_type=MESH
        )

    for load in loads:
        load.wait()
    last = SUBS - 1 + valid
    second = jnp.maximum(last - 1, SUBS)

    @pl.loop(0, groups)
    def _(g):
        for p in range(3):
            padded[p, g, SUBS : SUBS + cap, :] = streams[p, :, lanes(g)].astype(jnp.float32)
            tail[g, p : p + 1, :] = padded[p, g, pl.ds(last, 1), :]
            tail[g, 3 + p : 4 + p, :] = padded[p, g, pl.ds(second, 1), :]
        tail[g, 6:8, :] = jnp.zeros((2, LANES), jnp.float32)

    pl.semaphore_wait(barrier, seq_count - 1 + seq_count // 2)

    def halo_copy(distance):
        target = lax.rem(me + distance, seq_count)
        return pltpu.make_async_remote_copy(
            src_ref=tail, dst_ref=halo.at[distance - 1], send_sem=halo_send.at[distance - 1],
            recv_sem=halo_recv.at[distance - 1], device_id=seq_device(target), device_id_type=MESH,
        )

    for distance in (1, 2):
        halo_copy(distance).start()
    for distance in (1, 2):
        halo_copy(distance).wait_recv()

    row = lax.broadcasted_iota(jnp.int32, (cap, LANES), 0)
    before_size = sizes[lax.rem(me + seq_count - 1, seq_count)]

    def feature(p, g):
        at = lanes(g)
        last_one = jnp.where(me >= 1, halo[0, g, p : p + 1, :], 0.0)
        own_second = halo[0, g, 3 + p : 4 + p, :]
        far_last = jnp.where(me >= 2, halo[1, g, p : p + 1, :], 0.0)
        last_two = jnp.where(me >= 1, jnp.where(before_size >= 2, own_second, far_last), 0.0)
        padded[p, g, 6:7, :] = last_two
        padded[p, g, 7:8, :] = last_one
        return (
            taps[p, 0:1, at] * padded[p, g, 8 : 8 + cap, :]
            + taps[p, 1:2, at] * padded[p, g, 7 : 7 + cap, :]
            + taps[p, 2:3, at] * padded[p, g, 6 : 6 + cap, :]
        )

    @pl.loop(0, groups)
    def _(g):
        product = (feature(1, g) * feature(2, g)).astype(jnp.bfloat16).astype(jnp.float32)
        gated[g] = jnp.where(row < valid, product, 0.0)

    def mode_rows(ref, at):
        return [jnp.broadcast_to(ref[m : m + 1, at], (SUBS, LANES)) for m in range(modes)]

    @pl.loop(0, groups)
    def _(g):
        at = lanes(g)
        decay = [jnp.exp(-d) for d in mode_rows(damping, at)]
        weight = mode_rows(residue, at)

        def step(i, states):
            u = gated[g, pl.ds(i, SUBS, stride=step_rows), :]
            return tuple(a * h + r * u for a, h, r in zip(decay, states, weight, strict=True))

        zero = jnp.zeros((SUBS, LANES), jnp.float32)
        states = lax.fori_loop(0, step_rows, step, (zero,) * modes, unroll=4)
        left_over = (cap - valid).astype(jnp.float32)
        for m in range(modes):
            rate = damping[m : m + 1, at]
            total = states[m]
            for by in (1, 2, 4):
                total = total + jnp.exp(-rate * (step_rows * by)) * shift_down(total, by)
            partial[g, m] = shift_down(total, 1)
            ends[m, pl.ds(g, 1), :] = total[SUBS - 1 : SUBS, :] * jnp.exp(rate * left_over)

    def end_copy(owner):
        return pltpu.make_async_remote_copy(
            src_ref=ends.at[pl.ds(owner * per_owner, per_owner)], dst_ref=end_in.at[me],
            send_sem=end_send.at[owner], recv_sem=end_recv.at[me],
            device_id=seq_device(owner), device_id_type=MESH,
        )

    def end_arrival(source):
        return pltpu.make_async_remote_copy(
            src_ref=ends.at[pl.ds(0, per_owner)], dst_ref=end_in.at[source],
            send_sem=end_send.at[0], recv_sem=end_recv.at[source],
            device_id=seq_device(source), device_id_type=MESH,
        )

    def carry_copy(target):
        return pltpu.make_async_remote_copy(
            src_ref=carry_out.at[target], dst_ref=carry_in.at[me],
            send_sem=carry_send.at[target], recv_sem=carry_recv.at[me],
            device_id=seq_device(target), device_id_type=MESH,
        )

    def carry_arrival(owner):
        return pltpu.make_async_remote_copy(
            src_ref=carry_out.at[0], dst_ref=carry_in.at[owner],
            send_sem=carry_send.at[0], recv_sem=carry_recv.at[owner],
            device_id=seq_device(owner), device_id_type=MESH,
        )

    @pl.loop(0, owners)
    def _(k):
        owner = lax.rem(me + k, owners)

        @pl.when(owner != me)
        def _():
            end_copy(owner).start()

    @pl.when(me < owners)
    def _():
        end_in[me] = ends[pl.ds(me * per_owner, per_owner)]
        mode = lax.broadcasted_iota(jnp.int32, (modes, LANES), 0)
        for j in range(per_owner):
            for g in range(groups):
                block = damping[:, g * LANES : (g + 1) * LANES]
                rates_own[j, g : g + 1, :] = jnp.sum(
                    jnp.where(mode == me * per_owner + j, block, 0.0), axis=0, keepdims=True
                )

        @pl.loop(0, seq_count)
        def _(source):
            @pl.when(source != me)
            def _():
                end_arrival(source).wait_recv()

        rate = rates_own[...]

        def advance(source, carry):
            carry_out[source] = carry
            return jnp.exp(-rate * sizes[source].astype(jnp.float32)) * carry + end_in[source]

        lax.fori_loop(0, seq_count, advance, jnp.zeros_like(rate), unroll=8)
        carry_in[me] = carry_out[me]

        @pl.loop(0, seq_count)
        def _(target):
            @pl.when(target != me)
            def _():
                carry_copy(target).start()

    @pl.loop(0, groups)
    def _(g):
        query[g] = feature(0, g).astype(jnp.bfloat16).astype(jnp.float32)

    @pl.loop(0, owners)
    def _(owner):
        @pl.when(owner != me)
        def _():
            carry_arrival(owner).wait_recv()

    def goes_to(g):
        return my_core * (z_count // 2) + g // 2, lax.rem(g, 2)

    def is_me(x, g):
        z, core = goes_to(g)
        return jnp.logical_and(jnp.logical_and(x == my_x, z == my_z), core == my_core)

    def piece_copy(x, g):
        z, core = goes_to(g)
        return pltpu.make_async_remote_copy(
            src_ref=hidden.at[g, x], dst_ref=gathered.at[me], send_sem=piece_send.at[x, g],
            recv_sem=piece_recv.at[me], device_id={**at_x(x), "z": z, "core": core},
            device_id_type=MESH,
        )

    def piece_arrival(source):
        return pltpu.make_async_remote_copy(
            src_ref=hidden.at[0, 0], dst_ref=gathered.at[source], send_sem=piece_send.at[0, 0],
            recv_sem=piece_recv.at[source],
            device_id={**seq_device(source), "core": source_core}, device_id_type=MESH,
        )

    own_group = lax.rem(my_z, z_count // 2) * 2 + my_core
    own_copy = pltpu.make_async_copy(hidden.at[own_group, my_x], gathered.at[me], local_sem)
    quarter = cap // 4

    @pl.loop(0, groups)
    def _(k):
        g = lax.rem(my_z + 1 + k, groups)
        at = lanes(g)
        rates = mode_rows(damping, at)
        decay = [jnp.exp(-d) for d in rates]
        weight = mode_rows(residue, at)
        sub = lax.broadcasted_iota(jnp.int32, (SUBS, LANES), 0).astype(jnp.float32) * step_rows
        start = tuple(
            partial[g, m]
            + jnp.exp(-rates[m] * sub)
            * carry_in[m // per_owner, m % per_owner, pl.ds(g, 1), :]
            for m in range(modes)
        )

        def step(i, states):
            rows = pl.ds(i, SUBS, stride=step_rows)
            u = gated[g, rows, :]
            states = tuple(a * h + r * u for a, h, r in zip(decay, states, weight, strict=True))
            mixed[rows, :] = tree_sum(list(states))
            return states

        lax.fori_loop(0, step_rows, step, start, unroll=4)
        conv = mixed[...] + direct[0:1, at] * gated[g]
        value = query[g] * conv
        quarters = [value[q * quarter : (q + 1) * quarter] for q in range(4)]
        for x in range(x_count):
            hidden[g, x] = repack(quarters, x).astype(jnp.bfloat16)

            @pl.when(jnp.logical_not(is_me(x, g)))
            def _():
                piece_copy(x, g).start()

            @pl.when(is_me(x, g))
            def _():
                own_copy.start()

    from_self = source_core == my_core

    @pl.when(from_self)
    def _():
        own_copy.wait()

    @pl.loop(0, seq_count)
    def _(other):
        @pl.when(jnp.logical_not(jnp.logical_and(from_self, other == me)))
        def _():
            piece_arrival(other).wait_recv()

        x, g = other // z_count, lax.rem(other, z_count)

        @pl.when(jnp.logical_not(is_me(x, g)))
        def _():
            piece_copy(x, g).wait_send()

    for distance in (1, 2):
        halo_copy(distance).wait_send()

    @pl.loop(0, owners)
    def _(owner):
        @pl.when(owner != me)
        def _():
            end_copy(owner).wait_send()

    @pl.when(me < owners)
    def _():
        @pl.loop(0, seq_count)
        def _(target):
            @pl.when(target != me)
            def _():
                carry_copy(target).wait_send()


def conv_call(dims, streams, sizes, taps, residue, damping, direct):
    x_count, z_count = dims["x"], dims["z"]
    cap, width = streams.shape[1:]
    modes = residue.shape[0]
    seq_count = x_count * z_count
    per_owner = max(1, modes // seq_count)
    owners = modes // per_owner
    f32, bf16 = jnp.float32, jnp.bfloat16
    dma = pltpu.SemaphoreType.DMA
    vmem = pl.BlockSpec(memory_space=pltpu.VMEM)
    far = pl.BlockSpec(memory_space=pltpu.HBM)
    return pl.pallas_call(
        functools.partial(conv_kernel, x_count, z_count),
        out_shape=jax.ShapeDtypeStruct((seq_count, cap // 4, LANES), bf16),
        in_specs=[pl.BlockSpec(memory_space=pltpu.SMEM)] + [far] * 5,
        out_specs=pl.BlockSpec(memory_space=pl.ANY),
        scratch_shapes=[
            pltpu.VMEM(streams.shape, bf16),
            pltpu.VMEM(taps.shape, f32),
            pltpu.VMEM(residue.shape, f32),
            pltpu.VMEM(damping.shape, f32),
            pltpu.VMEM(direct.shape, f32),
            pltpu.VMEM((3, z_count, cap + SUBS, LANES), f32),
            pltpu.VMEM((z_count, SUBS, LANES), f32),
            pltpu.VMEM((per_owner, z_count, LANES), f32),
            pltpu.VMEM((z_count, cap, LANES), f32),
            pltpu.VMEM((z_count, cap, LANES), f32),
            pltpu.VMEM((cap, LANES), f32),
            pltpu.VMEM((z_count, modes, SUBS, LANES), f32),
            pltpu.VMEM((modes, z_count, LANES), f32),
            pltpu.VMEM((seq_count, per_owner, z_count, LANES), f32),
            pltpu.VMEM((seq_count, per_owner, z_count, LANES), f32),
            pltpu.VMEM((owners, per_owner, z_count, LANES), f32),
            pltpu.VMEM((z_count, x_count, cap // 4, LANES), bf16),
            pltpu.VMEM((2, z_count, SUBS, LANES), f32),
            dma((2,)), dma((2,)),
            dma((owners,)), dma((seq_count,)), dma((seq_count,)), dma((owners,)),
        ]
        + [dma((x_count, z_count)), dma((seq_count,)), dma((5,)), dma],
        compiler_params=pltpu.CompilerParams(
            collective_id=0, has_side_effects=True, vmem_limit_bytes=56 << 20
        ),
        name="convolve",
    )(sizes, streams, taps, residue, damping, direct)


def select_kernel(former, updated, remaining, pieces, chosen, sequence):
    seq_count, quarter, _ = pieces.shape
    lane_group = LANES // 4

    def place(s, start):
        piece = pieces[s].astype(jnp.float32)
        for q in range(4):
            turned = pltpu.roll(piece, (4 - q) % 4 * lane_group, 1)
            sequence[pl.ds(start + q * quarter, quarter), :] = turned
        return start + former[s]

    lax.fori_loop(0, seq_count, place, 0)
    row = lax.broadcasted_iota(jnp.int32, (quarter, LANES), 0)
    chosen[...] = jnp.zeros_like(chosen)

    def pick(k, start):
        quarters = []
        for q in range(4):
            rows = sequence[pl.ds(start + q * quarter, quarter), :]
            quarters.append(jnp.where(row + q * quarter < updated[k], rows, 0.0))
        chosen[remaining[k]] = repack(quarters, 0).astype(jnp.bfloat16)
        return start + updated[k]

    lax.fori_loop(0, updated.shape[0], pick, 0)


def select_call(seq_len, pieces, former, updated, remaining):
    smem = pl.BlockSpec(memory_space=pltpu.SMEM)
    vmem = pl.BlockSpec(memory_space=pltpu.VMEM)
    return pl.pallas_call(
        select_kernel,
        out_shape=jax.ShapeDtypeStruct(pieces.shape, jnp.bfloat16),
        in_specs=[smem] * 3 + [vmem],
        out_specs=vmem,
        scratch_shapes=[pltpu.VMEM((seq_len + 4 * pieces.shape[1], LANES), jnp.float32)],
        compiler_params=pltpu.CompilerParams(vmem_limit_bytes=24 << 20),
        name="reorder_rows",
    )(former, updated, remaining, pieces)


def project_kernel(
    x_count, z_count, y_count,
    chosen, block, out,
    landing, rows_in, weights, sum_out, sum_in,
    load_sem, own_sem, piece_send, piece_recv,
    right_send, right_recv, left_send, left_recv,
    far_a_send, far_a_recv, far_b_send, far_b_recv, core_send, core_recv,
    sum_send, sum_recv,
):
    cap, width = out.shape
    part_width = width // 2
    half, quarter = cap // 2, cap // 4
    reach = z_count // 2
    my_x, my_z = x_index(), lax.axis_index("z")
    my_y, my_core = lax.axis_index("y"), lax.axis_index("core")
    right, left = lax.rem(my_y + 1, y_count), lax.rem(my_y + y_count - 1, y_count)
    opposite = lax.rem(my_y + 2, y_count)
    other = 1 - my_core
    above, below = lax.rem(my_z + 1, z_count), lax.rem(my_z + z_count - 1, z_count)

    load = pltpu.make_async_copy(block, weights, load_sem)
    load.start()
    own_copy = pltpu.make_async_copy(
        chosen.at[pl.ds(my_x * z_count, z_count)], landing.at[my_x], own_sem
    )
    own_copy.start()

    barrier = pltpu.get_barrier_semaphore()
    for k in range(1, x_count):
        pl.semaphore_signal(
            barrier, inc=1, device_id=at_x(lax.rem(my_x + k, x_count)), device_id_type=MESH
        )
    for to in ({"y": right}, {"y": left}, {"core": other}, {"z": above}, {"z": below}):
        pl.semaphore_signal(barrier, inc=1, device_id=to, device_id_type=MESH)
    pl.semaphore_wait(barrier, x_count - 1 + 5)

    def piece_copy(x, owner):
        return pltpu.make_async_remote_copy(
            src_ref=chosen.at[x * z_count + owner], dst_ref=landing.at[my_x, owner],
            send_sem=piece_send.at[x, owner], recv_sem=piece_recv.at[my_x, owner],
            device_id=at_x(x), device_id_type=MESH,
        )

    def piece_arrival(x, owner):
        return pltpu.make_async_remote_copy(
            src_ref=chosen.at[owner], dst_ref=landing.at[x, owner],
            send_sem=piece_send.at[x, owner], recv_sem=piece_recv.at[x, owner],
            device_id=at_x(x), device_id_type=MESH,
        )

    order = [reach]
    for distance in range(reach - 1, 0, -1):
        order += [distance, z_count - distance]
    order = [lax.rem(my_z + d, z_count) for d in order + [0]]
    others = [lax.rem(my_x + k, x_count) for k in (1, 3, 2)]
    for owner in order:
        for x in others:
            piece_copy(x, owner).start()

    def columns(y, core):
        return pl.ds(pl.multiple_of((y * 2 + core) * LANES, LANES), LANES)

    def onward(y, core, owner, to, send, recv, first, rows):
        view = rows_in.at[owner, pl.ds(first, rows), columns(y, core)]
        return pltpu.make_async_remote_copy(
            src_ref=view, dst_ref=view, send_sem=send, recv_sem=recv,
            device_id=to, device_id_type=MESH,
        )

    def to_right(y, o):
        return onward(y, my_core, o, {"y": right}, right_send.at[o], right_recv.at[o], 0, cap)

    def to_left(y, o):
        return onward(y, my_core, o, {"y": left}, left_send.at[o], left_recv.at[o], 0, cap)

    def far_right(y, o):
        return onward(y, my_core, o, {"y": right}, far_a_send.at[o], far_a_recv.at[o], 0, half)

    def far_left(y, o):
        return onward(y, my_core, o, {"y": left}, far_b_send.at[o], far_b_recv.at[o], half, half)

    def to_core(y, core, o):
        return onward(y, core, o, {"core": other}, core_send.at[y, o], core_recv.at[y, o], 0, cap)

    def travels(way, distance, part):
        return distance < reach or part == way

    def slot(distance, part):
        return (distance - 1) * 2 + part

    def sum_copy(way, distance, part):
        at = slot(distance, part)
        return pltpu.make_async_remote_copy(
            src_ref=sum_out.at[way, at], dst_ref=sum_in.at[way, at],
            send_sem=sum_send.at[way, at], recv_sem=sum_recv.at[way, at],
            device_id={"z": below if way else above}, device_id_type=MESH,
        )

    def partial(owner, part):
        return jnp.dot(
            rows_in[owner], weights[:, part * part_width : (part + 1) * part_width],
            preferred_element_type=jnp.float32,
        )

    def ready(owner):
        @pl.loop(0, y_count)
        def _(y):
            to_core(y, other, owner).wait_recv()

    def send_sums(distance):
        owners = [lax.rem(my_z + d, z_count) for d in (distance, z_count - distance)]
        for owner in owners[: 1 if distance == reach else 2]:
            ready(owner)
        for way, part in ((0, 1), (1, 0), (0, 0), (1, 1)):
            if travels(way, distance, part):
                total = partial(owners[way], part)
                if distance < reach and travels(way, distance + 1, part):
                    sum_copy(way, distance + 1, part).wait_recv()
                    total = total + sum_in[way, slot(distance + 1, part)].astype(jnp.float32)
                sum_out[way, slot(distance, part)] = total.astype(jnp.bfloat16)
                sum_copy(way, distance, part).start()

    own_copy.wait()

    def launch(owner):
        for x in others:
            piece_arrival(x, owner).wait_recv()
        packed = [landing[x, owner].astype(jnp.float32) for x in range(x_count)]
        for q in range(4):
            rows_in[owner, q * quarter : (q + 1) * quarter, columns(my_y, my_core)] = repack(
                packed, q
            ).astype(jnp.bfloat16)
        to_right(my_y, owner).start()
        to_left(my_y, owner).start()
        to_core(my_y, my_core, owner).start()

    def finish(owner):
        far_right(opposite, owner).wait_recv()
        far_left(opposite, owner).wait_recv()
        to_core(opposite, my_core, owner).start()

    ahead, lag = 3, 2
    for owner in order[:ahead]:
        launch(owner)
    load.wait()
    sent = reach + 1
    for k in range(len(order) + lag):
        if k + ahead < len(order):
            launch(order[k + ahead])
        if k < len(order):
            owner = order[k]
            to_right(left, owner).wait_recv()
            far_right(left, owner).start()
            to_core(left, my_core, owner).start()
            to_left(right, owner).wait_recv()
            far_left(right, owner).start()
            to_core(right, my_core, owner).start()
        if k >= lag:
            finish(order[k - lag])
        if k == lag or k == lag + 2 and reach > 1:
            sent -= 1
            send_sums(sent)
    for distance in range(sent - 1, 0, -1):
        send_sums(distance)

    ready(my_z)
    for part in range(2):
        total = partial(my_z, part)
        for way in range(2):
            if travels(way, 1, part):
                sum_copy(way, 1, part).wait_recv()
                total = total + sum_in[way, slot(1, part)].astype(jnp.float32)
        out[:, part * part_width : (part + 1) * part_width] = total.astype(jnp.bfloat16)

    for distance in range(1, reach + 1):
        for part in range(2):
            for way in range(2):
                if travels(way, distance, part):
                    sum_copy(way, distance, part).wait_send()
    for owner in order:
        for x in others:
            piece_copy(x, owner).wait_send()

    @pl.loop(0, z_count)
    def _(o):
        for y in range(y_count):
            to_core(y, my_core, o).wait_send()
        to_right(my_y, o).wait_send()
        to_left(my_y, o).wait_send()
        far_right(left, o).wait_send()
        far_left(right, o).wait_send()


def project_call(dims, chosen, block):
    x_count, y_count, z_count = dims["x"], dims["y"], dims["z"]
    cap = chosen.shape[1] * 4
    depth, width = block.shape
    reach = z_count // 2
    bf16 = jnp.bfloat16
    dma = pltpu.SemaphoreType.DMA
    vmem = pl.BlockSpec(memory_space=pltpu.VMEM)
    return pl.pallas_call(
        functools.partial(project_kernel, x_count, z_count, y_count),
        out_shape=jax.ShapeDtypeStruct((cap, width), bf16),
        in_specs=[vmem, pl.BlockSpec(memory_space=pltpu.HBM)],
        out_specs=vmem,
        scratch_shapes=[
            pltpu.VMEM((x_count, z_count, cap // 4, LANES), bf16),
            pltpu.VMEM((z_count, cap, depth), bf16),
            pltpu.VMEM((depth, width), bf16),
            pltpu.VMEM((2, 2 * reach, cap, width // 2), bf16),
            pltpu.VMEM((2, 2 * reach, cap, width // 2), bf16),
            dma, dma, dma((x_count, z_count)), dma((x_count, z_count)),
        ]
        + [dma((z_count,))] * 8
        + [dma((y_count, z_count))] * 2
        + [dma((2, 2 * reach))] * 2,
        compiler_params=pltpu.CompilerParams(
            collective_id=1, has_side_effects=True, vmem_limit_bytes=60 << 20
        ),
        name="project_rows",
    )(chosen, block)


def shards(
    dims,
    input_triple_streams,
    former_piece_sizes,
    updated_piece_sizes,
    remaining_indices,
    short_causal_filters,
    pole_coefficients,
    pole_damping,
    direct_coefficient,
    final_projector,
):
    cap = input_triple_streams.shape[0]
    seq_len = cap * 4 // 5 * dims["x"] * dims["z"]

    block = lax.all_gather(final_projector, ("x_high", "x_low"), axis=0, tiled=True)
    pieces = conv_call(
        dims,
        jnp.transpose(input_triple_streams, (1, 0, 2)),
        former_piece_sizes,
        short_causal_filters,
        pole_coefficients,
        pole_damping,
        direct_coefficient[None, :],
    )
    chosen = select_call(
        seq_len, pieces, former_piece_sizes, updated_piece_sizes, remaining_indices
    )
    return project_call(dims, chosen, block)


def solution(mesh):
    grid = (2, 2, mesh.shape["seq"] // 4, mesh.shape["chan"] // 2, 2)
    dims = {"x": 4, "z": grid[2], "y": grid[3]}
    rows, channels = SEQ, ("y", "core")
    return jax.shard_map(
        functools.partial(shards, dims),
        mesh=Mesh(mesh.devices.reshape(grid), AXES),
        in_specs=(
            P(rows, None, channels),
            P(),
            P(),
            P(),
            P(None, None, channels),
            P(None, channels),
            P(None, channels),
            P(channels),
            P(rows, channels),
        ),
        out_specs=P(rows, channels),
        check_vma=False,
    )
```

```python
import functools

import jax
import jax.numpy as jnp
from jax import lax
from jax.experimental import pallas as pl
from jax.experimental.pallas import tpu as pltpu
from jax.sharding import Mesh
from jax.sharding import PartitionSpec as P

MESH = pl.DeviceIdType.MESH
LANES = 128
SUBS = 8
AXES = ("x_high", "x_low", "z", "y", "core")
SEQ = ("x_high", "x_low", "z")


def x_index():
    return lax.axis_index("x_high") * 2 + lax.axis_index("x_low")


def at_x(x):
    return {"x_high": x // 2, "x_low": lax.rem(x, 2)}


def repack(quarters, k):
    group = lax.broadcasted_iota(jnp.int32, quarters[0].shape, 1) // (LANES // 4)
    result = jnp.zeros_like(quarters[0])
    for q in range(4):
        turned = pltpu.roll(quarters[q], ((q - k) % 4) * (LANES // 4), 1)
        result = jnp.where(group == q, turned, result)
    return result


def shift_down(value, by):
    row = lax.broadcasted_iota(jnp.int32, value.shape, 0)
    return jnp.where(row >= by, pltpu.roll(value, by, 0), 0.0)


def tree_sum(terms):
    while len(terms) > 1:
        terms = [a + b for a, b in zip(terms[::2], terms[1::2], strict=True)]
    return terms[0]


def conv_kernel(
    x_count, z_count,
    sizes, streams_far, taps_far, residue_far, damping_far, direct_far,
    gathered,
    streams, taps, residue, damping, direct, padded, tail, rates_own, query, gated, mixed, partial, ends, end_in, carry_out, carry_in, hidden, halo,
    halo_send, halo_recv, end_send, end_recv, carry_send, carry_recv,
    piece_send, piece_recv, load_sem, local_sem,
):
    modes = residue.shape[0]
    cap = streams.shape[1]
    groups = z_count
    step_rows = cap // SUBS
    seq_count = x_count * z_count
    per_owner = max(1, modes // seq_count)
    owners = modes // per_owner
    my_x, my_z, my_core = x_index(), lax.axis_index("z"), lax.axis_index("core")
    me = my_x * z_count + my_z
    valid = sizes[me]

    def seq_device(index):
        return {**at_x(index // z_count), "z": lax.rem(index, z_count)}

    source_core = my_z // (z_count // 2)

    @pl.when(source_core != lax.axis_index("core"))
    def _():
        @pl.loop(0, seq_count)
        def _(k):
            pl.semaphore_signal(
                pltpu.get_barrier_semaphore(), inc=1,
                device_id={**seq_device(lax.rem(me + k, seq_count)), "core": source_core},
                device_id_type=MESH,
            )

    loads = [
        pltpu.make_async_copy(far, near, load_sem.at[i])
        for i, (far, near) in enumerate((
            (streams_far, streams), (taps_far, taps), (residue_far, residue),
            (damping_far, damping), (direct_far, direct),
        ))
    ]
    for load in loads:
        load.start()

    def lanes(g):
        return pl.ds(pl.multiple_of(g * LANES, LANES), LANES)

    barrier = pltpu.get_barrier_semaphore()

    @pl.loop(1, seq_count)
    def _(k):
        pl.semaphore_signal(
            barrier, inc=1, device_id=seq_device(lax.rem(me + k, seq_count)), device_id_type=MESH
        )

    for load in loads:
        load.wait()
    last = SUBS - 1 + valid
    second = jnp.maximum(last - 1, SUBS)

    @pl.loop(0, groups)
    def _(g):
        for p in range(3):
            padded[p, g, SUBS : SUBS + cap, :] = streams[p, :, lanes(g)].astype(jnp.float32)
            tail[g, p : p + 1, :] = padded[p, g, pl.ds(last, 1), :]
            tail[g, 3 + p : 4 + p, :] = padded[p, g, pl.ds(second, 1), :]
        tail[g, 6:8, :] = jnp.zeros((2, LANES), jnp.float32)

    pl.semaphore_wait(barrier, seq_count - 1 + seq_count // 2)

    def halo_copy(distance):
        target = lax.rem(me + distance, seq_count)
        return pltpu.make_async_remote_copy(
            src_ref=tail, dst_ref=halo.at[distance - 1], send_sem=halo_send.at[distance - 1],
            recv_sem=halo_recv.at[distance - 1], device_id=seq_device(target), device_id_type=MESH,
        )

    for distance in (1, 2):
        halo_copy(distance).start()
    for distance in (1, 2):
        halo_copy(distance).wait_recv()

    row = lax.broadcasted_iota(jnp.int32, (cap, LANES), 0)
    before_size = sizes[lax.rem(me + seq_count - 1, seq_count)]

    def feature(p, g):
        at = lanes(g)
        last_one = jnp.where(me >= 1, halo[0, g, p : p + 1, :], 0.0)
        own_second = halo[0, g, 3 + p : 4 + p, :]
        far_last = jnp.where(me >= 2, halo[1, g, p : p + 1, :], 0.0)
        last_two = jnp.where(me >= 1, jnp.where(before_size >= 2, own_second, far_last), 0.0)
        padded[p, g, 6:7, :] = last_two
        padded[p, g, 7:8, :] = last_one
        return (
            taps[p, 0:1, at] * padded[p, g, 8 : 8 + cap, :]
            + taps[p, 1:2, at] * padded[p, g, 7 : 7 + cap, :]
            + taps[p, 2:3, at] * padded[p, g, 6 : 6 + cap, :]
        )

    @pl.loop(0, groups)
    def _(g):
        product = (feature(1, g) * feature(2, g)).astype(jnp.bfloat16).astype(jnp.float32)
        gated[g] = jnp.where(row < valid, product, 0.0)

    def mode_rows(ref, at):
        return [jnp.broadcast_to(ref[m : m + 1, at], (SUBS, LANES)) for m in range(modes)]

    @pl.loop(0, groups)
    def _(g):
        at = lanes(g)
        decay = [jnp.exp(-d) for d in mode_rows(damping, at)]
        weight = mode_rows(residue, at)

        def step(i, states):
            u = gated[g, pl.ds(i, SUBS, stride=step_rows), :]
            return tuple(a * h + r * u for a, h, r in zip(decay, states, weight, strict=True))

        zero = jnp.zeros((SUBS, LANES), jnp.float32)
        states = lax.fori_loop(0, step_rows, step, (zero,) * modes, unroll=4)
        left_over = (cap - valid).astype(jnp.float32)
        for m in range(modes):
            rate = damping[m : m + 1, at]
            total = states[m]
            for by in (1, 2, 4):
                total = total + jnp.exp(-rate * (step_rows * by)) * shift_down(total, by)
            partial[g, m] = shift_down(total, 1)
            ends[m, pl.ds(g, 1), :] = total[SUBS - 1 : SUBS, :] * jnp.exp(rate * left_over)

    def end_copy(owner):
        return pltpu.make_async_remote_copy(
            src_ref=ends.at[pl.ds(owner * per_owner, per_owner)], dst_ref=end_in.at[me],
            send_sem=end_send.at[owner], recv_sem=end_recv.at[me],
            device_id=seq_device(owner), device_id_type=MESH,
        )

    def end_arrival(source):
        return pltpu.make_async_remote_copy(
            src_ref=ends.at[pl.ds(0, per_owner)], dst_ref=end_in.at[source],
            send_sem=end_send.at[0], recv_sem=end_recv.at[source],
            device_id=seq_device(source), device_id_type=MESH,
        )

    def carry_copy(target):
        return pltpu.make_async_remote_copy(
            src_ref=carry_out.at[target], dst_ref=carry_in.at[me],
            send_sem=carry_send.at[target], recv_sem=carry_recv.at[me],
            device_id=seq_device(target), device_id_type=MESH,
        )

    def carry_arrival(owner):
        return pltpu.make_async_remote_copy(
            src_ref=carry_out.at[0], dst_ref=carry_in.at[owner],
            send_sem=carry_send.at[0], recv_sem=carry_recv.at[owner],
            device_id=seq_device(owner), device_id_type=MESH,
        )

    @pl.loop(0, owners)
    def _(k):
        owner = lax.rem(me + k, owners)

        @pl.when(owner != me)
        def _():
            end_copy(owner).start()

    @pl.when(me < owners)
    def _():
        end_in[me] = ends[pl.ds(me * per_owner, per_owner)]
        mode = lax.broadcasted_iota(jnp.int32, (modes, LANES), 0)
        for j in range(per_owner):
            for g in range(groups):
                block = damping[:, g * LANES : (g + 1) * LANES]
                rates_own[j, g : g + 1, :] = jnp.sum(
                    jnp.where(mode == me * per_owner + j, block, 0.0), axis=0, keepdims=True
                )

        @pl.loop(0, seq_count)
        def _(source):
            @pl.when(source != me)
            def _():
                end_arrival(source).wait_recv()

        rate = rates_own[...]

        def advance(source, carry):
            carry_out[source] = carry
            return jnp.exp(-rate * sizes[source].astype(jnp.float32)) * carry + end_in[source]

        lax.fori_loop(0, seq_count, advance, jnp.zeros_like(rate), unroll=8)
        carry_in[me] = carry_out[me]

        @pl.loop(0, seq_count)
        def _(target):
            @pl.when(target != me)
            def _():
                carry_copy(target).start()

    @pl.loop(0, groups)
    def _(g):
        query[g] = feature(0, g).astype(jnp.bfloat16).astype(jnp.float32)

    @pl.loop(0, owners)
    def _(owner):
        @pl.when(owner != me)
        def _():
            carry_arrival(owner).wait_recv()

    def goes_to(g):
        return my_core * (z_count // 2) + g // 2, lax.rem(g, 2)

    def is_me(x, g):
        z, core = goes_to(g)
        return jnp.logical_and(jnp.logical_and(x == my_x, z == my_z), core == my_core)

    def piece_copy(x, g):
        z, core = goes_to(g)
        return pltpu.make_async_remote_copy(
            src_ref=hidden.at[g, x], dst_ref=gathered.at[me], send_sem=piece_send.at[x, g],
            recv_sem=piece_recv.at[me], device_id={**at_x(x), "z": z, "core": core},
            device_id_type=MESH,
        )

    def piece_arrival(source):
        return pltpu.make_async_remote_copy(
            src_ref=hidden.at[0, 0], dst_ref=gathered.at[source], send_sem=piece_send.at[0, 0],
            recv_sem=piece_recv.at[source],
            device_id={**seq_device(source), "core": source_core}, device_id_type=MESH,
        )

    own_group = lax.rem(my_z, z_count // 2) * 2 + my_core
    own_copy = pltpu.make_async_copy(hidden.at[own_group, my_x], gathered.at[me], local_sem)
    quarter = cap // 4

    @pl.loop(0, groups)
    def _(k):
        g = lax.rem(my_z + 1 + k, groups)
        at = lanes(g)
        rates = mode_rows(damping, at)
        decay = [jnp.exp(-d) for d in rates]
        weight = mode_rows(residue, at)
        sub = lax.broadcasted_iota(jnp.int32, (SUBS, LANES), 0).astype(jnp.float32) * step_rows
        start = tuple(
            partial[g, m]
            + jnp.exp(-rates[m] * sub)
            * carry_in[m // per_owner, m % per_owner, pl.ds(g, 1), :]
            for m in range(modes)
        )

        def step(i, states):
            rows = pl.ds(i, SUBS, stride=step_rows)
            u = gated[g, rows, :]
            states = tuple(a * h + r * u for a, h, r in zip(decay, states, weight, strict=True))
            mixed[rows, :] = tree_sum(list(states))
            return states

        lax.fori_loop(0, step_rows, step, start, unroll=4)
        conv = mixed[...] + direct[0:1, at] * gated[g]
        mixed[...] = query[g] * conv
        quarters = [mixed[pl.ds(q, quarter, stride=4), :] for q in range(4)]
        for x in range(x_count):
            hidden[g, x] = repack(quarters, x).astype(jnp.bfloat16)

            @pl.when(jnp.logical_not(is_me(x, g)))
            def _():
                piece_copy(x, g).start()

            @pl.when(is_me(x, g))
            def _():
                own_copy.start()

    from_self = source_core == my_core

    @pl.when(from_self)
    def _():
        own_copy.wait()

    @pl.loop(0, seq_count)
    def _(other):
        @pl.when(jnp.logical_not(jnp.logical_and(from_self, other == me)))
        def _():
            piece_arrival(other).wait_recv()

        x, g = other // z_count, lax.rem(other, z_count)

        @pl.when(jnp.logical_not(is_me(x, g)))
        def _():
            piece_copy(x, g).wait_send()

    for distance in (1, 2):
        halo_copy(distance).wait_send()

    @pl.loop(0, owners)
    def _(owner):
        @pl.when(owner != me)
        def _():
            end_copy(owner).wait_send()

    @pl.when(me < owners)
    def _():
        @pl.loop(0, seq_count)
        def _(target):
            @pl.when(target != me)
            def _():
                carry_copy(target).wait_send()


def conv_call(dims, streams, sizes, taps, residue, damping, direct):
    x_count, z_count = dims["x"], dims["z"]
    cap, width = streams.shape[1:]
    modes = residue.shape[0]
    seq_count = x_count * z_count
    per_owner = max(1, modes // seq_count)
    owners = modes // per_owner
    f32, bf16 = jnp.float32, jnp.bfloat16
    dma = pltpu.SemaphoreType.DMA
    vmem = pl.BlockSpec(memory_space=pltpu.VMEM)
    far = pl.BlockSpec(memory_space=pltpu.HBM)
    return pl.pallas_call(
        functools.partial(conv_kernel, x_count, z_count),
        out_shape=jax.ShapeDtypeStruct((seq_count, cap // 4, LANES), bf16),
        in_specs=[pl.BlockSpec(memory_space=pltpu.SMEM)] + [far] * 5,
        out_specs=pl.BlockSpec(memory_space=pl.ANY),
        scratch_shapes=[
            pltpu.VMEM(streams.shape, bf16),
            pltpu.VMEM(taps.shape, f32),
            pltpu.VMEM(residue.shape, f32),
            pltpu.VMEM(damping.shape, f32),
            pltpu.VMEM(direct.shape, f32),
            pltpu.VMEM((3, z_count, cap + SUBS, LANES), f32),
            pltpu.VMEM((z_count, SUBS, LANES), f32),
            pltpu.VMEM((per_owner, z_count, LANES), f32),
            pltpu.VMEM((z_count, cap, LANES), f32),
            pltpu.VMEM((z_count, cap, LANES), f32),
            pltpu.VMEM((cap, LANES), f32),
            pltpu.VMEM((z_count, modes, SUBS, LANES), f32),
            pltpu.VMEM((modes, z_count, LANES), f32),
            pltpu.VMEM((seq_count, per_owner, z_count, LANES), f32),
            pltpu.VMEM((seq_count, per_owner, z_count, LANES), f32),
            pltpu.VMEM((owners, per_owner, z_count, LANES), f32),
            pltpu.VMEM((z_count, x_count, cap // 4, LANES), bf16),
            pltpu.VMEM((2, z_count, SUBS, LANES), f32),
            dma((2,)), dma((2,)),
            dma((owners,)), dma((seq_count,)), dma((seq_count,)), dma((owners,)),
        ]
        + [dma((x_count, z_count)), dma((seq_count,)), dma((5,)), dma],
        compiler_params=pltpu.CompilerParams(
            collective_id=0, has_side_effects=True, vmem_limit_bytes=56 << 20
        ),
        name="convolve",
    )(sizes, streams, taps, residue, damping, direct)


def select_kernel(former, updated, remaining, pieces, chosen, sequence):
    seq_count, packed_rows, _ = pieces.shape
    width = LANES // 4
    lane = lax.broadcasted_iota(jnp.int32, (packed_rows, LANES), 1)
    line = lax.broadcasted_iota(jnp.int32, (packed_rows, LANES), 0)

    def place(s, start):
        at, offset = start // 4, lax.rem(start, 4) * width
        turned = pltpu.roll(pieces[s].astype(jnp.float32), offset, 1)
        present = jnp.broadcast_to(sequence[pl.ds(at, 1), :], turned.shape)
        before = jnp.where(line == 0, present, pltpu.roll(turned, 1, 0))
        sequence[pl.ds(at, packed_rows), :] = jnp.where(lane < offset, before, turned)
        sequence[pl.ds(at + packed_rows, 1), :] = turned[packed_rows - 1 :, :]
        return start + former[s]

    lax.fori_loop(0, seq_count, place, 0)
    row = line * 4 + lane // width
    chosen[...] = jnp.zeros_like(chosen)

    def pick(k, start):
        at, offset = start // 4, lax.rem(start, 4) * width
        here = sequence[pl.ds(at, packed_rows), :]
        after = sequence[pl.ds(at + 1, packed_rows), :]
        both = jnp.where(lane < offset, after, here)
        rows = pltpu.roll(both, lax.rem(LANES - offset, LANES), 1)
        chosen[remaining[k]] = jnp.where(row < updated[k], rows, 0.0).astype(jnp.bfloat16)
        return start + updated[k]

    lax.fori_loop(0, updated.shape[0], pick, 0)


def select_call(seq_len, pieces, former, updated, remaining):
    smem = pl.BlockSpec(memory_space=pltpu.SMEM)
    vmem = pl.BlockSpec(memory_space=pltpu.VMEM)
    return pl.pallas_call(
        select_kernel,
        out_shape=jax.ShapeDtypeStruct(pieces.shape, jnp.bfloat16),
        in_specs=[smem] * 3 + [vmem],
        out_specs=vmem,
        scratch_shapes=[pltpu.VMEM((seq_len // 4 + pieces.shape[1] + 8, LANES), jnp.float32)],
        compiler_params=pltpu.CompilerParams(vmem_limit_bytes=24 << 20),
        name="reorder_rows",
    )(former, updated, remaining, pieces)


def project_kernel(
    x_count, z_count, y_count,
    chosen, block, out,
    landing, unpacked, rows_in, weights, sum_out, sum_in,
    load_sem, own_sem, piece_send, piece_recv,
    right_send, right_recv, left_send, left_recv,
    far_a_send, far_a_recv, far_b_send, far_b_recv, core_send, core_recv,
    sum_send, sum_recv,
):
    cap, width = out.shape
    part_width = width // 2
    half, quarter = cap // 2, cap // 4
    reach = z_count // 2
    my_x, my_z = x_index(), lax.axis_index("z")
    my_y, my_core = lax.axis_index("y"), lax.axis_index("core")
    right, left = lax.rem(my_y + 1, y_count), lax.rem(my_y + y_count - 1, y_count)
    opposite = lax.rem(my_y + 2, y_count)
    other = 1 - my_core
    above, below = lax.rem(my_z + 1, z_count), lax.rem(my_z + z_count - 1, z_count)

    load = pltpu.make_async_copy(block, weights, load_sem)
    load.start()
    own_copy = pltpu.make_async_copy(
        chosen.at[pl.ds(my_x * z_count, z_count)], landing.at[my_x], own_sem
    )
    own_copy.start()

    barrier = pltpu.get_barrier_semaphore()
    for k in range(1, x_count):
        pl.semaphore_signal(
            barrier, inc=1, device_id=at_x(lax.rem(my_x + k, x_count)), device_id_type=MESH
        )
    for to in ({"y": right}, {"y": left}, {"core": other}, {"z": above}, {"z": below}):
        pl.semaphore_signal(barrier, inc=1, device_id=to, device_id_type=MESH)
    pl.semaphore_wait(barrier, x_count - 1 + 5)

    def piece_copy(x, owner):
        return pltpu.make_async_remote_copy(
            src_ref=chosen.at[x * z_count + owner], dst_ref=landing.at[my_x, owner],
            send_sem=piece_send.at[x, owner], recv_sem=piece_recv.at[my_x, owner],
            device_id=at_x(x), device_id_type=MESH,
        )

    def piece_arrival(x, owner):
        return pltpu.make_async_remote_copy(
            src_ref=chosen.at[owner], dst_ref=landing.at[x, owner],
            send_sem=piece_send.at[x, owner], recv_sem=piece_recv.at[x, owner],
            device_id=at_x(x), device_id_type=MESH,
        )

    order = [reach]
    for distance in range(reach - 1, 0, -1):
        order += [distance, z_count - distance]
    order = [lax.rem(my_z + d, z_count) for d in order + [0]]
    others = [lax.rem(my_x + k, x_count) for k in (1, 3, 2)]
    for owner in order:
        for x in others:
            piece_copy(x, owner).start()

    def columns(y, core):
        return pl.ds(pl.multiple_of((y * 2 + core) * LANES, LANES), LANES)

    def onward(y, core, owner, to, send, recv, first, rows):
        view = rows_in.at[owner, pl.ds(first, rows), columns(y, core)]
        return pltpu.make_async_remote_copy(
            src_ref=view, dst_ref=view, send_sem=send, recv_sem=recv,
            device_id=to, device_id_type=MESH,
        )

    def to_right(y, o):
        return onward(y, my_core, o, {"y": right}, right_send.at[o], right_recv.at[o], 0, cap)

    def to_left(y, o):
        return onward(y, my_core, o, {"y": left}, left_send.at[o], left_recv.at[o], 0, cap)

    def far_right(y, o):
        return onward(y, my_core, o, {"y": right}, far_a_send.at[o], far_a_recv.at[o], 0, half)

    def far_left(y, o):
        return onward(y, my_core, o, {"y": left}, far_b_send.at[o], far_b_recv.at[o], half, half)

    def to_core(y, core, o):
        return onward(y, core, o, {"core": other}, core_send.at[y, o], core_recv.at[y, o], 0, cap)

    def travels(way, distance, part):
        return distance < reach or part == way

    def slot(distance, part):
        return (distance - 1) * 2 + part

    def sum_copy(way, distance, part):
        at = slot(distance, part)
        return pltpu.make_async_remote_copy(
            src_ref=sum_out.at[way, at], dst_ref=sum_in.at[way, at],
            send_sem=sum_send.at[way, at], recv_sem=sum_recv.at[way, at],
            device_id={"z": below if way else above}, device_id_type=MESH,
        )

    def partial(owner, part):
        return jnp.dot(
            rows_in[owner], weights[:, part * part_width : (part + 1) * part_width],
            preferred_element_type=jnp.float32,
        )

    def ready(owner):
        @pl.loop(0, y_count)
        def _(y):
            to_core(y, other, owner).wait_recv()

    def send_sums(distance):
        owners = [lax.rem(my_z + d, z_count) for d in (distance, z_count - distance)]
        for owner in owners[: 1 if distance == reach else 2]:
            ready(owner)
        for way, part in ((0, 1), (1, 0), (0, 0), (1, 1)):
            if travels(way, distance, part):
                total = partial(owners[way], part)
                if distance < reach and travels(way, distance + 1, part):
                    sum_copy(way, distance + 1, part).wait_recv()
                    total = total + sum_in[way, slot(distance + 1, part)].astype(jnp.float32)
                sum_out[way, slot(distance, part)] = total.astype(jnp.bfloat16)
                sum_copy(way, distance, part).start()

    own_copy.wait()

    def launch(owner):
        for x in others:
            piece_arrival(x, owner).wait_recv()
        packed = [landing[x, owner].astype(jnp.float32) for x in range(x_count)]
        for q in range(4):
            unpacked[pl.ds(q, quarter, stride=4), :] = repack(packed, q)
        rows_in[owner, :, columns(my_y, my_core)] = unpacked[...].astype(jnp.bfloat16)
        to_right(my_y, owner).start()
        to_left(my_y, owner).start()
        to_core(my_y, my_core, owner).start()

    def finish(owner):
        far_right(opposite, owner).wait_recv()
        far_left(opposite, owner).wait_recv()
        to_core(opposite, my_core, owner).start()

    ahead, lag = 2, 1
    for owner in order[:ahead]:
        launch(owner)
    load.wait()
    sent = reach + 1
    for k in range(len(order) + lag):
        if k + ahead < len(order):
            launch(order[k + ahead])
        if k < len(order):
            owner = order[k]
            to_right(left, owner).wait_recv()
            far_right(left, owner).start()
            to_core(left, my_core, owner).start()
            to_left(right, owner).wait_recv()
            far_left(right, owner).start()
            to_core(right, my_core, owner).start()
        if k >= lag:
            finish(order[k - lag])
        if k == lag or k == lag + 2 and reach > 1:
            sent -= 1
            send_sums(sent)
    for distance in range(sent - 1, 0, -1):
        send_sums(distance)

    ready(my_z)
    for part in range(2):
        total = partial(my_z, part)
        for way in range(2):
            if travels(way, 1, part):
                sum_copy(way, 1, part).wait_recv()
                total = total + sum_in[way, slot(1, part)].astype(jnp.float32)
        out[:, part * part_width : (part + 1) * part_width] = total.astype(jnp.bfloat16)

    for distance in range(1, reach + 1):
        for part in range(2):
            for way in range(2):
                if travels(way, distance, part):
                    sum_copy(way, distance, part).wait_send()
    for owner in order:
        for x in others:
            piece_copy(x, owner).wait_send()

    @pl.loop(0, z_count)
    def _(o):
        for y in range(y_count):
            to_core(y, my_core, o).wait_send()
        to_right(my_y, o).wait_send()
        to_left(my_y, o).wait_send()
        far_right(left, o).wait_send()
        far_left(right, o).wait_send()


def project_call(dims, chosen, block):
    x_count, y_count, z_count = dims["x"], dims["y"], dims["z"]
    cap = chosen.shape[1] * 4
    depth, width = block.shape
    reach = z_count // 2
    bf16 = jnp.bfloat16
    dma = pltpu.SemaphoreType.DMA
    vmem = pl.BlockSpec(memory_space=pltpu.VMEM)
    return pl.pallas_call(
        functools.partial(project_kernel, x_count, z_count, y_count),
        out_shape=jax.ShapeDtypeStruct((cap, width), bf16),
        in_specs=[vmem, pl.BlockSpec(memory_space=pltpu.HBM)],
        out_specs=vmem,
        scratch_shapes=[
            pltpu.VMEM((x_count, z_count, cap // 4, LANES), bf16),
            pltpu.VMEM((cap, LANES), jnp.float32),
            pltpu.VMEM((z_count, cap, depth), bf16),
            pltpu.VMEM((depth, width), bf16),
            pltpu.VMEM((2, 2 * reach, cap, width // 2), bf16),
            pltpu.VMEM((2, 2 * reach, cap, width // 2), bf16),
            dma, dma, dma((x_count, z_count)), dma((x_count, z_count)),
        ]
        + [dma((z_count,))] * 8
        + [dma((y_count, z_count))] * 2
        + [dma((2, 2 * reach))] * 2,
        compiler_params=pltpu.CompilerParams(
            collective_id=1, has_side_effects=True, vmem_limit_bytes=53 << 20
        ),
        name="project_rows",
    )(chosen, block)


def shards(
    dims,
    input_triple_streams,
    former_piece_sizes,
    updated_piece_sizes,
    remaining_indices,
    short_causal_filters,
    pole_coefficients,
    pole_damping,
    direct_coefficient,
    final_projector,
):
    cap = input_triple_streams.shape[0]
    seq_len = cap * 4 // 5 * dims["x"] * dims["z"]

    block = lax.all_gather(final_projector, ("x_high", "x_low"), axis=0, tiled=True)
    pieces = conv_call(
        dims,
        jnp.transpose(input_triple_streams, (1, 0, 2)),
        former_piece_sizes,
        short_causal_filters,
        pole_coefficients,
        pole_damping,
        direct_coefficient[None, :],
    )
    chosen = select_call(
        seq_len, pieces, former_piece_sizes, updated_piece_sizes, remaining_indices
    )
    return project_call(dims, chosen, block)


def solution(mesh):
    grid = (2, 2, mesh.shape["seq"] // 4, mesh.shape["chan"] // 2, 2)
    dims = {"x": 4, "z": grid[2], "y": grid[3]}
    rows, channels = SEQ, ("y", "core")
    return jax.shard_map(
        functools.partial(shards, dims),
        mesh=Mesh(mesh.devices.reshape(grid), AXES),
        in_specs=(
            P(rows, None, channels),
            P(),
            P(),
            P(),
            P(None, None, channels),
            P(None, channels),
            P(None, channels),
            P(channels),
            P(rows, channels),
        ),
        out_specs=P(rows, channels),
        check_vma=False,
    )
```

```python
import functools

import jax
import jax.numpy as jnp
from jax import lax
from jax.experimental import pallas as pl
from jax.experimental.pallas import tpu as pltpu
from jax.sharding import Mesh
from jax.sharding import PartitionSpec as P

MESH = pl.DeviceIdType.MESH
LANES = 128
SUBS = 8
AXES = ("x_high", "x_low", "z", "y", "core")
SEQ = ("x_high", "x_low", "z")


def x_index():
    return lax.axis_index("x_high") * 2 + lax.axis_index("x_low")


def at_x(x):
    return {"x_high": x // 2, "x_low": lax.rem(x, 2)}


def repack(quarters, k):
    group = lax.broadcasted_iota(jnp.int32, quarters[0].shape, 1) // (LANES // 4)
    result = jnp.zeros_like(quarters[0])
    for q in range(4):
        turned = pltpu.roll(quarters[q], ((q - k) % 4) * (LANES // 4), 1)
        result = jnp.where(group == q, turned, result)
    return result


def shift_down(value, by):
    row = lax.broadcasted_iota(jnp.int32, value.shape, 0)
    return jnp.where(row >= by, pltpu.roll(value, by, 0), 0.0)


def tree_sum(terms):
    while len(terms) > 1:
        terms = [a + b for a, b in zip(terms[::2], terms[1::2], strict=True)]
    return terms[0]


def conv_kernel(
    x_count, z_count,
    sizes, streams_far, taps_far, residue_far, damping_far, direct_far,
    gathered,
    streams, taps, residue, damping, direct, padded, tail, rates_own, query, gated, mixed, partial, ends, end_in, carry_out, carry_in, hidden, halo,
    halo_send, halo_recv, end_send, end_recv, carry_send, carry_recv,
    piece_send, piece_recv, load_sem, local_sem,
):
    modes = residue.shape[0]
    cap = streams.shape[1]
    groups = z_count
    step_rows = cap // SUBS
    seq_count = x_count * z_count
    per_owner = max(1, modes // seq_count)
    owners = modes // per_owner
    my_x, my_z, my_core = x_index(), lax.axis_index("z"), lax.axis_index("core")
    me = my_x * z_count + my_z
    valid = sizes[me]

    def seq_device(index):
        return {**at_x(index // z_count), "z": lax.rem(index, z_count)}

    source_core = my_z // (z_count // 2)

    @pl.when(source_core != lax.axis_index("core"))
    def _():
        @pl.loop(0, seq_count)
        def _(k):
            pl.semaphore_signal(
                pltpu.get_barrier_semaphore(), inc=1,
                device_id={**seq_device(lax.rem(me + k, seq_count)), "core": source_core},
                device_id_type=MESH,
            )

    loads = [
        pltpu.make_async_copy(far, near, load_sem.at[i])
        for i, (far, near) in enumerate((
            (streams_far, streams), (taps_far, taps), (residue_far, residue),
            (damping_far, damping), (direct_far, direct),
        ))
    ]
    for load in loads:
        load.start()

    def lanes(g):
        return pl.ds(pl.multiple_of(g * LANES, LANES), LANES)

    barrier = pltpu.get_barrier_semaphore()

    @pl.loop(1, seq_count)
    def _(k):
        pl.semaphore_signal(
            barrier, inc=1, device_id=seq_device(lax.rem(me + k, seq_count)), device_id_type=MESH
        )

    for load in loads:
        load.wait()
    last = SUBS - 1 + valid
    second = jnp.maximum(last - 1, SUBS)

    @pl.loop(0, groups)
    def _(g):
        for p in range(3):
            padded[p, g, SUBS : SUBS + cap, :] = streams[p, :, lanes(g)].astype(jnp.float32)
            tail[g, p : p + 1, :] = padded[p, g, pl.ds(last, 1), :]
            tail[g, 3 + p : 4 + p, :] = padded[p, g, pl.ds(second, 1), :]
        tail[g, 6:8, :] = jnp.zeros((2, LANES), jnp.float32)

    pl.semaphore_wait(barrier, seq_count - 1 + seq_count // 2)

    def halo_copy(distance):
        target = lax.rem(me + distance, seq_count)
        return pltpu.make_async_remote_copy(
            src_ref=tail, dst_ref=halo.at[distance - 1], send_sem=halo_send.at[distance - 1],
            recv_sem=halo_recv.at[distance - 1], device_id=seq_device(target), device_id_type=MESH,
        )

    for distance in (1, 2):
        halo_copy(distance).start()
    for distance in (1, 2):
        halo_copy(distance).wait_recv()

    row = lax.broadcasted_iota(jnp.int32, (cap, LANES), 0)
    before_size = sizes[lax.rem(me + seq_count - 1, seq_count)]

    def feature(p, g):
        at = lanes(g)
        last_one = jnp.where(me >= 1, halo[0, g, p : p + 1, :], 0.0)
        own_second = halo[0, g, 3 + p : 4 + p, :]
        far_last = jnp.where(me >= 2, halo[1, g, p : p + 1, :], 0.0)
        last_two = jnp.where(me >= 1, jnp.where(before_size >= 2, own_second, far_last), 0.0)
        padded[p, g, 6:7, :] = last_two
        padded[p, g, 7:8, :] = last_one
        return (
            taps[p, 0:1, at] * padded[p, g, 8 : 8 + cap, :]
            + taps[p, 1:2, at] * padded[p, g, 7 : 7 + cap, :]
            + taps[p, 2:3, at] * padded[p, g, 6 : 6 + cap, :]
        )

    @pl.loop(0, groups)
    def _(g):
        product = (feature(1, g) * feature(2, g)).astype(jnp.bfloat16).astype(jnp.float32)
        gated[g] = jnp.where(row < valid, product, 0.0)

    def mode_rows(ref, at):
        return [jnp.broadcast_to(ref[m : m + 1, at], (SUBS, LANES)) for m in range(modes)]

    @pl.loop(0, groups)
    def _(g):
        at = lanes(g)
        decay = [jnp.exp(-d) for d in mode_rows(damping, at)]
        weight = mode_rows(residue, at)

        def step(i, states):
            u = gated[g, pl.ds(i, SUBS, stride=step_rows), :]
            return tuple(a * h + r * u for a, h, r in zip(decay, states, weight, strict=True))

        zero = jnp.zeros((SUBS, LANES), jnp.float32)
        states = lax.fori_loop(0, step_rows, step, (zero,) * modes, unroll=4)
        left_over = (cap - valid).astype(jnp.float32)
        for m in range(modes):
            rate = damping[m : m + 1, at]
            total = states[m]
            for by in (1, 2, 4):
                total = total + jnp.exp(-rate * (step_rows * by)) * shift_down(total, by)
            partial[g, m] = shift_down(total, 1)
            ends[m, pl.ds(g, 1), :] = total[SUBS - 1 : SUBS, :] * jnp.exp(rate * left_over)

    def end_copy(owner):
        return pltpu.make_async_remote_copy(
            src_ref=ends.at[pl.ds(owner * per_owner, per_owner)], dst_ref=end_in.at[me],
            send_sem=end_send.at[owner], recv_sem=end_recv.at[me],
            device_id=seq_device(owner), device_id_type=MESH,
        )

    def end_arrival(source):
        return pltpu.make_async_remote_copy(
            src_ref=ends.at[pl.ds(0, per_owner)], dst_ref=end_in.at[source],
            send_sem=end_send.at[0], recv_sem=end_recv.at[source],
            device_id=seq_device(source), device_id_type=MESH,
        )

    def carry_copy(target):
        return pltpu.make_async_remote_copy(
            src_ref=carry_out.at[target], dst_ref=carry_in.at[me],
            send_sem=carry_send.at[target], recv_sem=carry_recv.at[me],
            device_id=seq_device(target), device_id_type=MESH,
        )

    def carry_arrival(owner):
        return pltpu.make_async_remote_copy(
            src_ref=carry_out.at[0], dst_ref=carry_in.at[owner],
            send_sem=carry_send.at[0], recv_sem=carry_recv.at[owner],
            device_id=seq_device(owner), device_id_type=MESH,
        )

    @pl.loop(0, owners)
    def _(k):
        owner = lax.rem(me + k, owners)

        @pl.when(owner != me)
        def _():
            end_copy(owner).start()

    @pl.when(me < owners)
    def _():
        end_in[me] = ends[pl.ds(me * per_owner, per_owner)]
        mode = lax.broadcasted_iota(jnp.int32, (modes, LANES), 0)
        for j in range(per_owner):
            for g in range(groups):
                block = damping[:, g * LANES : (g + 1) * LANES]
                rates_own[j, g : g + 1, :] = jnp.sum(
                    jnp.where(mode == me * per_owner + j, block, 0.0), axis=0, keepdims=True
                )

        @pl.loop(0, seq_count)
        def _(source):
            @pl.when(source != me)
            def _():
                end_arrival(source).wait_recv()

        rate = rates_own[...]

        def advance(source, carry):
            carry_out[source] = carry
            return jnp.exp(-rate * sizes[source].astype(jnp.float32)) * carry + end_in[source]

        lax.fori_loop(0, seq_count, advance, jnp.zeros_like(rate), unroll=8)
        carry_in[me] = carry_out[me]

        @pl.loop(0, seq_count)
        def _(target):
            @pl.when(target != me)
            def _():
                carry_copy(target).start()

    @pl.loop(0, groups)
    def _(g):
        query[g] = feature(0, g).astype(jnp.bfloat16).astype(jnp.float32)

    @pl.loop(0, owners)
    def _(owner):
        @pl.when(owner != me)
        def _():
            carry_arrival(owner).wait_recv()

    def goes_to(g):
        return my_core * (z_count // 2) + g // 2, lax.rem(g, 2)

    def is_me(x, g):
        z, core = goes_to(g)
        return jnp.logical_and(jnp.logical_and(x == my_x, z == my_z), core == my_core)

    def piece_copy(x, g):
        z, core = goes_to(g)
        return pltpu.make_async_remote_copy(
            src_ref=hidden.at[g, x], dst_ref=gathered.at[me], send_sem=piece_send.at[x, g],
            recv_sem=piece_recv.at[me], device_id={**at_x(x), "z": z, "core": core},
            device_id_type=MESH,
        )

    def piece_arrival(source):
        return pltpu.make_async_remote_copy(
            src_ref=hidden.at[0, 0], dst_ref=gathered.at[source], send_sem=piece_send.at[0, 0],
            recv_sem=piece_recv.at[source],
            device_id={**seq_device(source), "core": source_core}, device_id_type=MESH,
        )

    own_group = lax.rem(my_z, z_count // 2) * 2 + my_core
    own_copy = pltpu.make_async_copy(hidden.at[own_group, my_x], gathered.at[me], local_sem)
    quarter = cap // 4

    @pl.loop(0, groups)
    def _(k):
        g = lax.rem(my_z + 1 + k, groups)
        at = lanes(g)
        rates = mode_rows(damping, at)
        decay = [jnp.exp(-d) for d in rates]
        weight = mode_rows(residue, at)
        sub = lax.broadcasted_iota(jnp.int32, (SUBS, LANES), 0).astype(jnp.float32) * step_rows
        start = tuple(
            partial[g, m]
            + jnp.exp(-rates[m] * sub)
            * carry_in[m // per_owner, m % per_owner, pl.ds(g, 1), :]
            for m in range(modes)
        )

        def step(i, states):
            rows = pl.ds(i, SUBS, stride=step_rows)
            u = gated[g, rows, :]
            states = tuple(a * h + r * u for a, h, r in zip(decay, states, weight, strict=True))
            mixed[rows, :] = tree_sum(list(states))
            return states

        lax.fori_loop(0, step_rows, step, start, unroll=4)
        conv = mixed[...] + direct[0:1, at] * gated[g]
        mixed[...] = query[g] * conv
        quarters = [mixed[pl.ds(q, quarter, stride=4), :] for q in range(4)]
        for x in range(x_count):
            hidden[g, x] = repack(quarters, x).astype(jnp.bfloat16)

            @pl.when(jnp.logical_not(is_me(x, g)))
            def _():
                piece_copy(x, g).start()

            @pl.when(is_me(x, g))
            def _():
                own_copy.start()

    from_self = source_core == my_core

    @pl.when(from_self)
    def _():
        own_copy.wait()

    @pl.loop(0, seq_count)
    def _(other):
        @pl.when(jnp.logical_not(jnp.logical_and(from_self, other == me)))
        def _():
            piece_arrival(other).wait_recv()

        x, g = other // z_count, lax.rem(other, z_count)

        @pl.when(jnp.logical_not(is_me(x, g)))
        def _():
            piece_copy(x, g).wait_send()

    for distance in (1, 2):
        halo_copy(distance).wait_send()

    @pl.loop(0, owners)
    def _(owner):
        @pl.when(owner != me)
        def _():
            end_copy(owner).wait_send()

    @pl.when(me < owners)
    def _():
        @pl.loop(0, seq_count)
        def _(target):
            @pl.when(target != me)
            def _():
                carry_copy(target).wait_send()


def conv_call(dims, streams, sizes, taps, residue, damping, direct):
    x_count, z_count = dims["x"], dims["z"]
    cap, width = streams.shape[1:]
    modes = residue.shape[0]
    seq_count = x_count * z_count
    per_owner = max(1, modes // seq_count)
    owners = modes // per_owner
    f32, bf16 = jnp.float32, jnp.bfloat16
    dma = pltpu.SemaphoreType.DMA
    vmem = pl.BlockSpec(memory_space=pltpu.VMEM)
    far = pl.BlockSpec(memory_space=pltpu.HBM)
    return pl.pallas_call(
        functools.partial(conv_kernel, x_count, z_count),
        out_shape=jax.ShapeDtypeStruct((seq_count, cap // 4, LANES), bf16),
        in_specs=[pl.BlockSpec(memory_space=pltpu.SMEM)] + [far] * 5,
        out_specs=pl.BlockSpec(memory_space=pl.ANY),
        scratch_shapes=[
            pltpu.VMEM(streams.shape, bf16),
            pltpu.VMEM(taps.shape, f32),
            pltpu.VMEM(residue.shape, f32),
            pltpu.VMEM(damping.shape, f32),
            pltpu.VMEM(direct.shape, f32),
            pltpu.VMEM((3, z_count, cap + SUBS, LANES), f32),
            pltpu.VMEM((z_count, SUBS, LANES), f32),
            pltpu.VMEM((per_owner, z_count, LANES), f32),
            pltpu.VMEM((z_count, cap, LANES), f32),
            pltpu.VMEM((z_count, cap, LANES), f32),
            pltpu.VMEM((cap, LANES), f32),
            pltpu.VMEM((z_count, modes, SUBS, LANES), f32),
            pltpu.VMEM((modes, z_count, LANES), f32),
            pltpu.VMEM((seq_count, per_owner, z_count, LANES), f32),
            pltpu.VMEM((seq_count, per_owner, z_count, LANES), f32),
            pltpu.VMEM((owners, per_owner, z_count, LANES), f32),
            pltpu.VMEM((z_count, x_count, cap // 4, LANES), bf16),
            pltpu.VMEM((2, z_count, SUBS, LANES), f32),
            dma((2,)), dma((2,)),
            dma((owners,)), dma((seq_count,)), dma((seq_count,)), dma((owners,)),
        ]
        + [dma((x_count, z_count)), dma((seq_count,)), dma((5,)), dma],
        compiler_params=pltpu.CompilerParams(
            collective_id=0, has_side_effects=True, vmem_limit_bytes=56 << 20
        ),
        name="convolve",
    )(sizes, streams, taps, residue, damping, direct)


def select_kernel(former, updated, remaining, pieces, chosen, sequence):
    seq_count, packed_rows, _ = pieces.shape
    width = LANES // 4
    lane = lax.broadcasted_iota(jnp.int32, (packed_rows, LANES), 1)
    line = lax.broadcasted_iota(jnp.int32, (packed_rows, LANES), 0)

    def place(s, start):
        at, offset = start // 4, lax.rem(start, 4) * width
        turned = pltpu.roll(pieces[s].astype(jnp.float32), offset, 1)
        present = jnp.broadcast_to(sequence[pl.ds(at, 1), :], turned.shape)
        before = jnp.where(line == 0, present, pltpu.roll(turned, 1, 0))
        sequence[pl.ds(at, packed_rows), :] = jnp.where(lane < offset, before, turned)
        sequence[pl.ds(at + packed_rows, 1), :] = turned[packed_rows - 1 :, :]
        return start + former[s]

    lax.fori_loop(0, seq_count, place, 0, unroll=8)
    row = line * 4 + lane // width
    chosen[...] = jnp.zeros_like(chosen)

    def pick(k, start):
        at, offset = start // 4, lax.rem(start, 4) * width
        here = sequence[pl.ds(at, packed_rows), :]
        after = sequence[pl.ds(at + 1, packed_rows), :]
        both = jnp.where(lane < offset, after, here)
        rows = pltpu.roll(both, lax.rem(LANES - offset, LANES), 1)
        chosen[remaining[k]] = jnp.where(row < updated[k], rows, 0.0).astype(jnp.bfloat16)
        return start + updated[k]

    lax.fori_loop(0, updated.shape[0], pick, 0, unroll=7)


def select_call(seq_len, pieces, former, updated, remaining):
    smem = pl.BlockSpec(memory_space=pltpu.SMEM)
    vmem = pl.BlockSpec(memory_space=pltpu.VMEM)
    return pl.pallas_call(
        select_kernel,
        out_shape=jax.ShapeDtypeStruct(pieces.shape, jnp.bfloat16),
        in_specs=[smem] * 3 + [vmem],
        out_specs=vmem,
        scratch_shapes=[pltpu.VMEM((seq_len // 4 + pieces.shape[1] + 8, LANES), jnp.float32)],
        compiler_params=pltpu.CompilerParams(vmem_limit_bytes=24 << 20),
        name="reorder_rows",
    )(former, updated, remaining, pieces)


def project_kernel(
    x_count, z_count, y_count,
    chosen, block, out,
    landing, unpacked, rows_in, weights, sum_out, sum_in,
    load_sem, own_sem, piece_send, piece_recv,
    right_send, right_recv, left_send, left_recv,
    far_a_send, far_a_recv, far_b_send, far_b_recv, core_send, core_recv,
    sum_send, sum_recv,
):
    cap, width = out.shape
    part_width = width // 2
    half, quarter = cap // 2, cap // 4
    reach = z_count // 2
    my_x, my_z = x_index(), lax.axis_index("z")
    my_y, my_core = lax.axis_index("y"), lax.axis_index("core")
    right, left = lax.rem(my_y + 1, y_count), lax.rem(my_y + y_count - 1, y_count)
    opposite = lax.rem(my_y + 2, y_count)
    other = 1 - my_core
    above, below = lax.rem(my_z + 1, z_count), lax.rem(my_z + z_count - 1, z_count)

    load = pltpu.make_async_copy(block, weights, load_sem)
    load.start()
    own_copy = pltpu.make_async_copy(
        chosen.at[pl.ds(my_x * z_count, z_count)], landing.at[my_x], own_sem
    )
    own_copy.start()

    barrier = pltpu.get_barrier_semaphore()
    for k in range(1, x_count):
        pl.semaphore_signal(
            barrier, inc=1, device_id=at_x(lax.rem(my_x + k, x_count)), device_id_type=MESH
        )
    for to in ({"y": right}, {"y": left}, {"core": other}, {"z": above}, {"z": below}):
        pl.semaphore_signal(barrier, inc=1, device_id=to, device_id_type=MESH)
    pl.semaphore_wait(barrier, x_count - 1 + 5)

    def piece_copy(x, owner):
        return pltpu.make_async_remote_copy(
            src_ref=chosen.at[x * z_count + owner], dst_ref=landing.at[my_x, owner],
            send_sem=piece_send.at[x, owner], recv_sem=piece_recv.at[my_x, owner],
            device_id=at_x(x), device_id_type=MESH,
        )

    def piece_arrival(x, owner):
        return pltpu.make_async_remote_copy(
            src_ref=chosen.at[owner], dst_ref=landing.at[x, owner],
            send_sem=piece_send.at[x, owner], recv_sem=piece_recv.at[x, owner],
            device_id=at_x(x), device_id_type=MESH,
        )

    order = [reach]
    for distance in range(reach - 1, 0, -1):
        order += [distance, z_count - distance]
    order = [lax.rem(my_z + d, z_count) for d in order + [0]]
    others = [lax.rem(my_x + k, x_count) for k in (1, 3, 2)]
    for owner in order:
        for x in others:
            piece_copy(x, owner).start()

    def columns(y, core):
        return pl.ds(pl.multiple_of((y * 2 + core) * LANES, LANES), LANES)

    def onward(y, core, owner, to, send, recv, first, rows):
        view = rows_in.at[owner, pl.ds(first, rows), columns(y, core)]
        return pltpu.make_async_remote_copy(
            src_ref=view, dst_ref=view, send_sem=send, recv_sem=recv,
            device_id=to, device_id_type=MESH,
        )

    def to_right(y, o):
        return onward(y, my_core, o, {"y": right}, right_send.at[o], right_recv.at[o], 0, cap)

    def to_left(y, o):
        return onward(y, my_core, o, {"y": left}, left_send.at[o], left_recv.at[o], 0, cap)

    def far_right(y, o):
        return onward(y, my_core, o, {"y": right}, far_a_send.at[o], far_a_recv.at[o], 0, half)

    def far_left(y, o):
        return onward(y, my_core, o, {"y": left}, far_b_send.at[o], far_b_recv.at[o], half, half)

    def to_core(y, core, o):
        return onward(y, core, o, {"core": other}, core_send.at[y, o], core_recv.at[y, o], 0, cap)

    def travels(way, distance, part):
        return distance < reach or part == way

    def slot(distance, part):
        return (distance - 1) * 2 + part

    def sum_copy(way, distance, part):
        at = slot(distance, part)
        return pltpu.make_async_remote_copy(
            src_ref=sum_out.at[way, at], dst_ref=sum_in.at[way, at],
            send_sem=sum_send.at[way, at], recv_sem=sum_recv.at[way, at],
            device_id={"z": below if way else above}, device_id_type=MESH,
        )

    def partial(owner, part):
        return jnp.dot(
            rows_in[owner], weights[:, part * part_width : (part + 1) * part_width],
            preferred_element_type=jnp.float32,
        )

    def ready(owner):
        @pl.loop(0, y_count)
        def _(y):
            to_core(y, other, owner).wait_recv()

    def send_sums(distance):
        owners = [lax.rem(my_z + d, z_count) for d in (distance, z_count - distance)]
        for owner in owners[: 1 if distance == reach else 2]:
            ready(owner)
        for way, part in ((0, 1), (1, 0), (0, 0), (1, 1)):
            if travels(way, distance, part):
                total = partial(owners[way], part)
                if distance < reach and travels(way, distance + 1, part):
                    sum_copy(way, distance + 1, part).wait_recv()
                    total = total + sum_in[way, slot(distance + 1, part)].astype(jnp.float32)
                sum_out[way, slot(distance, part)] = total.astype(jnp.bfloat16)
                sum_copy(way, distance, part).start()

    own_copy.wait()

    def launch(owner):
        for x in others:
            piece_arrival(x, owner).wait_recv()
        packed = [landing[x, owner].astype(jnp.float32) for x in range(x_count)]
        for q in range(4):
            unpacked[pl.ds(q, quarter, stride=4), :] = repack(packed, q)
        rows_in[owner, :, columns(my_y, my_core)] = unpacked[...].astype(jnp.bfloat16)
        to_right(my_y, owner).start()
        to_left(my_y, owner).start()
        to_core(my_y, my_core, owner).start()

    def finish(owner):
        far_right(opposite, owner).wait_recv()
        far_left(opposite, owner).wait_recv()
        to_core(opposite, my_core, owner).start()

    ahead, lag = 2, 1
    for owner in order[:ahead]:
        launch(owner)
    load.wait()
    sent = reach + 1
    for k in range(len(order) + lag):
        if k + ahead < len(order):
            launch(order[k + ahead])
        if k < len(order):
            owner = order[k]
            to_right(left, owner).wait_recv()
            far_right(left, owner).start()
            to_core(left, my_core, owner).start()
            to_left(right, owner).wait_recv()
            far_left(right, owner).start()
            to_core(right, my_core, owner).start()
        if k >= lag:
            finish(order[k - lag])
        if k == lag or k in (lag + 2, lag + 4) and reach > 1:
            sent -= 1
            send_sums(sent)
    for distance in range(sent - 1, 0, -1):
        send_sums(distance)

    ready(my_z)
    for part in range(2):
        total = partial(my_z, part)
        for way in range(2):
            if travels(way, 1, part):
                sum_copy(way, 1, part).wait_recv()
                total = total + sum_in[way, slot(1, part)].astype(jnp.float32)
        out[:, part * part_width : (part + 1) * part_width] = total.astype(jnp.bfloat16)

    for distance in range(1, reach + 1):
        for part in range(2):
            for way in range(2):
                if travels(way, distance, part):
                    sum_copy(way, distance, part).wait_send()
    for owner in order:
        for x in others:
            piece_copy(x, owner).wait_send()

    @pl.loop(0, z_count)
    def _(o):
        for y in range(y_count):
            to_core(y, my_core, o).wait_send()
        to_right(my_y, o).wait_send()
        to_left(my_y, o).wait_send()
        far_right(left, o).wait_send()
        far_left(right, o).wait_send()


def project_call(dims, chosen, block):
    x_count, y_count, z_count = dims["x"], dims["y"], dims["z"]
    cap = chosen.shape[1] * 4
    depth, width = block.shape
    reach = z_count // 2
    bf16 = jnp.bfloat16
    dma = pltpu.SemaphoreType.DMA
    vmem = pl.BlockSpec(memory_space=pltpu.VMEM)
    return pl.pallas_call(
        functools.partial(project_kernel, x_count, z_count, y_count),
        out_shape=jax.ShapeDtypeStruct((cap, width), bf16),
        in_specs=[vmem, pl.BlockSpec(memory_space=pltpu.HBM)],
        out_specs=vmem,
        scratch_shapes=[
            pltpu.VMEM((x_count, z_count, cap // 4, LANES), bf16),
            pltpu.VMEM((cap, LANES), jnp.float32),
            pltpu.VMEM((z_count, cap, depth), bf16),
            pltpu.VMEM((depth, width), bf16),
            pltpu.VMEM((2, 2 * reach, cap, width // 2), bf16),
            pltpu.VMEM((2, 2 * reach, cap, width // 2), bf16),
            dma, dma, dma((x_count, z_count)), dma((x_count, z_count)),
        ]
        + [dma((z_count,))] * 8
        + [dma((y_count, z_count))] * 2
        + [dma((2, 2 * reach))] * 2,
        compiler_params=pltpu.CompilerParams(
            collective_id=1, has_side_effects=True, vmem_limit_bytes=53 << 20
        ),
        name="project_rows",
    )(chosen, block)


def shards(
    dims,
    input_triple_streams,
    former_piece_sizes,
    updated_piece_sizes,
    remaining_indices,
    short_causal_filters,
    pole_coefficients,
    pole_damping,
    direct_coefficient,
    final_projector,
):
    cap = input_triple_streams.shape[0]
    seq_len = cap * 4 // 5 * dims["x"] * dims["z"]

    block = lax.all_gather(final_projector, ("x_high", "x_low"), axis=0, tiled=True)
    pieces = conv_call(
        dims,
        jnp.transpose(input_triple_streams, (1, 0, 2)),
        former_piece_sizes,
        short_causal_filters,
        pole_coefficients,
        pole_damping,
        direct_coefficient[None, :],
    )
    chosen = select_call(
        seq_len, pieces, former_piece_sizes, updated_piece_sizes, remaining_indices
    )
    return project_call(dims, chosen, block)


def solution(mesh):
    grid = (2, 2, mesh.shape["seq"] // 4, mesh.shape["chan"] // 2, 2)
    dims = {"x": 4, "z": grid[2], "y": grid[3]}
    rows, channels = SEQ, ("y", "core")
    return jax.shard_map(
        functools.partial(shards, dims),
        mesh=Mesh(mesh.devices.reshape(grid), AXES),
        in_specs=(
            P(rows, None, channels),
            P(),
            P(),
            P(),
            P(None, None, channels),
            P(None, channels),
            P(None, channels),
            P(channels),
            P(rows, channels),
        ),
        out_specs=P(rows, channels),
        check_vma=False,
    )
```

```python
import functools

import jax
import jax.numpy as jnp
from jax import lax
from jax.experimental import pallas as pl
from jax.experimental.pallas import tpu as pltpu
from jax.sharding import Mesh
from jax.sharding import PartitionSpec as P

MESH = pl.DeviceIdType.MESH
LANES = 128
SUBS = 8
AXES = ("x_high", "x_low", "z", "y", "core")
SEQ = ("x_high", "x_low", "z")


def x_index():
    return lax.axis_index("x_high") * 2 + lax.axis_index("x_low")


def at_x(x):
    return {"x_high": x // 2, "x_low": lax.rem(x, 2)}


def repack(quarters, k):
    group = lax.broadcasted_iota(jnp.int32, quarters[0].shape, 1) // (LANES // 4)
    result = jnp.zeros_like(quarters[0])
    for q in range(4):
        turned = pltpu.roll(quarters[q], ((q - k) % 4) * (LANES // 4), 1)
        result = jnp.where(group == q, turned, result)
    return result


def shift_down(value, by):
    row = lax.broadcasted_iota(jnp.int32, value.shape, 0)
    return jnp.where(row >= by, pltpu.roll(value, by, 0), 0.0)


def tree_sum(terms):
    while len(terms) > 1:
        terms = [a + b for a, b in zip(terms[::2], terms[1::2], strict=True)]
    return terms[0]


def conv_kernel(
    x_count, z_count,
    sizes, streams_far, taps_far, residue_far, damping_far, direct_far,
    gathered,
    streams, taps, residue, damping, direct, padded, tail, rates_own, query, gated, mixed, partial, ends, end_in, carry_out, carry_in, hidden, halo,
    halo_send, halo_recv, end_send, end_recv, carry_send, carry_recv,
    piece_send, piece_recv, load_sem, local_sem,
):
    modes = residue.shape[0]
    cap = streams.shape[1]
    groups = z_count
    step_rows = cap // SUBS
    seq_count = x_count * z_count
    per_owner = max(1, modes // seq_count)
    owners = modes // per_owner
    my_x, my_z, my_core = x_index(), lax.axis_index("z"), lax.axis_index("core")
    me = my_x * z_count + my_z
    valid = sizes[me]

    def seq_device(index):
        return {**at_x(index // z_count), "z": lax.rem(index, z_count)}

    source_core = my_z // (z_count // 2)

    @pl.when(source_core != lax.axis_index("core"))
    def _():
        @pl.loop(0, seq_count)
        def _(k):
            pl.semaphore_signal(
                pltpu.get_barrier_semaphore(), inc=1,
                device_id={**seq_device(lax.rem(me + k, seq_count)), "core": source_core},
                device_id_type=MESH,
            )

    loads = [
        pltpu.make_async_copy(far, near, load_sem.at[i])
        for i, (far, near) in enumerate((
            (streams_far, streams), (taps_far, taps), (residue_far, residue),
            (damping_far, damping), (direct_far, direct),
        ))
    ]
    for load in loads:
        load.start()

    def lanes(g):
        return pl.ds(pl.multiple_of(g * LANES, LANES), LANES)

    barrier = pltpu.get_barrier_semaphore()

    @pl.loop(1, seq_count)
    def _(k):
        pl.semaphore_signal(
            barrier, inc=1, device_id=seq_device(lax.rem(me + k, seq_count)), device_id_type=MESH
        )

    for load in loads:
        load.wait()
    last = SUBS - 1 + valid
    second = jnp.maximum(last - 1, SUBS)

    @pl.loop(0, groups)
    def _(g):
        for p in range(3):
            padded[p, g, SUBS : SUBS + cap, :] = streams[p, :, lanes(g)].astype(jnp.float32)
            tail[g, p : p + 1, :] = padded[p, g, pl.ds(last, 1), :]
            tail[g, 3 + p : 4 + p, :] = padded[p, g, pl.ds(second, 1), :]
        tail[g, 6:8, :] = jnp.zeros((2, LANES), jnp.float32)

    pl.semaphore_wait(barrier, seq_count - 1 + seq_count // 2)

    def halo_copy(distance):
        target = lax.rem(me + distance, seq_count)
        return pltpu.make_async_remote_copy(
            src_ref=tail, dst_ref=halo.at[distance - 1], send_sem=halo_send.at[distance - 1],
            recv_sem=halo_recv.at[distance - 1], device_id=seq_device(target), device_id_type=MESH,
        )

    for distance in (1, 2):
        halo_copy(distance).start()
    for distance in (1, 2):
        halo_copy(distance).wait_recv()

    row = lax.broadcasted_iota(jnp.int32, (cap, LANES), 0)
    before_size = sizes[lax.rem(me + seq_count - 1, seq_count)]

    def feature(p, g):
        at = lanes(g)
        last_one = jnp.where(me >= 1, halo[0, g, p : p + 1, :], 0.0)
        own_second = halo[0, g, 3 + p : 4 + p, :]
        far_last = jnp.where(me >= 2, halo[1, g, p : p + 1, :], 0.0)
        last_two = jnp.where(me >= 1, jnp.where(before_size >= 2, own_second, far_last), 0.0)
        padded[p, g, 6:7, :] = last_two
        padded[p, g, 7:8, :] = last_one
        return (
            taps[p, 0:1, at] * padded[p, g, 8 : 8 + cap, :]
            + taps[p, 1:2, at] * padded[p, g, 7 : 7 + cap, :]
            + taps[p, 2:3, at] * padded[p, g, 6 : 6 + cap, :]
        )

    @pl.loop(0, groups)
    def _(g):
        product = (feature(1, g) * feature(2, g)).astype(jnp.bfloat16).astype(jnp.float32)
        gated[g] = jnp.where(row < valid, product, 0.0)

    def mode_rows(ref, at):
        return [jnp.broadcast_to(ref[m : m + 1, at], (SUBS, LANES)) for m in range(modes)]

    @pl.loop(0, groups)
    def _(g):
        at = lanes(g)
        decay = [jnp.exp(-d) for d in mode_rows(damping, at)]
        weight = mode_rows(residue, at)

        def step(i, states):
            u = gated[g, pl.ds(i, SUBS, stride=step_rows), :]
            return tuple(a * h + r * u for a, h, r in zip(decay, states, weight, strict=True))

        zero = jnp.zeros((SUBS, LANES), jnp.float32)
        states = lax.fori_loop(0, step_rows, step, (zero,) * modes, unroll=4)
        left_over = (cap - valid).astype(jnp.float32)
        for m in range(modes):
            rate = damping[m : m + 1, at]
            total = states[m]
            for by in (1, 2, 4):
                total = total + jnp.exp(-rate * (step_rows * by)) * shift_down(total, by)
            partial[g, m] = shift_down(total, 1)
            ends[m, pl.ds(g, 1), :] = total[SUBS - 1 : SUBS, :] * jnp.exp(rate * left_over)

    def end_copy(owner):
        return pltpu.make_async_remote_copy(
            src_ref=ends.at[pl.ds(owner * per_owner, per_owner)], dst_ref=end_in.at[me],
            send_sem=end_send.at[owner], recv_sem=end_recv.at[me],
            device_id=seq_device(owner), device_id_type=MESH,
        )

    def end_arrival(source):
        return pltpu.make_async_remote_copy(
            src_ref=ends.at[pl.ds(0, per_owner)], dst_ref=end_in.at[source],
            send_sem=end_send.at[0], recv_sem=end_recv.at[source],
            device_id=seq_device(source), device_id_type=MESH,
        )

    def carry_copy(target):
        return pltpu.make_async_remote_copy(
            src_ref=carry_out.at[target], dst_ref=carry_in.at[me],
            send_sem=carry_send.at[target], recv_sem=carry_recv.at[me],
            device_id=seq_device(target), device_id_type=MESH,
        )

    def carry_arrival(owner):
        return pltpu.make_async_remote_copy(
            src_ref=carry_out.at[0], dst_ref=carry_in.at[owner],
            send_sem=carry_send.at[0], recv_sem=carry_recv.at[owner],
            device_id=seq_device(owner), device_id_type=MESH,
        )

    @pl.loop(0, owners)
    def _(k):
        owner = lax.rem(me + k, owners)

        @pl.when(owner != me)
        def _():
            end_copy(owner).start()

    @pl.when(me < owners)
    def _():
        end_in[me] = ends[pl.ds(me * per_owner, per_owner)]
        mode = lax.broadcasted_iota(jnp.int32, (modes, LANES), 0)
        for j in range(per_owner):
            for g in range(groups):
                block = damping[:, g * LANES : (g + 1) * LANES]
                rates_own[j, g : g + 1, :] = jnp.sum(
                    jnp.where(mode == me * per_owner + j, block, 0.0), axis=0, keepdims=True
                )

        @pl.loop(0, seq_count)
        def _(source):
            @pl.when(source != me)
            def _():
                end_arrival(source).wait_recv()

        rate = rates_own[...]

        def advance(source, carry):
            carry_out[source] = carry
            return jnp.exp(-rate * sizes[source].astype(jnp.float32)) * carry + end_in[source]

        lax.fori_loop(0, seq_count, advance, jnp.zeros_like(rate), unroll=8)
        carry_in[me] = carry_out[me]

        @pl.loop(0, seq_count)
        def _(target):
            @pl.when(target != me)
            def _():
                carry_copy(target).start()

    @pl.loop(0, groups)
    def _(g):
        query[g] = feature(0, g).astype(jnp.bfloat16).astype(jnp.float32)

    @pl.loop(0, owners)
    def _(owner):
        @pl.when(owner != me)
        def _():
            carry_arrival(owner).wait_recv()

    def goes_to(g):
        return my_core * (z_count // 2) + g // 2, lax.rem(g, 2)

    def is_me(x, g):
        z, core = goes_to(g)
        return jnp.logical_and(jnp.logical_and(x == my_x, z == my_z), core == my_core)

    def piece_copy(x, g):
        z, core = goes_to(g)
        return pltpu.make_async_remote_copy(
            src_ref=hidden.at[g, x], dst_ref=gathered.at[me], send_sem=piece_send.at[x, g],
            recv_sem=piece_recv.at[me], device_id={**at_x(x), "z": z, "core": core},
            device_id_type=MESH,
        )

    def piece_arrival(source):
        return pltpu.make_async_remote_copy(
            src_ref=hidden.at[0, 0], dst_ref=gathered.at[source], send_sem=piece_send.at[0, 0],
            recv_sem=piece_recv.at[source],
            device_id={**seq_device(source), "core": source_core}, device_id_type=MESH,
        )

    own_group = lax.rem(my_z, z_count // 2) * 2 + my_core
    own_copy = pltpu.make_async_copy(hidden.at[own_group, my_x], gathered.at[me], local_sem)
    quarter = cap // 4

    @pl.loop(0, groups)
    def _(k):
        g = lax.rem(my_z + 1 + k, groups)
        at = lanes(g)
        rates = mode_rows(damping, at)
        decay = [jnp.exp(-d) for d in rates]
        weight = mode_rows(residue, at)
        sub = lax.broadcasted_iota(jnp.int32, (SUBS, LANES), 0).astype(jnp.float32) * step_rows
        start = tuple(
            partial[g, m]
            + jnp.exp(-rates[m] * sub)
            * carry_in[m // per_owner, m % per_owner, pl.ds(g, 1), :]
            for m in range(modes)
        )

        def step(i, states):
            rows = pl.ds(i, SUBS, stride=step_rows)
            u = gated[g, rows, :]
            states = tuple(a * h + r * u for a, h, r in zip(decay, states, weight, strict=True))
            mixed[rows, :] = tree_sum(list(states))
            return states

        lax.fori_loop(0, step_rows, step, start, unroll=4)
        conv = mixed[...] + direct[0:1, at] * gated[g]
        mixed[...] = query[g] * conv
        quarters = [mixed[pl.ds(q, quarter, stride=4), :] for q in range(4)]
        for x in range(x_count):
            hidden[g, x] = repack(quarters, x).astype(jnp.bfloat16)

            @pl.when(jnp.logical_not(is_me(x, g)))
            def _():
                piece_copy(x, g).start()

            @pl.when(is_me(x, g))
            def _():
                own_copy.start()

    from_self = source_core == my_core

    @pl.when(from_self)
    def _():
        own_copy.wait()

    @pl.loop(0, seq_count)
    def _(other):
        @pl.when(jnp.logical_not(jnp.logical_and(from_self, other == me)))
        def _():
            piece_arrival(other).wait_recv()

        x, g = other // z_count, lax.rem(other, z_count)

        @pl.when(jnp.logical_not(is_me(x, g)))
        def _():
            piece_copy(x, g).wait_send()

    for distance in (1, 2):
        halo_copy(distance).wait_send()

    @pl.loop(0, owners)
    def _(owner):
        @pl.when(owner != me)
        def _():
            end_copy(owner).wait_send()

    @pl.when(me < owners)
    def _():
        @pl.loop(0, seq_count)
        def _(target):
            @pl.when(target != me)
            def _():
                carry_copy(target).wait_send()


def conv_call(dims, streams, sizes, taps, residue, damping, direct):
    x_count, z_count = dims["x"], dims["z"]
    cap, width = streams.shape[1:]
    modes = residue.shape[0]
    seq_count = x_count * z_count
    per_owner = max(1, modes // seq_count)
    owners = modes // per_owner
    f32, bf16 = jnp.float32, jnp.bfloat16
    dma = pltpu.SemaphoreType.DMA
    vmem = pl.BlockSpec(memory_space=pltpu.VMEM)
    far = pl.BlockSpec(memory_space=pltpu.HBM)
    return pl.pallas_call(
        functools.partial(conv_kernel, x_count, z_count),
        out_shape=jax.ShapeDtypeStruct((seq_count, cap // 4, LANES), bf16),
        in_specs=[pl.BlockSpec(memory_space=pltpu.SMEM)] + [far] * 5,
        out_specs=pl.BlockSpec(memory_space=pl.ANY),
        scratch_shapes=[
            pltpu.VMEM(streams.shape, bf16),
            pltpu.VMEM(taps.shape, f32),
            pltpu.VMEM(residue.shape, f32),
            pltpu.VMEM(damping.shape, f32),
            pltpu.VMEM(direct.shape, f32),
            pltpu.VMEM((3, z_count, cap + SUBS, LANES), f32),
            pltpu.VMEM((z_count, SUBS, LANES), f32),
            pltpu.VMEM((per_owner, z_count, LANES), f32),
            pltpu.VMEM((z_count, cap, LANES), f32),
            pltpu.VMEM((z_count, cap, LANES), f32),
            pltpu.VMEM((cap, LANES), f32),
            pltpu.VMEM((z_count, modes, SUBS, LANES), f32),
            pltpu.VMEM((modes, z_count, LANES), f32),
            pltpu.VMEM((seq_count, per_owner, z_count, LANES), f32),
            pltpu.VMEM((seq_count, per_owner, z_count, LANES), f32),
            pltpu.VMEM((owners, per_owner, z_count, LANES), f32),
            pltpu.VMEM((z_count, x_count, cap // 4, LANES), bf16),
            pltpu.VMEM((2, z_count, SUBS, LANES), f32),
            dma((2,)), dma((2,)),
            dma((owners,)), dma((seq_count,)), dma((seq_count,)), dma((owners,)),
        ]
        + [dma((x_count, z_count)), dma((seq_count,)), dma((5,)), dma],
        compiler_params=pltpu.CompilerParams(
            collective_id=0, has_side_effects=True, vmem_limit_bytes=56 << 20
        ),
        name="convolve",
    )(sizes, streams, taps, residue, damping, direct)


def select_kernel(former, updated, remaining, pieces, chosen, sequence):
    seq_count, packed_rows, _ = pieces.shape
    width = LANES // 4
    lane = lax.broadcasted_iota(jnp.int32, (packed_rows, LANES), 1)
    line = lax.broadcasted_iota(jnp.int32, (packed_rows, LANES), 0)

    def place(s, start):
        at, offset = start // 4, lax.rem(start, 4) * width
        turned = pltpu.roll(pieces[s].astype(jnp.float32), offset, 1)
        present = jnp.broadcast_to(sequence[pl.ds(at, 1), :], turned.shape)
        before = jnp.where(line == 0, present, pltpu.roll(turned, 1, 0))
        sequence[pl.ds(at, packed_rows), :] = jnp.where(lane < offset, before, turned)
        sequence[pl.ds(at + packed_rows, 1), :] = turned[packed_rows - 1 :, :]
        return start + former[s]

    lax.fori_loop(0, seq_count, place, 0, unroll=8)
    row = line * 4 + lane // width
    chosen[...] = jnp.zeros_like(chosen)

    def pick(k, start):
        at, offset = start // 4, lax.rem(start, 4) * width
        here = sequence[pl.ds(at, packed_rows), :]
        after = sequence[pl.ds(at + 1, packed_rows), :]
        both = jnp.where(lane < offset, after, here)
        rows = pltpu.roll(both, lax.rem(LANES - offset, LANES), 1)
        chosen[remaining[k]] = jnp.where(row < updated[k], rows, 0.0).astype(jnp.bfloat16)
        return start + updated[k]

    lax.fori_loop(0, updated.shape[0], pick, 0, unroll=7)


def select_call(seq_len, pieces, former, updated, remaining):
    smem = pl.BlockSpec(memory_space=pltpu.SMEM)
    vmem = pl.BlockSpec(memory_space=pltpu.VMEM)
    return pl.pallas_call(
        select_kernel,
        out_shape=jax.ShapeDtypeStruct(pieces.shape, jnp.bfloat16),
        in_specs=[smem] * 3 + [vmem],
        out_specs=vmem,
        scratch_shapes=[pltpu.VMEM((seq_len // 4 + pieces.shape[1] + 8, LANES), jnp.float32)],
        compiler_params=pltpu.CompilerParams(vmem_limit_bytes=24 << 20),
        name="reorder_rows",
    )(former, updated, remaining, pieces)


def project_kernel(
    x_count, z_count, y_count,
    chosen, block, out,
    landing, unpacked, rows_in, weights, sum_out, sum_in,
    load_sem, own_sem, piece_send, piece_recv,
    right_send, right_recv, left_send, left_recv,
    far_a_send, far_a_recv, far_b_send, far_b_recv, core_send, core_recv,
    sum_send, sum_recv,
):
    cap, width = out.shape
    part_width = width // 2
    half, quarter = cap // 2, cap // 4
    reach = z_count // 2
    my_x, my_z = x_index(), lax.axis_index("z")
    my_y, my_core = lax.axis_index("y"), lax.axis_index("core")
    right, left = lax.rem(my_y + 1, y_count), lax.rem(my_y + y_count - 1, y_count)
    opposite = lax.rem(my_y + 2, y_count)
    other = 1 - my_core
    above, below = lax.rem(my_z + 1, z_count), lax.rem(my_z + z_count - 1, z_count)

    load = pltpu.make_async_copy(block, weights, load_sem)
    load.start()
    own_copy = pltpu.make_async_copy(
        chosen.at[pl.ds(my_x * z_count, z_count)], landing.at[my_x], own_sem
    )
    own_copy.start()

    barrier = pltpu.get_barrier_semaphore()
    for k in range(1, x_count):
        pl.semaphore_signal(
            barrier, inc=1, device_id=at_x(lax.rem(my_x + k, x_count)), device_id_type=MESH
        )
    for to in ({"y": right}, {"y": left}, {"core": other}, {"z": above}, {"z": below}):
        pl.semaphore_signal(barrier, inc=1, device_id=to, device_id_type=MESH)
    pl.semaphore_wait(barrier, x_count - 1 + 5)

    def piece_copy(x, owner):
        return pltpu.make_async_remote_copy(
            src_ref=chosen.at[x * z_count + owner], dst_ref=landing.at[my_x, owner],
            send_sem=piece_send.at[x, owner], recv_sem=piece_recv.at[my_x, owner],
            device_id=at_x(x), device_id_type=MESH,
        )

    def piece_arrival(x, owner):
        return pltpu.make_async_remote_copy(
            src_ref=chosen.at[owner], dst_ref=landing.at[x, owner],
            send_sem=piece_send.at[x, owner], recv_sem=piece_recv.at[x, owner],
            device_id=at_x(x), device_id_type=MESH,
        )

    order = [reach]
    for distance in range(reach - 1, 0, -1):
        order += [distance, z_count - distance]
    order = [lax.rem(my_z + d, z_count) for d in order + [0]]
    others = [lax.rem(my_x + k, x_count) for k in (1, 3, 2)]
    def send_pieces(owners):
        for owner in owners:
            for x in others:
                piece_copy(x, owner).start()

    send_pieces(order[:2])

    def columns(y, core):
        return pl.ds(pl.multiple_of((y * 2 + core) * LANES, LANES), LANES)

    def onward(y, core, owner, to, send, recv, first, rows):
        view = rows_in.at[owner, pl.ds(first, rows), columns(y, core)]
        return pltpu.make_async_remote_copy(
            src_ref=view, dst_ref=view, send_sem=send, recv_sem=recv,
            device_id=to, device_id_type=MESH,
        )

    def to_right(y, o):
        return onward(y, my_core, o, {"y": right}, right_send.at[o], right_recv.at[o], 0, cap)

    def to_left(y, o):
        return onward(y, my_core, o, {"y": left}, left_send.at[o], left_recv.at[o], 0, cap)

    def far_right(y, o):
        return onward(y, my_core, o, {"y": right}, far_a_send.at[o], far_a_recv.at[o], 0, half)

    def far_left(y, o):
        return onward(y, my_core, o, {"y": left}, far_b_send.at[o], far_b_recv.at[o], half, half)

    def to_core(y, core, o):
        return onward(y, core, o, {"core": other}, core_send.at[y, o], core_recv.at[y, o], 0, cap)

    def travels(way, distance, part):
        return distance < reach or part == way

    def slot(distance, part):
        return (distance - 1) * 2 + part

    def sum_copy(way, distance, part):
        at = slot(distance, part)
        return pltpu.make_async_remote_copy(
            src_ref=sum_out.at[way, at], dst_ref=sum_in.at[way, at],
            send_sem=sum_send.at[way, at], recv_sem=sum_recv.at[way, at],
            device_id={"z": below if way else above}, device_id_type=MESH,
        )

    def partial(owner, part):
        return jnp.dot(
            rows_in[owner], weights[:, part * part_width : (part + 1) * part_width],
            preferred_element_type=jnp.float32,
        )

    def ready(owner):
        @pl.loop(0, y_count)
        def _(y):
            to_core(y, other, owner).wait_recv()

    def send_sums(distance):
        owners = [lax.rem(my_z + d, z_count) for d in (distance, z_count - distance)]
        for owner in owners[: 1 if distance == reach else 2]:
            ready(owner)
        for way, part in ((0, 1), (1, 0), (0, 0), (1, 1)):
            if travels(way, distance, part):
                total = partial(owners[way], part)
                if distance < reach and travels(way, distance + 1, part):
                    sum_copy(way, distance + 1, part).wait_recv()
                    total = total + sum_in[way, slot(distance + 1, part)].astype(jnp.float32)
                sum_out[way, slot(distance, part)] = total.astype(jnp.bfloat16)
                sum_copy(way, distance, part).start()

    own_copy.wait()

    def launch(owner):
        for x in others:
            piece_arrival(x, owner).wait_recv()
        packed = [landing[x, owner].astype(jnp.float32) for x in range(x_count)]
        for q in range(4):
            unpacked[pl.ds(q, quarter, stride=4), :] = repack(packed, q)
        rows_in[owner, :, columns(my_y, my_core)] = unpacked[...].astype(jnp.bfloat16)
        to_right(my_y, owner).start()
        to_left(my_y, owner).start()
        to_core(my_y, my_core, owner).start()

    def finish(owner):
        far_right(opposite, owner).wait_recv()
        far_left(opposite, owner).wait_recv()
        to_core(opposite, my_core, owner).start()

    ahead, lag = 2, 1
    launch(order[0])
    send_pieces(order[2:])
    for owner in order[1:ahead]:
        launch(owner)
    load.wait()
    sent = reach + 1
    for k in range(len(order) + lag):
        if k + ahead < len(order):
            launch(order[k + ahead])
        if k < len(order):
            owner = order[k]
            to_right(left, owner).wait_recv()
            far_right(left, owner).start()
            to_core(left, my_core, owner).start()
            to_left(right, owner).wait_recv()
            far_left(right, owner).start()
            to_core(right, my_core, owner).start()
        if k >= lag:
            finish(order[k - lag])
        if k == lag or k in (lag + 2, lag + 4) and reach > 1:
            sent -= 1
            send_sums(sent)
    for distance in range(sent - 1, 0, -1):
        send_sums(distance)

    ready(my_z)
    for part in range(2):
        total = partial(my_z, part)
        for way in range(2):
            if travels(way, 1, part):
                sum_copy(way, 1, part).wait_recv()
                total = total + sum_in[way, slot(1, part)].astype(jnp.float32)
        out[:, part * part_width : (part + 1) * part_width] = total.astype(jnp.bfloat16)

    for distance in range(1, reach + 1):
        for part in range(2):
            for way in range(2):
                if travels(way, distance, part):
                    sum_copy(way, distance, part).wait_send()
    for owner in order:
        for x in others:
            piece_copy(x, owner).wait_send()

    @pl.loop(0, z_count)
    def _(o):
        for y in range(y_count):
            to_core(y, my_core, o).wait_send()
        to_right(my_y, o).wait_send()
        to_left(my_y, o).wait_send()
        far_right(left, o).wait_send()
        far_left(right, o).wait_send()


def project_call(dims, chosen, block):
    x_count, y_count, z_count = dims["x"], dims["y"], dims["z"]
    cap = chosen.shape[1] * 4
    depth, width = block.shape
    reach = z_count // 2
    bf16 = jnp.bfloat16
    dma = pltpu.SemaphoreType.DMA
    vmem = pl.BlockSpec(memory_space=pltpu.VMEM)
    return pl.pallas_call(
        functools.partial(project_kernel, x_count, z_count, y_count),
        out_shape=jax.ShapeDtypeStruct((cap, width), bf16),
        in_specs=[vmem, pl.BlockSpec(memory_space=pltpu.HBM)],
        out_specs=vmem,
        scratch_shapes=[
            pltpu.VMEM((x_count, z_count, cap // 4, LANES), bf16),
            pltpu.VMEM((cap, LANES), jnp.float32),
            pltpu.VMEM((z_count, cap, depth), bf16),
            pltpu.VMEM((depth, width), bf16),
            pltpu.VMEM((2, 2 * reach, cap, width // 2), bf16),
            pltpu.VMEM((2, 2 * reach, cap, width // 2), bf16),
            dma, dma, dma((x_count, z_count)), dma((x_count, z_count)),
        ]
        + [dma((z_count,))] * 8
        + [dma((y_count, z_count))] * 2
        + [dma((2, 2 * reach))] * 2,
        compiler_params=pltpu.CompilerParams(
            collective_id=1, has_side_effects=True, vmem_limit_bytes=53 << 20
        ),
        name="project_rows",
    )(chosen, block)


def shards(
    dims,
    input_triple_streams,
    former_piece_sizes,
    updated_piece_sizes,
    remaining_indices,
    short_causal_filters,
    pole_coefficients,
    pole_damping,
    direct_coefficient,
    final_projector,
):
    cap = input_triple_streams.shape[0]
    seq_len = cap * 4 // 5 * dims["x"] * dims["z"]

    block = lax.all_gather(final_projector, ("x_high", "x_low"), axis=0, tiled=True)
    pieces = conv_call(
        dims,
        jnp.transpose(input_triple_streams, (1, 0, 2)),
        former_piece_sizes,
        short_causal_filters,
        pole_coefficients,
        pole_damping,
        direct_coefficient[None, :],
    )
    chosen = select_call(
        seq_len, pieces, former_piece_sizes, updated_piece_sizes, remaining_indices
    )
    return project_call(dims, chosen, block)


def solution(mesh):
    grid = (2, 2, mesh.shape["seq"] // 4, mesh.shape["chan"] // 2, 2)
    dims = {"x": 4, "z": grid[2], "y": grid[3]}
    rows, channels = SEQ, ("y", "core")
    return jax.shard_map(
        functools.partial(shards, dims),
        mesh=Mesh(mesh.devices.reshape(grid), AXES),
        in_specs=(
            P(rows, None, channels),
            P(),
            P(),
            P(),
            P(None, None, channels),
            P(None, channels),
            P(None, channels),
            P(channels),
            P(rows, channels),
        ),
        out_specs=P(rows, channels),
        check_vma=False,
    )
```
